32 devices in a mesh: seq: 4 (over z), dp: 8 (over y, x, core).
Axes of the slice: x: 2, y: 2, z: 4, core: 2. Of those that a mesh axis runs over, the one named last changes fastest.
Arguments:
- tokens: bfloat16 [8, 1024, 2048], P('dp', 'seq'), may hold values from -6 to 6
- norm_gain: float32 [2048], replicated, may hold values from 0.5 to 1.5
- key_value_weight: bfloat16 [2048, 4096], P('seq'), may hold values from -0.125 to 0.125
- router_weight: bfloat16 [2048, 8], replicated, may hold values from -0.09375 to 0.09375
- query_weight: bfloat16 [8, 2048, 2048], P('dp', 'seq'), may hold values from -0.25 to 0.25
- output_weight: bfloat16 [8, 2048, 2048], P('dp', 'seq'), may hold values from -0.375 to 0.375
- mlp_gain: float32 [2048], replicated, may hold values from 0.5 to 1.5
- mlp_router_weight: bfloat16 [2048, 8], replicated, may hold values from -0.09375 to 0.09375
- mlp_in_weight: bfloat16 [8, 2048, 11264], P('dp', 'seq'), may hold values from -0.125 to 0.125
- mlp_out_weight: bfloat16 [8, 5632, 2048], P('dp', 'seq'), may hold values from -0.21875 to 0.21875
- key_value_down: bfloat16 [8, 2048, 16], replicated, may hold values from -0.125 to 0.125
- key_value_up: bfloat16 [8, 16, 4096], replicated, may hold values from -0.47851562 to 0.47851562
- query_down: bfloat16 [8, 2048, 16], replicated, may hold values from -0.125 to 0.125
- query_up: bfloat16 [8, 16, 2048], replicated, may hold values from -0.8984375 to 0.8984375
- output_down: bfloat16 [8, 2048, 16], replicated, may hold values from -0.375 to 0.375
- output_up: bfloat16 [8, 16, 2048], replicated, may hold values from -0.71875 to 0.71875
- mlp_in_down: bfloat16 [8, 2048, 16], replicated, may hold values from -0.125 to 0.125
- mlp_in_up: bfloat16 [8, 16, 11264], replicated, may hold values from -0.8984375 to 0.8984375
- mlp_out_down: bfloat16 [8, 5632, 16], replicated, may hold values from -0.21875 to 0.21875
- mlp_out_up: bfloat16 [8, 16, 2048], replicated, may hold values from -0.71875 to 0.71875
- routes: int32 [8, 1024, 2], P('dp', 'seq'), may hold values from 0 to 7, all different within a row; in each aligned block of 256 rows (0 to 255, 256 to 511, ..., all dimensions but the last counted through in order) at most 96 rows name the same one
- mlp_routes: int32 [8, 1024, 2], P('dp', 'seq'), may hold values from 0 to 7, all different within a row; in each aligned block of 256 rows (0 to 255, 256 to 511, ..., all dimensions but the last counted through in order) at most 96 rows name the same one
- adapter_index: int32 [8], P('dp'), may hold values from 0 to 7
- prefix_length: int32 [8], P('dp'), may hold values from 1 to 512
- out_grad: bfloat16 [8, 1024, 2048], P('dp', 'seq'), may hold values from -6 to 6
Outputs:
- out_tokens: bfloat16 [8, 1024, 2048], P('dp', 'seq')
- input_grad: float32 [8, 1024, 2048], P('dp', 'seq')
- key_value_down_grad: float32 [8, 2048, 16], replicated
- key_value_up_grad: float32 [8, 16, 4096], replicated
- query_down_grad: float32 [8, 2048, 16], replicated
- query_up_grad: float32 [8, 16, 2048], replicated
- output_down_grad: float32 [8, 2048, 16], replicated
- output_up_grad: float32 [8, 16, 2048], replicated
- mlp_in_down_grad: float32 [8, 2048, 16], replicated
- mlp_in_up_grad: float32 [8, 16, 11264], replicated
- mlp_out_down_grad: float32 [8, 5632, 16], replicated
- mlp_out_up_grad: float32 [8, 16, 2048], replicated
The draws below stay inside these ranges and needn't reach their ends.
Inputs may be any that keep to these rules, and one draw needn't show every extreme that they name: `routes`: in each aligned block of 256 rows (one sequence's tokens on one device) no expert is named by more than 96 rows; a token's two experts differ. `mlp_routes`: in each aligned block of 256 rows (one sequence's tokens on one device) no expert is named by more than 96 rows; a token's two experts differ.
All inputs are finite; a program needn't handle non-finite values.
Results may differ from the reference program's by a relative error of at most 0.02.
Values may be sent and summed in bfloat16 or wider, within the bound.
No kernel may reach another device: no remote copies, remote signals or barrier semaphores. Data moves between devices by JAX's collectives and lax.ppermute only.
A program may use at most 448 MiB of HBM per device.

```python
import math
import jax
import jax.numpy as jnp
import numpy as np
from jax import lax

D = 2048
KV_HEADS = 16
EXP_HEADS = 16
HD = 128
FF = 5632
EXPERTS = 8
TOP = 2
RANK = 16
ADAPTERS = 8
SEQ_LEN = 1024
SEQS_DEV = 1
SEQS = 8
TOK_SEQ_DEV = 256
SPLIT = 1
QW = 2048
FW = 5632
MOST = 96


def set_ends(values, key, smallest, largest):
    longest = values.shape.index(max(values.shape))
    spots = []
    for shift in (0, 1):
        where = [jax.random.randint(jax.random.fold_in(key, axis), (), 0, length) for axis, length in enumerate(values.shape)]
        where[longest] = (where[longest] + shift) % values.shape[longest]
        spots.append(tuple(where))
    return values.at[spots[0]].set(smallest).at[spots[1]].set(largest)


def block_scale(key, shape, cuts, least, high):
    def one(axis_at, parts):
        draws = jax.random.uniform(jax.random.fold_in(jax.random.fold_in(key, 6), axis_at), (parts,), jnp.float32, least / len(cuts), high / len(cuts))
        return jnp.repeat(jnp.exp(draws), shape[axis_at] // parts).reshape((-1,) + (1,) * (len(shape) - axis_at - 1))

    level = one(*cuts[0])
    for cut in cuts[1:]:
        level = level * one(*cut)
    return level


def assign_block(stream_key, own, number, rows, count, top, limit, skew):
    ranking = jax.random.permutation(stream_key, count)
    heavy_load, usual = shares(count, rows * top, limit, skew, True), shares(count, rows * top, limit, skew, False)
    places = jnp.arange(count)

    def named(sizes, turn):
        used = int((sizes > 0).sum())
        fixed = max(1, used // 4)
        passed = fixed + (places - fixed + turn * (used - fixed)) % max(1, count - fixed)
        return jnp.zeros((count,), jnp.int32).at[ranking[jnp.where(places < fixed, places, passed)]].set(jnp.asarray(sizes, jnp.int32))

    sizes = jnp.where(number % 4 == 0, named(heavy_load, number // 4), named(usual, number - number // 4 - 1))
    mixed = jax.random.permutation(jax.random.fold_in(own, 3), count)
    donor, sink = mixed[0:count // 2 * 2:2], mixed[1:count // 2 * 2:2]
    slack = jnp.minimum(sizes[donor] - 1, limit - sizes[sink]) // 2
    slack = jnp.where((donor == ranking[0]) | (sink == ranking[0]) | (sizes[sink] == 0), 0, jnp.maximum(slack, 0))
    passed = jax.random.randint(jax.random.fold_in(own, 4), (count // 2,), 0, 1 << 20) % (slack + 1)
    sizes = sizes.at[donor].add(-passed).at[sink].add(passed)
    items = jnp.searchsorted(jnp.cumsum(sizes), jnp.arange(rows * top), side="right").astype(jnp.int32)
    listing = items.reshape(top, rows).T
    listing = listing[jax.random.permutation(jax.random.fold_in(own, 1), rows)]
    turn = jax.random.randint(jax.random.fold_in(own, 2), (rows, 1), 0, top)
    return jnp.take_along_axis(listing, (jnp.arange(top)[None, :] + turn) % top, axis=1)


def shares(count, total, reach, lean, full):
    weights = [(1 << 20) // math.isqrt(rank ** lean) + 1 for rank in range(1, count + 1)]
    largest = reach if full else min(reach, max(-(-total // count), total * weights[0] // sum(weights)))
    least = 1 if total - largest >= count - 1 else 0
    holding, rest = [largest] + [least] * (count - 1), total - largest - least * (count - 1)
    while rest > 0:
        movable = [i for i in range(1, count) if holding[i] < largest] or [i for i in range(1, count) if holding[i] < reach]
        whole, budget = sum([weights[i] for i in movable]), rest
        for i in movable:
            addition = min(reach - holding[i], max(1, budget * weights[i] // whole), rest)
            holding[i] = holding[i] + addition
            rest = rest - addition
    return np.array(holding)


def normal_values(key, extent, spread, most, cuts=(), dtype=jnp.bfloat16):
    values = jax.random.normal(key, extent, jnp.float32) * spread
    if len(cuts) > 0:
        values = block_scale(key, extent, cuts, -0.22, 0.18) * values
    return jnp.clip(values, min=-most, max=most).astype(dtype)


def setup_inputs(seed: int = 0) -> dict:
    seeds = jax.random.split(jax.random.key(seed), 26)
    tokens = normal_values(seeds[0], (SEQS, SEQ_LEN, D), 1.0, 6.0, ((0, 8), (1, 4)))
    norm_gain = jnp.clip(1.0 + 0.1 * jax.random.normal(seeds[1], (D,), jnp.float32), 0.5, 1.5)
    key_value_weight = normal_values(seeds[2], (D, 2 * KV_HEADS * HD), D ** -0.5, 0.125, ((0, 4),))
    router_weight = normal_values(seeds[3], (D, EXPERTS), (2 * D) ** -0.5, 0.09375)
    query_weight = normal_values(seeds[4], (EXPERTS * SPLIT, D, QW), (D // 4) ** -0.5, 0.25, ((0, 8), (1, 4)))
    output_weight = normal_values(seeds[5], (EXPERTS * SPLIT, QW, D), (EXP_HEADS * HD // 8) ** -0.5, 0.375, ((0, 8), (1, 4)))
    mlp_gain = jnp.clip(1.0 + 0.1 * jax.random.normal(seeds[6], (D,), jnp.float32), 0.5, 1.5)
    mlp_router_weight = normal_values(seeds[7], (D, EXPERTS), (2 * D) ** -0.5, 0.09375)
    mlp_in_weight = normal_values(seeds[8], (EXPERTS * SPLIT, D, 2 * FW), D ** -0.5, 0.125, ((0, 8), (1, 4)))
    mlp_out_weight = normal_values(seeds[9], (EXPERTS * SPLIT, FW, D), (FF // 8) ** -0.5, 0.21875, ((0, 8), (1, 4)))
    key_value_down = normal_values(seeds[10], (ADAPTERS, D, RANK), D ** -0.5, 0.125)
    key_value_up = normal_values(seeds[11], (ADAPTERS, RANK, 2 * KV_HEADS * HD), 0.08, 0.47851562)
    query_down = normal_values(seeds[12], (ADAPTERS, D, RANK), D ** -0.5, 0.125)
    query_up = normal_values(seeds[13], (ADAPTERS, RANK, EXP_HEADS * HD), 0.15, 0.8984375)
    output_down = normal_values(seeds[14], (ADAPTERS, EXP_HEADS * HD, RANK), (EXP_HEADS * HD // 8) ** -0.5, 0.375)
    output_up = normal_values(seeds[15], (ADAPTERS, RANK, D), 0.12, 0.71875)
    mlp_in_down = normal_values(seeds[16], (ADAPTERS, D, RANK), D ** -0.5, 0.125)
    mlp_in_up = normal_values(seeds[17], (ADAPTERS, RANK, 2 * FF), 0.15, 0.8984375)
    mlp_out_down = normal_values(seeds[18], (ADAPTERS, FF, RANK), (FF // 8) ** -0.5, 0.21875)
    mlp_out_up = normal_values(seeds[19], (ADAPTERS, RANK, D), 0.12, 0.71875)
    routes_keys = jax.random.split(jax.random.fold_in(seeds[20], 1), SEQS * SEQ_LEN // TOK_SEQ_DEV)
    routes_turns = jax.random.permutation(jax.random.fold_in(seeds[20], 3), SEQS * SEQ_LEN // TOK_SEQ_DEV)
    routes = jax.vmap(lambda own, number: assign_block(jax.random.fold_in(seeds[20], 2), own, number, TOK_SEQ_DEV, EXPERTS, TOP, MOST, 1))(routes_keys, routes_turns).reshape((SEQS, SEQ_LEN, TOP))
    mlp_routes_keys = jax.random.split(jax.random.fold_in(seeds[21], 1), SEQS * SEQ_LEN // TOK_SEQ_DEV)
    mlp_routes_turns = jax.random.permutation(jax.random.fold_in(seeds[21], 3), SEQS * SEQ_LEN // TOK_SEQ_DEV)
    mlp_routes = jax.vmap(lambda own, number: assign_block(jax.random.fold_in(seeds[21], 2), own, number, TOK_SEQ_DEV, EXPERTS, TOP, MOST, 1))(mlp_routes_keys, mlp_routes_turns).reshape((SEQS, SEQ_LEN, TOP))
    adapter_index = set_ends(jax.random.randint(seeds[22], (SEQS,), 0, ADAPTERS), jax.random.fold_in(seeds[22], 1), 0, ADAPTERS - 1).astype(jnp.int32)
    prefix_length = set_ends(jax.random.randint(seeds[23], (SEQS,), 1, SEQ_LEN // 2 + 1), jax.random.fold_in(seeds[23], 1), 1, (SEQ_LEN // 2 + 1) - 1).astype(jnp.int32)
    out_grad = normal_values(seeds[24], (SEQS, SEQ_LEN, D), 1.0, 6.0, ((0, 8), (1, 4)))
    return dict(tokens=tokens, norm_gain=norm_gain, key_value_weight=key_value_weight, router_weight=router_weight, query_weight=query_weight, output_weight=output_weight, mlp_gain=mlp_gain, mlp_router_weight=mlp_router_weight, mlp_in_weight=mlp_in_weight, mlp_out_weight=mlp_out_weight, key_value_down=key_value_down, key_value_up=key_value_up, query_down=query_down, query_up=query_up, output_down=output_down, output_up=output_up, mlp_in_down=mlp_in_down, mlp_in_up=mlp_in_up, mlp_out_down=mlp_out_down, mlp_out_up=mlp_out_up, routes=routes, mlp_routes=mlp_routes, adapter_index=adapter_index, prefix_length=prefix_length, out_grad=out_grad)


@jax.custom_vjp
def low(v):
    return lax.optimization_barrier(v.astype(jnp.bfloat16)).astype(jnp.float32)

@jax.custom_vjp
def lower_rank_backward(v):
    return v

def low_keep(v):
    return (low(v), None)

def low_pass(kept, grad):
    return (grad,)

def back_keep(v):
    return (v, None)

def back_low(kept, grad):
    return (low(grad),)
low.defvjp(low_keep, low_pass)
lower_rank_backward.defvjp(back_keep, back_low)
norm_eps = 1e-05
rope_base = 10000.0
masked_score = -1e+30
largest_entry = lax.Precision.HIGHEST

def rms_norm(values, gain_vector):
    mean_square = lax.optimization_barrier(jnp.mean(values * values, axis=-1, keepdims=True))
    return values * lax.rsqrt(mean_square + norm_eps) * gain_vector

def rope_tables(positions, head_dim):
    half_width = head_dim // 2
    step_ids = jnp.arange(half_width).astype(jnp.float32)
    frequency = jnp.power(rope_base, -step_ids / half_width)
    angles = positions[:, None] * frequency[None, :]
    return (jnp.cos(angles), jnp.sin(angles))

def rotate(values, cosine_table, sine_table):
    half_width = values.shape[-1] // 2
    first_half = values[..., :half_width]
    second_half = values[..., half_width:]
    return jnp.concatenate([first_half * cosine_table - second_half * sine_table, second_half * cosine_table + first_half * sine_table], axis=-1)

def gate_softmax(logits, route_ids):
    chosen = jnp.take_along_axis(logits, route_ids, axis=-1)
    highest_score = lax.optimization_barrier(jnp.max(chosen, axis=-1, keepdims=True))
    weights = jnp.exp(chosen - highest_score)
    return weights / lax.optimization_barrier(jnp.sum(weights, axis=-1, keepdims=True))

def allowed_keys(query_pos, length, prefix):
    key_pos = jnp.arange(length)
    return (key_pos[None, :] <= query_pos[:, None]) | (key_pos[None, :] < prefix)

def attend_whole(operands):
    query_seq, key_seq, value_seq, prefix = operands
    length = key_seq.shape[0]
    positions = jnp.arange(length)
    scores = lower_rank_backward(jnp.einsum('trhd,jhd->rhtj', query_seq, key_seq, precision=largest_entry) * (1.0 / math.sqrt(HD)))
    scores = jnp.where(allowed_keys(positions, length, prefix), scores, masked_score)
    highest_score = lax.optimization_barrier(jnp.max(scores, axis=-1, keepdims=True))
    weights = jnp.exp(scores - highest_score)
    probabilities = weights / lax.optimization_barrier(jnp.sum(weights, axis=-1, keepdims=True))
    return jnp.einsum('rhtj,jhd->trhd', low(probabilities), value_seq, precision=largest_entry)

def layer(inputs, adapters, route_ids, mlp_route_ids, adapter_ids, prefixes, gain_vector, adapter_pair_weight, router, query_experts, output_experts, mlp_gain_vector, mlp_router, mlp_in_experts, mlp_out_experts):
    pair_down, adapter_pair_upper, query_lower, query_upper, output_lower, output_upper, inner_down, inner_up, outer_down, outer_up = adapters
    group_size = inputs.shape[0]
    length = inputs.shape[1]
    normalized_input = low(rms_norm(inputs, gain_vector))
    adapter_hot = (adapter_ids[:, None] == jnp.arange(ADAPTERS)[None, :]).astype(jnp.float32)

    def choose_entries(lookup):
        return jnp.einsum('ga,a...->g...', adapter_hot, lookup, precision=largest_entry)
    adapter_pair_lower = low(jnp.einsum('gld,gdr->glr', normalized_input, choose_entries(pair_down), precision=largest_entry))
    adapter_pair_values = jnp.einsum('xyq,qm->xym', normalized_input, adapter_pair_weight, precision=largest_entry)
    adapter_pair_values = lower_rank_backward(adapter_pair_values + jnp.einsum('fyk,fko->fyo', adapter_pair_lower, choose_entries(adapter_pair_upper), precision=largest_entry))
    kv_width = KV_HEADS * HD
    cosine_table, sine_table = rope_tables(jnp.arange(length).astype(jnp.float32), HD)
    keys = low(rotate(adapter_pair_values[..., :kv_width].reshape(group_size, length, KV_HEADS, HD), cosine_table[:, None, :], sine_table[:, None, :]))
    values = low(adapter_pair_values[..., kv_width:].reshape(group_size, length, KV_HEADS, HD))
    logits = jnp.einsum('gld,de->gle', normalized_input, router, precision=largest_entry)
    gate_values = gate_softmax(logits, route_ids)
    expert_hits = (route_ids[..., None] == jnp.arange(EXPERTS)).astype(jnp.float32)
    query_all = jnp.einsum('gld,edq->gleq', normalized_input, query_experts, precision=largest_entry)
    query_base = jnp.einsum('glre,gleq->glrq', expert_hits, query_all, precision=largest_entry)
    query_low = low(jnp.einsum('gld,gdr->glr', normalized_input, choose_entries(query_lower), precision=largest_entry))
    query_extra = jnp.einsum('glr,grq->glq', query_low, choose_entries(query_upper), precision=largest_entry)
    query_pre = lower_rank_backward(query_base + query_extra[:, :, None, :])
    query_rot = low(rotate(query_pre.reshape(group_size, length, TOP, EXP_HEADS, HD), cosine_table[:, None, None, :], sine_table[:, None, None, :]))
    attended = lax.map(jax.checkpoint(attend_whole), (query_rot, keys, values, prefixes))
    attended = low(lower_rank_backward(attended.reshape(group_size, length, TOP, EXP_HEADS * HD)))
    attended_expert = jnp.einsum('glre,glrq->gleq', expert_hits, attended, precision=largest_entry)
    projected_all = jnp.einsum('gleq,eqd->gled', attended_expert, output_experts, precision=largest_entry)
    projected = jnp.einsum('glre,gled->glrd', expert_hits, projected_all, precision=largest_entry)
    output_low = low(jnp.einsum('glrq,gqk->glrk', attended, choose_entries(output_lower), precision=largest_entry))
    branch = lower_rank_backward(projected + jnp.einsum('glrk,gkd->glrd', output_low, choose_entries(output_upper), precision=largest_entry))
    middle = inputs + lax.optimization_barrier(jnp.sum(gate_values[..., None] * branch, axis=2))
    normed_mlp = low(rms_norm(middle, mlp_gain_vector))
    mlp_logits = jnp.einsum('gld,de->gle', normed_mlp, mlp_router, precision=largest_entry)
    mlp_gates = gate_softmax(mlp_logits, mlp_route_ids)
    mlp_hits = (mlp_route_ids[..., None] == jnp.arange(EXPERTS)).astype(jnp.float32)
    inner_low = low(jnp.einsum('gld,gdr->glr', normed_mlp, choose_entries(inner_down), precision=largest_entry))
    inner_extra = jnp.einsum('glr,grf->glf', inner_low, choose_entries(inner_up), precision=largest_entry)
    inner_all = jnp.einsum('gld,edf->glef', normed_mlp, mlp_in_experts, precision=largest_entry)
    inner_pre = jnp.einsum('glre,glef->glrf', mlp_hits, inner_all, precision=largest_entry)
    inner_pre = lower_rank_backward(inner_pre + inner_extra[:, :, None, :])
    gate_part = inner_pre[..., :FF]
    up_part = inner_pre[..., FF:]
    activated = low(jax.nn.silu(gate_part) * up_part)
    activated_expert = jnp.einsum('glre,glrf->glef', mlp_hits, activated, precision=largest_entry)
    mlp_all = jnp.einsum('glef,efd->gled', activated_expert, mlp_out_experts, precision=largest_entry)
    mlp_projected = jnp.einsum('glre,gled->glrd', mlp_hits, mlp_all, precision=largest_entry)
    outer_low = low(lower_rank_backward(jnp.einsum('glrf,gfk->glrk', activated, choose_entries(outer_down), precision=largest_entry)))
    mlp_branch = lower_rank_backward(mlp_projected + jnp.einsum('glrk,gkd->glrd', outer_low, choose_entries(outer_up), precision=largest_entry))
    return middle + lax.optimization_barrier(jnp.sum(mlp_gates[..., None] * mlp_branch, axis=2))

def reference(tokens, norm_gain, key_value_weight, router_weight, query_weight, output_weight, mlp_gain, mlp_router_weight, mlp_in_weight, mlp_out_weight, key_value_down, key_value_up, query_down, query_up, output_down, output_up, mlp_in_down, mlp_in_up, mlp_out_down, mlp_out_up, routes, mlp_routes, adapter_index, prefix_length, out_grad):
    query_experts = query_weight.astype(jnp.float32).reshape(EXPERTS, SPLIT, D, QW)
    query_experts = query_experts.transpose(0, 2, 1, 3).reshape(EXPERTS, D, SPLIT * QW)
    output_experts = output_weight.astype(jnp.float32).reshape(EXPERTS, SPLIT * QW, D)
    mlp_in_experts = mlp_in_weight.astype(jnp.float32).reshape(EXPERTS, SPLIT, D, 2, FW)
    mlp_in_experts = mlp_in_experts.transpose(0, 2, 3, 1, 4).reshape(EXPERTS, D, 2 * FF)
    mlp_out_experts = mlp_out_weight.astype(jnp.float32).reshape(EXPERTS, FF, D)
    adapter_pair_weight = key_value_weight.astype(jnp.float32)
    router = router_weight.astype(jnp.float32)
    mlp_router = mlp_router_weight.astype(jnp.float32)
    adapters = (key_value_down.astype(jnp.float32), key_value_up.astype(jnp.float32), query_down.astype(jnp.float32), query_up.astype(jnp.float32), output_down.astype(jnp.float32), output_up.astype(jnp.float32), mlp_in_down.astype(jnp.float32), mlp_in_up.astype(jnp.float32), mlp_out_down.astype(jnp.float32), mlp_out_up.astype(jnp.float32))
    group_count = SEQS // SEQS_DEV

    def grouped(array):
        return array.reshape((group_count, SEQS_DEV) + array.shape[1:])
    scanned = (grouped(tokens.astype(jnp.float32)), grouped(out_grad.astype(jnp.float32)), grouped(routes), grouped(mlp_routes), grouped(adapter_index), grouped(prefix_length))

    def group_step(carried, operands):
        inputs, grad_group, route_ids, mlp_route_ids, adapter_ids, prefixes = operands

        def forward(input_values, adapter_values):
            return layer(input_values, adapter_values, route_ids, mlp_route_ids, adapter_ids, prefixes, norm_gain, adapter_pair_weight, router, query_experts, output_experts, mlp_gain, mlp_router, mlp_in_experts, mlp_out_experts)
        output_values, pull_back = jax.vjp(forward, inputs, adapters)
        input_grads, adapter_grads = pull_back(grad_group)
        carried = tuple((total + extra for total, extra in zip(carried, adapter_grads)))
        return (carried, (output_values.astype(jnp.bfloat16), input_grads))
    initial = tuple((jnp.zeros(array.shape, jnp.float32) for array in adapters))
    adapter_totals, (output_groups, grad_groups) = lax.scan(group_step, initial, scanned)
    out_tokens = output_groups.reshape(SEQS, SEQ_LEN, D)
    input_grad = grad_groups.reshape(SEQS, SEQ_LEN, D)
    return (out_tokens, input_grad, adapter_totals[0], adapter_totals[1], adapter_totals[2], adapter_totals[3], adapter_totals[4], adapter_totals[5], adapter_totals[6], adapter_totals[7], adapter_totals[8], adapter_totals[9])
```

```python
import functools
import math

import jax
import jax.numpy as jnp
from jax import lax
from jax.experimental import pallas as pl
from jax.experimental.pallas import tpu as pltpu
from jax.sharding import PartitionSpec as P

KV_HEADS = 16
HD = 128

norm_eps = 1e-05
rope_base = 10000.0
masked_score = -1e30
vmem_bytes = 48 * 2**20

bf16 = jnp.bfloat16
f32 = jnp.float32


def product(left, right, left_dim, right_dim):
    return lax.dot_general(
        left, right, (((left_dim,), (right_dim,)), ((), ())), preferred_element_type=f32
    )


def nn(left, right):
    return product(left, right, 1, 0)


def nt(left, right):
    return product(left, right, 1, 1)


def tn(left, right):
    return product(left, right, 0, 0)


def pair_kernel(key_blocks, n_ref, w_ref, low_ref, up_ref, cos_ref, sin_ref, out_ref):
    made = nn(n_ref[...], w_ref[...]) + nn(low_ref[...], up_ref[...])

    @pl.when(pl.program_id(0) < key_blocks)
    def _():
        for start in range(0, made.shape[1], HD):
            head = made[:, start : start + HD]
            turned = head * cos_ref[...] + pltpu.roll(head, HD // 2, 1) * sin_ref[...]
            out_ref[:, start : start + HD] = turned.astype(bf16)

    @pl.when(pl.program_id(0) >= key_blocks)
    def _():
        out_ref[...] = made.astype(bf16)


def project_pairs(normed, weight, low, upper, cosine, sine):
    rows, width = normed.shape
    columns = weight.shape[1]
    block = 512
    return pl.pallas_call(
        functools.partial(pair_kernel, columns // 2 // block),
        grid=(columns // block,),
        in_specs=[
            pl.BlockSpec((rows, width), lambda i: (0, 0)),
            pl.BlockSpec((width, block), lambda i: (0, i)),
            pl.BlockSpec(low.shape, lambda i: (0, 0)),
            pl.BlockSpec((upper.shape[0], block), lambda i: (0, i)),
            pl.BlockSpec((rows, HD), lambda i: (0, 0)),
            pl.BlockSpec((rows, HD), lambda i: (0, 0)),
        ],
        out_specs=pl.BlockSpec((rows, block), lambda i: (0, i)),
        out_shape=jax.ShapeDtypeStruct((rows, columns), bf16),
        compiler_params=pltpu.CompilerParams(vmem_limit_bytes=vmem_bytes),
        name="pairs",
    )(normed, weight, low, upper, cosine, sine)


def attend_kernel(
    scale,
    home_ref,
    place_ref,
    low_ref,
    up_ref,
    cos_ref,
    sin_ref,
    key_ref,
    value_ref,
    bias_ref,
    attended_ref,
    slots_ref,
    query_ref,
    total_ref,
):
    rows = cos_ref.shape[0]
    base = nn(place_ref[...], home_ref[...])
    extra = nn(low_ref[...], up_ref[...])
    keys, values = key_ref[...], value_ref[...]
    for route in range(2):
        part = pl.ds(route * rows, rows)
        query = base[route * rows : (route + 1) * rows] + extra
        query = query * cos_ref[...] + pltpu.roll(query, HD // 2, 1) * sin_ref[...]
        query = query.astype(bf16)
        query_ref[part, :] = query
        scores = nt(query, keys) * scale + bias_ref[...]
        highest = jnp.max(scores, axis=1, keepdims=True)
        weights = jnp.exp(scores - highest)
        total = jnp.sum(weights, axis=1, keepdims=True)
        attended = nn(weights.astype(bf16), values) / total
        attended_ref[part, :] = attended.astype(bf16)
        total_ref[0, part, :] = highest + jnp.log(total)
    slots_ref[...] = tn(place_ref[...], attended_ref[...]).astype(bf16)


def attend(home, place, low, upper, cosine, sine, pairs, bias):
    rows2, slots = place.shape
    rows, length = bias.shape
    heads = home.shape[1] // HD
    kv_heads = pairs.shape[1] // (2 * HD)
    whole = lambda array: pl.BlockSpec(array.shape, lambda h: (0, 0))
    return pl.pallas_call(
        functools.partial(attend_kernel, 1.0 / math.sqrt(HD)),
        grid=(heads,),
        in_specs=[
            pl.BlockSpec((slots, HD), lambda h: (0, h)),
            whole(place),
            whole(low),
            pl.BlockSpec((upper.shape[0], HD), lambda h: (0, h)),
            whole(cosine),
            whole(sine),
            pl.BlockSpec((length, HD), lambda h: (0, h)),
            pl.BlockSpec((length, HD), lambda h: (0, kv_heads + h)),
            whole(bias),
        ],
        out_specs=[
            pl.BlockSpec((rows2, HD), lambda h: (0, h)),
            pl.BlockSpec((slots, HD), lambda h: (0, h)),
            pl.BlockSpec((rows2, HD), lambda h: (0, h)),
            pl.BlockSpec((1, rows2, 1), lambda h: (h, 0, 0)),
        ],
        out_shape=[
            jax.ShapeDtypeStruct((rows2, heads * HD), bf16),
            jax.ShapeDtypeStruct((slots, heads * HD), bf16),
            jax.ShapeDtypeStruct((rows2, heads * HD), bf16),
            jax.ShapeDtypeStruct((heads, rows2, 1), f32),
        ],
        compiler_params=pltpu.CompilerParams(vmem_limit_bytes=vmem_bytes),
        cost_estimate=pl.CostEstimate(
            flops=4 * heads * rows2 * length * HD,
            bytes_accessed=4 * length * heads * HD,
            transcendentals=heads * rows2 * length,
        ),
        name="attend",
    )(home, place, low, upper, cosine, sine, pairs, pairs, bias)


def attend_back_kernel(
    scale,
    query_ref,
    key_ref,
    value_ref,
    bias_ref,
    total_ref,
    home_ref,
    place_ref,
    gate_ref,
    low_ref,
    down_ref,
    cos_ref,
    sin_ref,
    cos_all_ref,
    sin_all_ref,
    pair_ref,
    slots_ref,
    sum_ref,
    turned_ref,
):
    rows = cos_ref.shape[0]
    base = nn(place_ref[...], home_ref[...])
    extra = nn(low_ref[...], down_ref[...])
    keys, values = key_ref[...], value_ref[...]
    key_grad = value_grad = None
    for route in range(2):
        part = pl.ds(route * rows, rows)
        query = query_ref[part, :]
        grad = (base[route * rows : (route + 1) * rows] + extra) * gate_ref[part, :]
        grad = grad.astype(bf16)
        scores = nt(query, keys) * scale + bias_ref[...]
        weights = jnp.exp(scores - total_ref[0, part, :])
        weight_grad = nt(grad, values)
        mean_grad = jnp.sum(weights * weight_grad, axis=1, keepdims=True)
        score_grad = (weights * (weight_grad - mean_grad)).astype(bf16)
        query_grad = nn(score_grad, keys) * scale
        query_grad = query_grad * cos_ref[...] - pltpu.roll(query_grad, HD // 2, 1) * sin_ref[...]
        turned_ref[part, :] = query_grad.astype(bf16)
        key_part = tn(score_grad, query)
        value_part = tn(weights.astype(bf16), grad)
        key_grad = key_part if route == 0 else key_grad + key_part
        value_grad = value_part if route == 0 else value_grad + value_part
    key_grad = key_grad * scale
    key_grad = key_grad * cos_all_ref[...] - pltpu.roll(key_grad, HD // 2, 1) * sin_all_ref[...]
    pair_ref[0, :, :] = key_grad.astype(bf16)
    pair_ref[1, :, :] = value_grad.astype(bf16)
    slots_ref[...] = tn(place_ref[...], turned_ref[...]).astype(bf16)
    first = turned_ref[pl.ds(0, rows), :].astype(f32)
    sum_ref[...] = (first + turned_ref[pl.ds(rows, rows), :].astype(f32)).astype(bf16)


def attend_back(query, pairs, bias, totals, home, place, gates, low, down, cosine, sine, cosine_all, sine_all):
    rows2, slots = place.shape
    rows, length = bias.shape
    heads = home.shape[1] // HD
    kv_heads = pairs.shape[1] // (2 * HD)
    whole = lambda array: pl.BlockSpec(array.shape, lambda h: (0, 0))
    return pl.pallas_call(
        functools.partial(attend_back_kernel, 1.0 / math.sqrt(HD)),
        grid=(heads,),
        in_specs=[
            pl.BlockSpec((rows2, HD), lambda h: (0, h)),
            pl.BlockSpec((length, HD), lambda h: (0, h)),
            pl.BlockSpec((length, HD), lambda h: (0, kv_heads + h)),
            whole(bias),
            pl.BlockSpec((1, rows2, 1), lambda h: (h, 0, 0)),
            pl.BlockSpec((slots, HD), lambda h: (0, h)),
            whole(place),
            whole(gates),
            whole(low),
            pl.BlockSpec((down.shape[0], HD), lambda h: (0, h)),
            whole(cosine),
            whole(sine),
            whole(cosine_all),
            whole(sine_all),
        ],
        out_specs=[
            pl.BlockSpec((2, length, HD), lambda h: (0, 0, h)),
            pl.BlockSpec((slots, HD), lambda h: (0, h)),
            pl.BlockSpec((rows, HD), lambda h: (0, h)),
        ],
        out_shape=[
            jax.ShapeDtypeStruct((2, length, heads * HD), bf16),
            jax.ShapeDtypeStruct((slots, heads * HD), bf16),
            jax.ShapeDtypeStruct((rows, heads * HD), bf16),
        ],
        scratch_shapes=[pltpu.VMEM((rows2, HD), bf16)],
        compiler_params=pltpu.CompilerParams(vmem_limit_bytes=vmem_bytes),
        cost_estimate=pl.CostEstimate(
            flops=10 * heads * rows2 * length * HD,
            bytes_accessed=8 * length * heads * HD,
            transcendentals=heads * rows2 * length,
        ),
        name="attend_back",
    )(query, pairs, pairs, bias, totals, home, place, gates, low, down, cosine, sine, cosine_all, sine_all)


def exchange(buffer):
    return lax.all_to_all(buffer, "dp", split_axis=0, concat_axis=0, tiled=True)


def shifted(array, shift, size):
    if shift == 0:
        return array
    return lax.ppermute(array, "seq", [(k, (k - shift) % size) for k in range(size)])


def send_full(slots, experts, copies):
    buffer = slots.reshape(experts, slots.shape[0] // experts, slots.shape[1])
    if copies > 1:
        buffer = jnp.repeat(buffer, copies, axis=0)
    return exchange(buffer)


def send_cut(slots, experts, copies):
    buffer = slots.reshape(experts, slots.shape[0] // experts, slots.shape[1])
    if copies > 1:
        _, rows, columns = buffer.shape
        buffer = buffer.reshape(experts, rows, copies, columns // copies).transpose(0, 2, 1, 3)
        buffer = buffer.reshape(experts * copies, rows, columns // copies)
    return exchange(buffer)


def home_join(parts, experts, copies):
    home = exchange(parts)
    _, rows, columns = home.shape
    if copies > 1:
        home = home.reshape(experts, copies, rows, columns).transpose(0, 2, 1, 3)
    return home.reshape(experts * rows, copies * columns)


def home_add(parts, experts, copies):
    home = exchange(parts)
    _, rows, columns = home.shape
    if copies > 1:
        home = home.reshape(experts, copies, rows, columns).astype(f32)
        home = jnp.sum(home, axis=1).astype(parts.dtype)
    return home.reshape(experts * rows, columns)


def slot_layout(route_ids, experts, capacity):
    flat = route_ids.T.reshape(-1)
    count = flat.shape[0]
    hits = flat[:, None] == jnp.arange(experts)[None, :]
    earlier = jnp.arange(count)[:, None] > jnp.arange(count)[None, :]
    before = nn(earlier.astype(bf16), hits.astype(bf16))
    rank = jnp.sum(jnp.where(hits, before, 0.0), axis=1).astype(jnp.int32)
    slot = flat * capacity + rank
    return (slot[:, None] == jnp.arange(experts * capacity)[None, :]).astype(bf16)


def either(place):
    rows = place.shape[0] // 2
    return place[:rows] + place[rows:]


def norm_back(values, scale, gain, grad):
    weighted = grad * gain
    mean = jnp.mean(weighted * values, axis=-1, keepdims=True)
    return weighted * scale - values * (scale * scale * scale * mean)


def norm_scale(values):
    return lax.rsqrt(jnp.mean(values * values, axis=-1, keepdims=True) + norm_eps)


def gate_pair(logits, route_ids):
    hits = (route_ids[:, :, None] == jnp.arange(logits.shape[1])).astype(f32)
    chosen = jnp.sum(hits * logits[:, None, :], axis=2)
    weights = jnp.exp(chosen - jnp.max(chosen, axis=1, keepdims=True))
    return weights / jnp.sum(weights, axis=1, keepdims=True), hits


def gate_back(gates, hits, grad):
    mean = jnp.sum(gates * grad, axis=1, keepdims=True)
    return jnp.sum((gates * (grad - mean))[:, :, None] * hits, axis=1)


def rope_full(positions):
    half = HD // 2
    frequency = jnp.power(rope_base, -jnp.arange(half).astype(f32) / half)
    angles = positions.astype(f32)[:, None] * frequency[None, :]
    cosine, sine = jnp.cos(angles), jnp.sin(angles)
    return jnp.concatenate([cosine, cosine], 1), jnp.concatenate([-sine, sine], 1)


def picked(lookup, index):
    return lax.dynamic_index_in_dim(lookup, index, 0, keepdims=False)


def body(
    tokens,
    norm_gain,
    key_value_weight,
    router_weight,
    query_weight,
    output_weight,
    mlp_gain,
    mlp_router_weight,
    mlp_in_weight,
    mlp_out_weight,
    key_value_down,
    key_value_up,
    query_down,
    query_up,
    output_down,
    output_up,
    mlp_in_down,
    mlp_in_up,
    mlp_out_down,
    mlp_out_up,
    routes,
    mlp_routes,
    adapter_index,
    prefix_length,
    out_grad,
):
    seqs, rows, width = tokens.shape
    assert seqs == 1
    size, spot = lax.axis_size("seq"), lax.axis_index("seq")
    holders, holder = lax.axis_size("dp"), lax.axis_index("dp")
    experts = router_weight.shape[1]
    copies = holders // experts
    part = holder % copies
    capacity = 3 * rows // 8
    length = rows * size
    adapters, _, rank = key_value_down.shape
    codes = adapters * rank
    hidden = mlp_in_weight.shape[2] // 2
    share = hidden // size

    def flat_down(lookup):
        return lookup.transpose(0, 2, 1)

    adapter = adapter_index[0]
    adapter_all = lax.all_gather(adapter_index, "dp", axis=0, tiled=True)

    piece = key_value_weight.shape[0] // holders
    pair_weight = lax.all_gather(
        lax.dynamic_slice_in_dim(key_value_weight, holder * piece, piece, 0),
        ("seq", "dp"),
        axis=0,
        tiled=True,
    )
    query_full = lax.all_gather(query_weight[0], "seq", axis=0, tiled=True)
    output_full = lax.all_gather(output_weight[0], "seq", axis=0, tiled=True)
    inner_cut = mlp_in_weight[0].reshape(-1, 2, size, share)
    inner_full = jnp.zeros((size, inner_cut.shape[0], 2 * share), bf16)
    for shift in range(size):
        target = (spot - shift) % size
        sent = lax.dynamic_index_in_dim(inner_cut, target, 2, keepdims=False)
        got = shifted(sent.reshape(-1, 2 * share), shift, size)
        inner_full = lax.dynamic_update_index_in_dim(inner_full, got, (spot + shift) % size, 0)
    inner_full = inner_full.reshape(-1, 2 * share)
    outer_full = mlp_out_weight[0]

    inputs = tokens[0].astype(f32)
    input_scale = norm_scale(inputs)
    normed = (inputs * input_scale * norm_gain).astype(bf16)
    pair_down, pair_up = picked(flat_down(key_value_down), adapter), picked(key_value_up, adapter)
    query_lower, query_upper = picked(flat_down(query_down), adapter), picked(query_up, adapter)
    output_lower, output_upper = picked(flat_down(output_down), adapter), picked(output_up, adapter)
    pair_low = nt(normed, pair_down).astype(bf16)
    query_low = nt(normed, query_lower).astype(bf16)
    cosine_all, sine_all = rope_full(jnp.arange(length))
    positions = spot * rows + jnp.arange(rows)
    cosine = lax.dynamic_slice_in_dim(cosine_all, spot * rows, rows, 0)
    sine = lax.dynamic_slice_in_dim(sine_all, spot * rows, rows, 0)
    key_pos = jnp.arange(length)
    allowed = (key_pos[None, :] <= positions[:, None]) | (key_pos[None, :] < prefix_length[0])
    bias = jnp.where(allowed, 0.0, masked_score).astype(f32)
    pairs_local = project_pairs(normed, pair_weight, pair_low, pair_up, cosine, sine)
    pairs = lax.all_gather(pairs_local, "seq", axis=0, tiled=True)

    gates, hits = gate_pair(nn(normed, router_weight), routes[0])
    place = slot_layout(routes[0], experts, capacity)
    place_any = either(place)

    query_rows = send_full(tn(place_any, normed).astype(bf16), experts, copies)
    query_parts = nn(query_rows.reshape(-1, width), query_full).astype(bf16)
    query_home = home_join(query_parts.reshape(holders, capacity, -1), experts, copies)
    attended, output_slots, query_rot, totals = attend(
        query_home, place, query_low, query_upper, cosine, sine, pairs, bias
    )

    output_rows = send_cut(output_slots, experts, copies)
    output_parts = nn(output_rows.reshape(holders * capacity, -1), output_full).astype(bf16)
    output_home = home_add(output_parts.reshape(holders, capacity, width), experts, copies)
    output_low = nt(attended, output_lower).astype(bf16)
    branch = nn(place, output_home) + nn(output_low, output_upper)
    branch = branch.reshape(2, rows, width)
    middle = inputs + gates[:, :1] * branch[0] + gates[:, 1:] * branch[1]
    middle_scale = norm_scale(middle)
    normed_mlp = (middle * middle_scale * mlp_gain).astype(bf16)
    mlp_gates, mlp_hits = gate_pair(nn(normed_mlp, mlp_router_weight), mlp_routes[0])

    mask = (jnp.arange(codes)[None, None, :] // rank == adapter_all[:, None, None]).astype(bf16)
    mask = jnp.broadcast_to(mask, (holders, capacity, codes)).reshape(-1, codes)
    inner_down = flat_down(mlp_in_down).reshape(codes, width)
    outer_up = mlp_out_up.reshape(codes, width)
    inner_up = mlp_in_up.reshape(codes, 2, copies, size, share)
    inner_up = lax.dynamic_index_in_dim(inner_up, part, 2, keepdims=False)
    inner_up = lax.dynamic_index_in_dim(inner_up, spot, 2, keepdims=False).reshape(codes, 2 * share)
    outer_down = flat_down(mlp_out_down).reshape(codes, copies, size, share)
    outer_down = lax.dynamic_index_in_dim(outer_down, part, 1, keepdims=False)
    outer_down = lax.dynamic_index_in_dim(outer_down, spot, 1, keepdims=False)

    places = [slot_layout(shifted(mlp_routes[0], d, size), experts, capacity) for d in range(size)]
    grad_rows, hidden_grads, outer_codes = [], [], []
    for d in range(size):
        rows_there = shifted(out_grad[0], d, size)
        got = send_full(tn(either(places[d]), rows_there).astype(bf16), experts, copies)
        got = got.reshape(-1, width)
        code = nt(got, outer_up).astype(bf16) * mask
        grad_rows.append(got)
        outer_codes.append(code)
        hidden_grads.append((nt(got, outer_full) + nn(code, outer_down)).astype(bf16))

    order = list(range(size))
    gates_there = [shifted(mlp_gates, d, size) for d in order]
    gate_slots = jnp.stack(
        [
            jnp.sum(places[d].astype(f32) * gates_there[d].T.reshape(-1)[:, None], axis=0)
            for d in order
        ]
    )
    gate_slots = gate_slots.reshape(size, experts, capacity).transpose(1, 0, 2)
    gate_slots = exchange(jnp.repeat(gate_slots, copies, axis=0))

    row_total, down_total = None, None
    gate_sums, sums = [], None
    for d in order:
        rows_there = shifted(normed_mlp, d, size)
        got = send_full(tn(either(places[d]), rows_there).astype(bf16), experts, copies)
        got = got.reshape(-1, width)
        code = nt(got, inner_down).astype(bf16) * mask
        pre = nn(got, inner_full) + nn(code, inner_up)
        gate_part, up_part = pre[:, :share], pre[:, share:]
        sigmoid = 1.0 / (1.0 + jnp.exp(-gate_part))
        active = gate_part * sigmoid
        activated = (active * up_part).astype(bf16)
        hidden_grad = hidden_grads[d].astype(f32)
        gate_sums.append(jnp.sum(activated.astype(f32) * hidden_grad, axis=1))
        pre_grad = jnp.concatenate(
            [
                (hidden_grad * up_part * sigmoid * (1.0 + gate_part * (1.0 - sigmoid))).astype(bf16),
                (hidden_grad * active).astype(bf16),
            ],
            axis=1,
        )
        code_grad = nt(pre_grad, inner_up).astype(bf16) * mask
        row_grad = (nt(pre_grad, inner_full) + nn(code_grad, inner_down)).astype(bf16)
        outer_low = nt(activated, outer_down).astype(bf16) * mask
        down = (nn(activated, outer_full) + nn(outer_low, outer_up)).astype(bf16)
        weight = gates_there[d].T.reshape(-1)[:, None]
        combine = either((places[d].astype(f32) * weight).astype(bf16))
        row_home = home_add(row_grad.reshape(holders, capacity, width), experts, copies)
        row_back = shifted(nn(combine, row_home).astype(bf16), -d % size, size).astype(f32)
        row_total = row_back if row_total is None else row_total + row_back
        down_home = home_add(down.reshape(holders, capacity, width), experts, copies)
        down_back = shifted(nn(combine, down_home).astype(bf16), -d % size, size).astype(f32)
        down_total = down_back if down_total is None else down_total + down_back
        scale = gate_slots[:, d, :].reshape(-1, 1)

        def scaled(array):
            return (array.astype(f32) * scale).astype(bf16)

        new = (
            tn(scaled(code), pre_grad),
            tn(scaled(outer_codes[d]), activated),
            tn(scaled(code_grad), got),
            tn(scaled(outer_low), grad_rows[d]),
        )
        sums = new if sums is None else tuple(a + b for a, b in zip(sums, new))

    gate_sums = jnp.stack(gate_sums, 0).reshape(size, holders, capacity).transpose(1, 0, 2)
    gate_sums = exchange(gate_sums).reshape(experts, copies, size, capacity)
    gate_sums = jnp.sum(gate_sums, axis=1).transpose(1, 0, 2).reshape(size, -1)
    gate_parts = [
        jnp.sum(places[d].astype(f32) * gate_sums[d][None, :], axis=1).reshape(2, rows)
        for d in range(size)
    ]
    mlp_gate_grad = gate_parts[0]
    for d in range(1, size):
        mlp_gate_grad = mlp_gate_grad + shifted(gate_parts[d], -d % size, size)
    mlp_logit_grad = gate_back(mlp_gates, mlp_hits, mlp_gate_grad.T)
    result = (middle + down_total).astype(bf16)

    inner_up_sum, outer_down_sum, inner_down_sum, outer_up_sum = sums

    def widened(array):
        if copies == 1:
            return array
        whole = jnp.zeros((codes, copies, array.shape[1]), f32)
        whole = lax.dynamic_update_index_in_dim(whole, array, part, 1)
        return whole.reshape(codes, -1)

    wide = [widened(inner_up_sum), widened(outer_down_sum), inner_down_sum, outer_up_sum]
    ends = [sum(a.shape[1] for a in wide[: k + 1]) for k in range(3)]
    mlp_sums = lax.psum_scatter(
        jnp.concatenate(wide, axis=1), "dp", scatter_dimension=0, tiled=True
    ).astype(bf16)
    mlp_sums = lax.all_gather(mlp_sums, ("seq", "dp"), axis=0, tiled=True)
    mlp_sums = mlp_sums.astype(f32).reshape(size, codes, -1)
    inner_up_grad, outer_down_grad, inner_down_grad, outer_up_grad = jnp.split(mlp_sums, ends, axis=2)
    inner_up_grad = inner_up_grad.reshape(size, codes, copies, 2, share).transpose(1, 3, 2, 0, 4)
    inner_up_grad = inner_up_grad.reshape(adapters, rank, -1)
    outer_down_grad = outer_down_grad.reshape(size, codes, copies, share).transpose(1, 2, 0, 3)
    outer_down_grad = outer_down_grad.reshape(adapters, rank, -1).transpose(0, 2, 1)
    inner_down_grad = jnp.sum(inner_down_grad, 0).reshape(adapters, rank, width).transpose(0, 2, 1)
    outer_up_grad = jnp.sum(outer_up_grad, 0).reshape(adapters, rank, width)

    normed_mlp_grad = row_total + nt(mlp_logit_grad.astype(bf16), mlp_router_weight)
    middle_grad = norm_back(middle, middle_scale, mlp_gain, normed_mlp_grad)
    middle_grad = middle_grad + out_grad[0].astype(f32)
    middle_low = middle_grad.astype(bf16)
    branch_rows = send_full(tn(place_any, middle_low).astype(bf16), experts, copies)
    head_parts = nt(branch_rows.reshape(-1, width), output_full).astype(bf16)
    head_home = home_join(head_parts.reshape(holders, capacity, -1), experts, copies)
    gate_grad = jnp.sum(middle_grad[None] * branch, axis=2).T
    logit_grad = gate_back(gates, hits, gate_grad)
    gate_column = gates.T.reshape(-1, 1)
    output_low_grad = nt(middle_low, output_upper)
    output_low_back = output_low_grad.astype(bf16)
    output_low_scaled = (jnp.tile(output_low_grad, (2, 1)) * gate_column).astype(bf16)
    output_lower_grad = tn(output_low_scaled, attended)
    output_low_sum = (output_low.astype(f32) * gate_column).reshape(2, rows, rank).sum(0)
    output_upper_grad = tn(output_low_sum.astype(bf16), middle_low)

    pair_parts, query_slots, query_sum = attend_back(
        query_rot,
        pairs,
        bias,
        totals,
        head_home,
        place,
        gate_column,
        output_low_back,
        output_lower,
        cosine,
        sine,
        cosine_all,
        sine_all,
    )
    query_back = send_cut(query_slots, experts, copies)
    pair_grad = lax.psum_scatter(pair_parts, "seq", scatter_dimension=1, tiled=True)
    input_parts = nt(query_back.reshape(holders * capacity, -1), query_full).astype(bf16)
    input_home = home_add(input_parts.reshape(holders, capacity, width), experts, copies)
    query_low_grad = nt(query_sum, query_upper).astype(bf16)
    query_upper_grad = tn(query_low, query_sum)
    query_lower_grad = tn(query_low_grad, normed)
    normed_grad = nn(place_any, input_home) + nn(query_low_grad, query_lower)
    normed_grad = normed_grad + nt(logit_grad.astype(bf16), router_weight)
    key_grad, value_grad = pair_grad[0], pair_grad[1]
    half = key_grad.shape[1]
    pair_low_grad = nt(key_grad, pair_up[:, :half]) + nt(value_grad, pair_up[:, half:])
    pair_low_grad = pair_low_grad.astype(bf16)
    pair_upper_grad = jnp.concatenate([tn(pair_low, key_grad), tn(pair_low, value_grad)], axis=1)
    pair_lower_grad = tn(pair_low_grad, normed)
    normed_grad = normed_grad + nt(key_grad, pair_weight[:, :half])
    normed_grad = normed_grad + nt(value_grad, pair_weight[:, half:])
    normed_grad = normed_grad + nn(pair_low_grad, pair_down)
    input_grad = norm_back(inputs, input_scale, norm_gain, normed_grad) + middle_grad

    def over_sequences(arrays):
        ends = [sum(a.shape[1] for a in arrays[: k + 1]) for k in range(len(arrays) - 1)]
        joined = jnp.concatenate(arrays, axis=1)
        joined = joined.reshape(rank, size, -1).transpose(1, 0, 2)
        mine = lax.psum_scatter(joined, "seq", scatter_dimension=0, tiled=True)
        every = lax.all_gather(mine[0].astype(bf16), ("seq", "dp"), axis=0, tiled=False)
        every = every.reshape(size, holders, rank, -1).astype(f32)
        chosen = (adapter_all[:, None] == jnp.arange(adapters)[None, :]).astype(f32)
        total = sum(
            every[:, k, None] * chosen[k][None, :, None, None] for k in range(holders)
        )
        total = total.transpose(1, 2, 0, 3).reshape(adapters, rank, -1)
        return jnp.split(total, ends, axis=2)

    late = over_sequences(
        [
            pair_lower_grad,
            pair_upper_grad,
            query_lower_grad,
            query_upper_grad,
            output_lower_grad,
            output_upper_grad,
        ]
    )
    return (
        result[None],
        input_grad[None],
        late[0].transpose(0, 2, 1),
        late[1],
        late[2].transpose(0, 2, 1),
        late[3],
        late[4].transpose(0, 2, 1),
        late[5],
        inner_down_grad,
        inner_up_grad,
        outer_down_grad,
        outer_up_grad,
    )


def solution(mesh):
    split = P("dp", "seq", None)
    placed = (
        (split, P(), P("seq", None), P(), split, split, P(), P(), split, split)
        + (P(),) * 10
        + (split, split, P("dp"), P("dp"), split)
    )
    return jax.shard_map(
        body,
        mesh=mesh,
        in_specs=placed,
        out_specs=(split, split) + (P(),) * 10,
        check_vma=False,
    )
```

```python
import functools
import math

import jax
import jax.numpy as jnp
import numpy as np
from jax import lax
from jax.experimental import pallas as pl
from jax.experimental.pallas import tpu as pltpu
from jax.sharding import PartitionSpec as P

KV_HEADS = 16
HD = 128

norm_eps = 1e-05
rope_base = 10000.0
masked_score = -1e30
vmem_bytes = 48 * 2**20

bf16 = jnp.bfloat16
f32 = jnp.float32


def product(left, right, left_dim, right_dim):
    return lax.dot_general(
        left, right, (((left_dim,), (right_dim,)), ((), ())), preferred_element_type=f32
    )


def nn(left, right):
    return product(left, right, 1, 0)


def nt(left, right):
    return product(left, right, 1, 1)


def tn(left, right):
    return product(left, right, 0, 0)


def pair_kernel(count, key_blocks, *refs):
    normed_refs = refs[:count]
    w_ref, down_ref, up_ref, cos_ref, sin_ref, out_ref, low_ref = refs[count:]
    rows = normed_refs[0].shape[0]
    step = pl.program_id(0)

    @pl.when(step == 0)
    def _():
        for k in range(count):
            low_ref[pl.ds(k * rows, rows), :] = nt(normed_refs[k][...], down_ref[...]).astype(bf16)

    for k in range(count):
        part = pl.ds(k * rows, rows)
        made = nn(normed_refs[k][...], w_ref[...]) + nn(low_ref[part, :], up_ref[...])

        @pl.when(step < key_blocks)
        def _():
            for start in range(0, made.shape[1], HD):
                head = made[:, start : start + HD]
                turned = head * cos_ref[part, :] + pltpu.roll(head, HD // 2, 1) * sin_ref[part, :]
                out_ref[part, start : start + HD] = turned.astype(bf16)

        @pl.when(step >= key_blocks)
        def _():
            out_ref[part, :] = made.astype(bf16)


def project_pairs(normed_parts, weight, down, upper, cosine, sine):
    count = len(normed_parts)
    rows, width = normed_parts[0].shape
    columns = weight.shape[1]
    block = 512
    whole = lambda array: pl.BlockSpec(array.shape, lambda i: (0, 0))
    return pl.pallas_call(
        functools.partial(pair_kernel, count, columns // 2 // block),
        grid=(columns // block,),
        in_specs=[whole(n) for n in normed_parts]
        + [
            pl.BlockSpec((width, block), lambda i: (0, i)),
            whole(down),
            pl.BlockSpec((upper.shape[0], block), lambda i: (0, i)),
            whole(cosine),
            whole(sine),
        ],
        out_specs=[
            pl.BlockSpec((count * rows, block), lambda i: (0, i)),
            pl.BlockSpec((count * rows, down.shape[0]), lambda i: (0, 0)),
        ],
        out_shape=[
            jax.ShapeDtypeStruct((count * rows, columns), bf16),
            jax.ShapeDtypeStruct((count * rows, down.shape[0]), bf16),
        ],
        compiler_params=pltpu.CompilerParams(vmem_limit_bytes=vmem_bytes),
        cost_estimate=pl.CostEstimate(
            flops=2 * count * rows * width * columns,
            bytes_accessed=2 * width * columns,
            transcendentals=0,
        ),
        name="pairs",
    )(*normed_parts, weight, down, upper, cosine, sine)


def attend_kernel(
    scale,
    home_ref,
    place_ref,
    low_ref,
    up_ref,
    cos_ref,
    sin_ref,
    key_ref,
    value_ref,
    bias_ref,
    attended_ref,
    slots_ref,
    query_ref,
    total_ref,
):
    rows = cos_ref.shape[0]
    base = nn(place_ref[...], home_ref[...])
    extra = nn(low_ref[...], up_ref[...])
    keys, values = key_ref[...], value_ref[...]
    for route in range(2):
        part = pl.ds(route * rows, rows)
        query = base[route * rows : (route + 1) * rows] + extra
        query = query * cos_ref[...] + pltpu.roll(query, HD // 2, 1) * sin_ref[...]
        query = query.astype(bf16)
        query_ref[part, :] = query
        scores = nt(query, keys) * scale + bias_ref[...]
        highest = jnp.max(scores, axis=1, keepdims=True)
        weights = jnp.exp(scores - highest)
        total = jnp.sum(weights, axis=1, keepdims=True)
        attended = nn(weights.astype(bf16), values) / total
        attended_ref[part, :] = attended.astype(bf16)
        total_ref[0, part, :] = highest + jnp.log(total)
    slots_ref[...] = tn(place_ref[...], attended_ref[...]).astype(bf16)


def attend(home, place, low, upper, cosine, sine, pairs, bias):
    rows2, slots = place.shape
    rows, length = bias.shape
    heads = home.shape[1] // HD
    kv_heads = pairs.shape[1] // (2 * HD)
    whole = lambda array: pl.BlockSpec(array.shape, lambda h: (0, 0))
    return pl.pallas_call(
        functools.partial(attend_kernel, 1.0 / math.sqrt(HD)),
        grid=(heads,),
        in_specs=[
            pl.BlockSpec((slots, HD), lambda h: (0, h)),
            whole(place),
            whole(low),
            pl.BlockSpec((upper.shape[0], HD), lambda h: (0, h)),
            whole(cosine),
            whole(sine),
            pl.BlockSpec((length, HD), lambda h: (0, h)),
            pl.BlockSpec((length, HD), lambda h: (0, kv_heads + h)),
            whole(bias),
        ],
        out_specs=[
            pl.BlockSpec((rows2, HD), lambda h: (0, h)),
            pl.BlockSpec((slots, HD), lambda h: (0, h)),
            pl.BlockSpec((rows2, HD), lambda h: (0, h)),
            pl.BlockSpec((1, rows2, 1), lambda h: (h, 0, 0)),
        ],
        out_shape=[
            jax.ShapeDtypeStruct((rows2, heads * HD), bf16),
            jax.ShapeDtypeStruct((slots, heads * HD), bf16),
            jax.ShapeDtypeStruct((rows2, heads * HD), bf16),
            jax.ShapeDtypeStruct((heads, rows2, 1), f32),
        ],
        compiler_params=pltpu.CompilerParams(vmem_limit_bytes=vmem_bytes),
        cost_estimate=pl.CostEstimate(
            flops=4 * heads * rows2 * length * HD,
            bytes_accessed=4 * length * heads * HD,
            transcendentals=heads * rows2 * length,
        ),
        name="attend",
    )(home, place, low, upper, cosine, sine, pairs, pairs, bias)


def attend_back_kernel(
    scale,
    query_ref,
    key_ref,
    value_ref,
    bias_ref,
    total_ref,
    home_ref,
    place_ref,
    gate_ref,
    low_ref,
    down_ref,
    cos_ref,
    sin_ref,
    cos_all_ref,
    sin_all_ref,
    key_grad_ref,
    value_grad_ref,
    slots_ref,
    sum_ref,
    turned_ref,
):
    rows = cos_ref.shape[0]
    base = nn(place_ref[...], home_ref[...])
    extra = nn(low_ref[...], down_ref[...])
    keys, values = key_ref[...], value_ref[...]
    key_grad = value_grad = None
    for route in range(2):
        part = pl.ds(route * rows, rows)
        query = query_ref[part, :]
        grad = (base[route * rows : (route + 1) * rows] + extra) * gate_ref[part, :]
        grad = grad.astype(bf16)
        scores = nt(query, keys) * scale + bias_ref[...]
        weights = jnp.exp(scores - total_ref[0, part, :])
        weight_grad = nt(grad, values)
        mean_grad = jnp.sum(weights * weight_grad, axis=1, keepdims=True)
        score_grad = (weights * (weight_grad - mean_grad)).astype(bf16)
        query_grad = nn(score_grad, keys) * scale
        query_grad = query_grad * cos_ref[...] - pltpu.roll(query_grad, HD // 2, 1) * sin_ref[...]
        turned_ref[part, :] = query_grad.astype(bf16)
        key_part = tn(score_grad, query)
        value_part = tn(weights.astype(bf16), grad)
        key_grad = key_part if route == 0 else key_grad + key_part
        value_grad = value_part if route == 0 else value_grad + value_part
    key_grad = key_grad * scale
    key_grad = key_grad * cos_all_ref[...] - pltpu.roll(key_grad, HD // 2, 1) * sin_all_ref[...]
    key_grad_ref[...] = key_grad.astype(bf16)
    value_grad_ref[...] = value_grad.astype(bf16)
    slots_ref[...] = tn(place_ref[...], turned_ref[...]).astype(bf16)
    first = turned_ref[pl.ds(0, rows), :].astype(f32)
    sum_ref[...] = (first + turned_ref[pl.ds(rows, rows), :].astype(f32)).astype(bf16)


def attend_back(query, pairs, bias, totals, home, place, gates, low, down, cosine, sine, cosine_all, sine_all):
    rows2, slots = place.shape
    rows, length = bias.shape
    heads = home.shape[1] // HD
    kv_heads = pairs.shape[1] // (2 * HD)
    whole = lambda array: pl.BlockSpec(array.shape, lambda h: (0, 0))
    return pl.pallas_call(
        functools.partial(attend_back_kernel, 1.0 / math.sqrt(HD)),
        grid=(heads,),
        in_specs=[
            pl.BlockSpec((rows2, HD), lambda h: (0, h)),
            pl.BlockSpec((length, HD), lambda h: (0, h)),
            pl.BlockSpec((length, HD), lambda h: (0, kv_heads + h)),
            whole(bias),
            pl.BlockSpec((1, rows2, 1), lambda h: (h, 0, 0)),
            pl.BlockSpec((slots, HD), lambda h: (0, h)),
            whole(place),
            whole(gates),
            whole(low),
            pl.BlockSpec((down.shape[0], HD), lambda h: (0, h)),
            whole(cosine),
            whole(sine),
            whole(cosine_all),
            whole(sine_all),
        ],
        out_specs=[
            pl.BlockSpec((length, HD), lambda h: (0, h)),
            pl.BlockSpec((length, HD), lambda h: (0, h)),
            pl.BlockSpec((slots, HD), lambda h: (0, h)),
            pl.BlockSpec((rows, HD), lambda h: (0, h)),
        ],
        out_shape=[
            jax.ShapeDtypeStruct((length, heads * HD), bf16),
            jax.ShapeDtypeStruct((length, heads * HD), bf16),
            jax.ShapeDtypeStruct((slots, heads * HD), bf16),
            jax.ShapeDtypeStruct((rows, heads * HD), bf16),
        ],
        scratch_shapes=[pltpu.VMEM((rows2, HD), bf16)],
        compiler_params=pltpu.CompilerParams(vmem_limit_bytes=vmem_bytes),
        cost_estimate=pl.CostEstimate(
            flops=10 * heads * rows2 * length * HD,
            bytes_accessed=8 * length * heads * HD,
            transcendentals=heads * rows2 * length,
        ),
        name="attend_back",
    )(query, pairs, pairs, bias, totals, home, place, gates, low, down, cosine, sine, cosine_all, sine_all)


def exchange(buffer):
    return lax.all_to_all(buffer, "dp", split_axis=0, concat_axis=0, tiled=True)


def shifted(array, shift, size):
    if shift == 0:
        return array
    return lax.ppermute(array, "seq", [(k, (k - shift) % size) for k in range(size)])


def send_full(slots, experts, copies):
    buffer = slots.reshape(experts, slots.shape[0] // experts, slots.shape[1])
    if copies > 1:
        buffer = jnp.repeat(buffer, copies, axis=0)
    return exchange(buffer)


def send_cut(slots, experts, copies):
    buffer = slots.reshape(experts, slots.shape[0] // experts, slots.shape[1])
    if copies > 1:
        _, rows, columns = buffer.shape
        buffer = buffer.reshape(experts, rows, copies, columns // copies).transpose(0, 2, 1, 3)
        buffer = buffer.reshape(experts * copies, rows, columns // copies)
    return exchange(buffer)


def home_join(parts, experts, copies):
    home = exchange(parts)
    _, rows, columns = home.shape
    if copies > 1:
        home = home.reshape(experts, copies, rows, columns).transpose(0, 2, 1, 3)
    return home.reshape(experts * rows, copies * columns)


def home_add(parts, experts, copies):
    home = exchange(parts)
    _, rows, columns = home.shape
    if copies > 1:
        home = home.reshape(experts, copies, rows, columns).astype(f32)
        home = jnp.sum(home, axis=1).astype(parts.dtype)
    return home.reshape(experts * rows, columns)


def slot_layout(route_ids, experts, capacity):
    flat = route_ids.T.reshape(-1)
    count = flat.shape[0]
    hits = flat[:, None] == jnp.arange(experts)[None, :]
    earlier = jnp.arange(count)[:, None] > jnp.arange(count)[None, :]
    before = nn(earlier.astype(bf16), hits.astype(bf16))
    rank = jnp.sum(jnp.where(hits, before, 0.0), axis=1).astype(jnp.int32)
    slot = flat * capacity + rank
    return (slot[:, None] == jnp.arange(experts * capacity)[None, :]).astype(bf16)


def either(place):
    rows = place.shape[0] // 2
    return place[:rows] + place[rows:]


def norm_back(values, scale, gain, grad):
    weighted = grad * gain
    mean = jnp.mean(weighted * values, axis=-1, keepdims=True)
    return weighted * scale - values * (scale * scale * scale * mean)


def norm_scale(values):
    return lax.rsqrt(jnp.mean(values * values, axis=-1, keepdims=True) + norm_eps)


def gate_pair(logits, route_ids):
    hits = (route_ids[:, :, None] == jnp.arange(logits.shape[1])).astype(f32)
    chosen = jnp.sum(hits * logits[:, None, :], axis=2)
    weights = jnp.exp(chosen - jnp.max(chosen, axis=1, keepdims=True))
    return weights / jnp.sum(weights, axis=1, keepdims=True), hits


def gate_back(gates, hits, grad):
    mean = jnp.sum(gates * grad, axis=1, keepdims=True)
    return jnp.sum((gates * (grad - mean))[:, :, None] * hits, axis=1)


def rope_full(length, start):
    half = HD // 2
    frequency = rope_base ** (-np.arange(half) / half)
    angles = np.arange(length)[:, None] * frequency[None, :]
    cosine, sine = np.cos(angles), np.sin(angles)
    tables = np.concatenate([cosine, cosine, -sine, sine], 1).astype(np.float32)
    tables = jnp.asarray(np.concatenate([tables, tables], 0))
    tables = lax.dynamic_slice_in_dim(tables, start, length, 0)
    return tables[:, :HD], tables[:, HD:]


def after(array, *earlier):
    return lax.optimization_barrier((array,) + earlier)[0]


def cut_kernel(target_ref, in_ref, out_ref):
    out_ref[...] = in_ref[...]


def cut_share(weight, target, size):
    rows, columns = weight.shape
    share = columns // 2 // size
    if share % 128:
        cut = weight.reshape(rows, 2, size, share)
        return lax.dynamic_index_in_dim(cut, target, 2, keepdims=False).reshape(rows, 2 * share)
    return pl.pallas_call(
        cut_kernel,
        grid_spec=pltpu.PrefetchScalarGridSpec(
            num_scalar_prefetch=1,
            grid=(2,),
            in_specs=[pl.BlockSpec((rows, share), lambda i, t: (0, i * size + t[0]))],
            out_specs=pl.BlockSpec((rows, share), lambda i, t: (0, i)),
        ),
        out_shape=jax.ShapeDtypeStruct((rows, 2 * share), bf16),
        compiler_params=pltpu.CompilerParams(vmem_limit_bytes=vmem_bytes),
        name="cut",
    )(target.reshape(1).astype(jnp.int32), weight)


def unpack_kernel(size, share, in_ref, inner_up_ref, outer_down_ref, inner_down_ref, outer_up_ref):
    spot = pl.program_id(1)
    got = in_ref[0, 0].astype(f32)
    hidden = size * share
    width = inner_down_ref.shape[2]
    start = pl.multiple_of(spot * share, 128)
    inner_up_ref[0, :, pl.ds(start, share)] = got[:, :share]
    inner_up_ref[0, :, pl.ds(pl.multiple_of(hidden + start, 128), share)] = got[:, share : 2 * share]
    outer_down_ref[0, :, pl.ds(start, share)] = got[:, 2 * share : 3 * share]
    inner_down = got[:, 3 * share : 3 * share + width]
    outer_up = got[:, 3 * share + width :]

    @pl.when(spot == 0)
    def _():
        inner_down_ref[0] = inner_down
        outer_up_ref[0] = outer_up

    @pl.when(spot > 0)
    def _():
        inner_down_ref[0] += inner_down
        outer_up_ref[0] += outer_up


def unpack_sums(sums, share, width):
    size, adapters, rank, columns = sums.shape
    hidden = size * share
    shapes = [2 * hidden, hidden, width, width]
    return pl.pallas_call(
        functools.partial(unpack_kernel, size, share),
        grid=(adapters, size),
        in_specs=[pl.BlockSpec((1, 1, rank, columns), lambda a, k: (k, a, 0, 0))],
        out_specs=[pl.BlockSpec((1, rank, n), lambda a, k: (a, 0, 0)) for n in shapes],
        out_shape=[jax.ShapeDtypeStruct((adapters, rank, n), f32) for n in shapes],
        compiler_params=pltpu.CompilerParams(vmem_limit_bytes=vmem_bytes),
        name="unpack",
    )(sums)


def silu_parts(gate_part, up_part, hidden_grad):
    sigmoid = 1.0 / (1.0 + jnp.exp(-gate_part))
    active = gate_part * sigmoid
    activated = (active * up_part).astype(bf16)
    gate_grad = hidden_grad * up_part * sigmoid * (1.0 + gate_part * (1.0 - sigmoid))
    return activated, gate_grad.astype(bf16), (hidden_grad * active).astype(bf16)


def halves(value):
    high = value.astype(bf16)
    return high, (value - high.astype(f32)).astype(bf16)


def expert_kernel(size, share, spot_ref, x_ref, hidden_ref, mask_ref, up_ref, down_ref, *refs):
    w_refs = refs[:size]
    row_ref, active_ref, pre_ref, code_ref, back_ref = refs[size:]
    depth = w_refs[0].shape[0]
    width = size * depth
    columns = [pl.ds(pl.multiple_of((spot_ref[0] + k) % size * depth, 128), depth) for k in range(size)]
    code = nt(x_ref[...], down_ref[...]).astype(bf16) * mask_ref[...]
    code_ref[...] = code
    sums = None
    for start in range(0, share, 256):
        end = min(start + 256, share)

        def hidden(first, last):
            made = nn(code, up_ref[:, first:last])
            for k in range(size):
                made = made + nn(x_ref[:, columns[k]], w_refs[k][:, first:last])
            return made

        gate_part, up_part = hidden(start, end), hidden(share + start, share + end)
        hidden_grad = hidden_ref[:, start:end].astype(f32)
        activated, gate_grad, up_grad = silu_parts(gate_part, up_part, hidden_grad)
        active_ref[:, start:end] = activated
        pre_ref[:, start:end] = gate_grad
        pre_ref[:, share + start : share + end] = up_grad
        part = jnp.sum(activated.astype(f32) * hidden_grad, axis=1, keepdims=True)
        sums = part if sums is None else sums + part
    back = nt(pre_ref[...], up_ref[...]).astype(bf16) * mask_ref[...]
    back_ref[...] = back
    for k in range(size):
        base = (spot_ref[0] + k) % size * depth
        for start in range(0, depth, 256):
            end = min(start + 256, depth)
            here = pl.ds(pl.multiple_of(base + start, 128), end - start)
            made = nt(pre_ref[...], w_refs[k][start:end, :]) + nn(back, down_ref[:, here])
            row_ref[:, here] = made.astype(bf16)
    high, low = halves(sums)
    lane = lax.broadcasted_iota(jnp.int32, (sums.shape[0], 128), 1)
    packed = jnp.where(lane == 0, high.astype(f32), jnp.where(lane == 1, low.astype(f32), 0.0))
    row_ref[:, width:] = packed.astype(bf16)


def expert_block(got, hidden_grad, mask, inner_up, inner_down, inner_parts, spot):
    size = len(inner_parts)
    rows, width = got.shape
    share = hidden_grad.shape[1]
    codes = mask.shape[1]
    if share % 128 or width // size % 256:
        code = nt(got, inner_down).astype(bf16) * mask
        twice = jnp.concatenate(inner_parts + inner_parts, axis=0)
        first = (size - spot) % size * (width // size)
        inner_full = lax.dynamic_slice_in_dim(twice, first, width, 0)
        pre = nn(got, inner_full) + nn(code, inner_up)
        hidden_float = hidden_grad.astype(f32)
        activated, gate_grad, up_grad = silu_parts(pre[:, :share], pre[:, share:], hidden_float)
        pre_grad = jnp.concatenate([gate_grad, up_grad], axis=1)
        back = nt(pre_grad, inner_up).astype(bf16) * mask
        row_grad = (nt(pre_grad, inner_full) + nn(back, inner_down)).astype(bf16)
        sums = jnp.stack(halves(jnp.sum(activated.astype(f32) * hidden_float, axis=1)), axis=1)
        row_grad = jnp.concatenate([row_grad, jnp.pad(sums, ((0, 0), (0, 126)))], axis=1)
        return row_grad, activated, pre_grad, code, back
    block = rows // 2
    ahead = lambda n: pl.BlockSpec((block, n), lambda i, s: (i, 0))
    whole = lambda array: pl.BlockSpec(array.shape, lambda i, s: (0, 0), pipeline_mode=pl.Buffered(1))
    shapes = [width + 128, share, 2 * share, codes, codes]
    return pl.pallas_call(
        functools.partial(expert_kernel, size, share),
        grid_spec=pltpu.PrefetchScalarGridSpec(
            num_scalar_prefetch=1,
            grid=(2,),
            in_specs=[ahead(width), ahead(share), ahead(codes), whole(inner_up), whole(inner_down)]
            + [whole(part) for part in inner_parts],
            out_specs=[ahead(n) for n in shapes],
        ),
        out_shape=[jax.ShapeDtypeStruct((rows, n), bf16) for n in shapes],
        compiler_params=pltpu.CompilerParams(vmem_limit_bytes=vmem_bytes),
        cost_estimate=pl.CostEstimate(
            flops=8 * rows * width * share,
            bytes_accessed=4 * width * share + 10 * rows * width,
            transcendentals=rows * share,
        ),
        name="experts",
    )(spot.reshape(1).astype(jnp.int32), got, hidden_grad, mask, inner_up, inner_down, *inner_parts)


def picked(lookup, index):
    return lax.dynamic_index_in_dim(lookup, index, 0, keepdims=False)


def body(
    tokens,
    norm_gain,
    key_value_weight,
    router_weight,
    query_weight,
    output_weight,
    mlp_gain,
    mlp_router_weight,
    mlp_in_weight,
    mlp_out_weight,
    key_value_down,
    key_value_up,
    query_down,
    query_up,
    output_down,
    output_up,
    mlp_in_down,
    mlp_in_up,
    mlp_out_down,
    mlp_out_up,
    routes,
    mlp_routes,
    adapter_index,
    prefix_length,
    out_grad,
):
    seqs, rows, width = tokens.shape
    assert seqs == 1
    size, spot = lax.axis_size("seq"), lax.axis_index("seq")
    holders, holder = lax.axis_size("dp"), lax.axis_index("dp")
    experts = router_weight.shape[1]
    copies = holders // experts
    part = holder % copies
    capacity = 3 * rows // 8
    length = rows * size
    adapters, _, rank = key_value_down.shape
    codes = adapters * rank
    hidden = mlp_in_weight.shape[2] // 2
    share = hidden // size

    def flat_down(lookup):
        return lookup.transpose(0, 2, 1)

    adapter = adapter_index[0]
    adapter_all = exchange(jnp.broadcast_to(adapter_index[None], (holders, 128)))[:, 0]
    inputs = tokens[0].astype(f32)
    input_scale = norm_scale(inputs)
    normed = (inputs * input_scale * norm_gain).astype(bf16)

    piece = key_value_weight.shape[0] // holders
    pair_weight = lax.all_gather(
        lax.dynamic_slice_in_dim(key_value_weight, holder * piece, piece, 0),
        ("seq", "dp"),
        axis=0,
        tiled=True,
    )
    lanes = jnp.pad(mlp_routes[0].astype(bf16), ((0, 0), (0, 126)))
    packet = jnp.concatenate([normed, out_grad[0], lanes], axis=1)
    early = [packet] + [shifted(packet, d, size) for d in range(1, size)]
    normed_parts = [normed] + [p[:, :width] for p in early[1:]]
    grad_parts = [out_grad[0]] + [p[:, width : 2 * width] for p in early[1:]]
    routes_there = [p[:, 2 * width : 2 * width + 2].astype(jnp.int32) for p in early]
    gates, hits = gate_pair(nn(normed, router_weight), routes[0])
    place = slot_layout(routes[0], experts, capacity)
    place_any = either(place)
    query_rows = send_full(tn(place_any, normed).astype(bf16), experts, copies)
    query_own = after(query_weight[0], pair_weight, query_rows, *early[1:])
    query_full = lax.all_gather(query_own, "seq", axis=0, tiled=True)
    output_full = lax.all_gather(after(output_weight[0], query_full), "seq", axis=0, tiled=True)
    outer_full = mlp_out_weight[0]

    pair_down, pair_up = picked(flat_down(key_value_down), adapter), picked(key_value_up, adapter)
    query_lower, query_upper = picked(flat_down(query_down), adapter), picked(query_up, adapter)
    output_lower, output_upper = picked(flat_down(output_down), adapter), picked(output_up, adapter)
    query_low = nt(normed, query_lower).astype(bf16)
    positions = spot * rows + jnp.arange(rows)
    key_pos = (spot * rows + jnp.arange(length)) % length
    cosine_all, sine_all = rope_full(length, spot * rows)
    cosine, sine = cosine_all[:rows], sine_all[:rows]
    allowed = (key_pos[None, :] <= positions[:, None]) | (key_pos[None, :] < prefix_length[0])
    bias = jnp.where(allowed, 0.0, masked_score).astype(f32)

    mask = (jnp.arange(codes)[None, None, :] // rank == adapter_all[:, None, None]).astype(bf16)
    mask = jnp.broadcast_to(mask, (holders, capacity, codes)).reshape(-1, codes)
    inner_down = flat_down(mlp_in_down).reshape(codes, width)
    outer_up = mlp_out_up.reshape(codes, width)
    inner_up = mlp_in_up.reshape(codes, 2, copies, size, share)
    inner_up = lax.dynamic_index_in_dim(inner_up, part, 2, keepdims=False)
    inner_up = lax.dynamic_index_in_dim(inner_up, spot, 2, keepdims=False).reshape(codes, 2 * share)
    outer_down = flat_down(mlp_out_down).reshape(codes, copies, size, share)
    outer_down = lax.dynamic_index_in_dim(outer_down, part, 1, keepdims=False)
    outer_down = lax.dynamic_index_in_dim(outer_down, spot, 1, keepdims=False)

    places = [slot_layout(routes_there[d], experts, capacity) for d in range(size)]
    grad_rows, hidden_grads, outer_codes = [], [], []
    for d in range(size):
        got = send_full(tn(either(places[d]), grad_parts[d]).astype(bf16), experts, copies)
        got = got.reshape(-1, width)
        code = nt(got, outer_up).astype(bf16) * mask
        grad_rows.append(got)
        outer_codes.append(code)
        hidden_grads.append((nt(got, outer_full) + nn(code, outer_down)).astype(bf16))

    query_parts = nn(query_rows.reshape(-1, width), query_full).astype(bf16)
    query_home = home_join(query_parts.reshape(holders, capacity, -1), experts, copies)
    pairs, pair_low = project_pairs(
        normed_parts, pair_weight, pair_down, pair_up, cosine_all, sine_all
    )
    far = size // 2
    inner_sent = [cut_share(mlp_in_weight[0], (spot - d) % size, size) for d in range(size)]
    inner_parts = list(inner_sent)
    inner_parts[far] = shifted(after(inner_sent[far], query_full), far, size)
    query_home = after(query_home, *grad_rows[:2])
    attended, output_slots, query_rot, totals = attend(
        query_home, place, query_low, query_upper, cosine, sine, pairs, bias
    )

    output_rows = send_cut(output_slots, experts, copies)
    output_rows = after(output_rows, inner_parts[far], *grad_rows[2:])
    output_parts = nn(output_rows.reshape(holders * capacity, -1), output_full).astype(bf16)
    distances = [d for d in range(1, size) if d != far]
    for d in distances[:-1]:
        inner_parts[d] = shifted(after(inner_sent[d], output_full), d, size)
    output_home = home_add(output_parts.reshape(holders, capacity, width), experts, copies)
    output_low = nt(attended, output_lower).astype(bf16)
    branch = nn(place, output_home) + nn(output_low, output_upper)
    branch = branch.reshape(2, rows, width)
    middle = inputs + gates[:, :1] * branch[0] + gates[:, 1:] * branch[1]
    middle_scale = norm_scale(middle)
    normed_mlp = (middle * middle_scale * mlp_gain).astype(bf16)
    mlp_gates, mlp_hits = gate_pair(nn(normed_mlp, mlp_router_weight), mlp_routes[0])

    lanes = jnp.pad(jnp.concatenate(halves(mlp_gates), axis=1), ((0, 0), (0, 124)))
    packet = jnp.concatenate([normed_mlp, lanes], axis=1)
    packet = after(packet, *(inner_parts[d] for d in distances[:-1]))
    packet_all = lax.all_gather(packet, "seq", axis=0, tiled=True)
    for d in distances[-1:]:
        inner_parts[d] = shifted(after(inner_sent[d], inner_parts[distances[0]]), d, size)
    packet_all = after(packet_all, *(inner_parts[d] for d in distances[-1:]))
    packets = [packet] + [
        lax.dynamic_slice_in_dim(packet_all, (spot + d) % size * rows, rows, 0)
        for d in range(1, size)
    ]
    gates_there = [
        (p[:, width : width + 2].astype(f32) + p[:, width + 2 : width + 4].astype(f32)).T.reshape(-1, 1)
        for p in packets
    ]
    combines = [either((places[d].astype(f32) * gates_there[d]).astype(bf16)) for d in range(size)]
    got_rows = [
        send_full(tn(either(places[d]), packets[d][:, :width]).astype(bf16), experts, copies)
        for d in range(size)
    ]
    gate_slots = jnp.stack(
        [jnp.sum(places[d].astype(f32) * gates_there[d], axis=0) for d in range(size)]
    )
    gate_slots = gate_slots.reshape(size, experts, capacity).transpose(1, 0, 2)
    gate_slots = exchange(jnp.repeat(gate_slots, copies, axis=0))

    order = [d for d in range(1, size) if d != far] + ([far] if size > 1 else []) + [0]
    kept, row_total, backs = {}, None, []
    for turn, d in enumerate(order):
        if turn:
            got_rows[d] = after(got_rows[d], kept[order[turn - 1]][0])
        kept[d] = expert_block(
            got_rows[d].reshape(-1, width),
            hidden_grads[d],
            mask,
            inner_up,
            inner_down,
            inner_parts,
            spot,
        )
        row_grad = after(kept[d][0], backs[0]) if turn > 2 else kept[d][0]
        row_home = home_add(row_grad.reshape(holders, capacity, -1), experts, copies)
        row_sum = nn(combines[d], row_home[:, :width])
        gate_sum = nn(places[d], row_home[:, width:])
        lanes = gate_sum[:rows] + jnp.roll(gate_sum[rows:], 2, axis=1)
        row_back = jnp.concatenate([row_sum, lanes], axis=1)
        if d:
            row_back = shifted(row_back.astype(bf16), -d % size, size)
        backs.append(row_back)
        row_back = row_back.astype(f32)
        row_total = row_back if row_total is None else row_total + row_back
    gate_sum = row_total[:, width : width + 4]
    row_total = row_total[:, :width]
    mlp_gate_grad = gate_sum.reshape(rows, 2, 2).sum(2)
    mlp_logit_grad = gate_back(mlp_gates, mlp_hits, mlp_gate_grad)

    down_near, down_parts, down_sent, sums = [], [], [], None
    for d in order:
        _, activated, pre_grad, code, back = kept[d]
        outer_low = nt(activated, outer_down).astype(bf16) * mask
        down = (nn(activated, outer_full) + nn(outer_low, outer_up)).astype(bf16)
        if d in (0, 1, size - 1):
            if d:
                down_sent.append(down)
                down = shifted(after(down, row_home), -d % size, size)
            down_near.append(down)
        else:
            down_sent.append(down)
            down_parts.append((d, down))
        scale = gate_slots[:, d, :].reshape(-1, 1)

        def scaled(array):
            return (array.astype(f32) * scale).astype(bf16)

        new = (
            tn(scaled(code), pre_grad),
            tn(scaled(outer_codes[d]), activated),
            tn(scaled(back), got_rows[d].reshape(-1, width)),
            tn(scaled(outer_low), grad_rows[d]),
        )
        sums = new if sums is None else tuple(a + b for a, b in zip(sums, new))

    inner_up_sum, outer_down_sum, inner_down_sum, outer_up_sum = sums

    def widened(array):
        if copies == 1:
            return array
        whole = jnp.zeros((codes, copies, array.shape[1]), f32)
        whole = lax.dynamic_update_index_in_dim(whole, array, part, 1)
        return whole.reshape(codes, -1)

    wide = [widened(inner_up_sum), widened(outer_down_sum), inner_down_sum, outer_up_sum]
    ends = [sum(a.shape[1] for a in wide[: k + 1]) for k in range(3)]
    mlp_own = jnp.concatenate(wide, axis=1).astype(bf16)
    mlp_sums = lax.psum_scatter(mlp_own, "dp", scatter_dimension=0, tiled=True)
    mlp_sums = lax.all_gather(mlp_sums, ("seq", "dp"), axis=0, tiled=True)
    if copies == 1 and share % 128 == 0:
        inner_up_grad, outer_down_grad, inner_down_grad, outer_up_grad = unpack_sums(
            mlp_sums.reshape(size, adapters, rank, -1), share, width
        )
    else:
        mlp_sums = mlp_sums.astype(f32).reshape(size, codes, -1)
        inner_up_grad, outer_down_grad, inner_down_grad, outer_up_grad = jnp.split(mlp_sums, ends, axis=2)
        inner_up_grad = inner_up_grad.reshape(size, codes, copies, 2, share).transpose(1, 3, 2, 0, 4)
        inner_up_grad = inner_up_grad.reshape(adapters, rank, -1)
        outer_down_grad = outer_down_grad.reshape(size, codes, copies, share).transpose(1, 2, 0, 3)
        outer_down_grad = outer_down_grad.reshape(adapters, rank, -1)
        inner_down_grad = jnp.sum(inner_down_grad, 0).reshape(adapters, rank, width)
        outer_up_grad = jnp.sum(outer_up_grad, 0).reshape(adapters, rank, width)

    normed_mlp_grad = row_total + nt(mlp_logit_grad.astype(bf16), mlp_router_weight)
    middle_grad = norm_back(middle, middle_scale, mlp_gain, normed_mlp_grad)
    middle_grad = middle_grad + out_grad[0].astype(f32)
    middle_low = middle_grad.astype(bf16)
    branch_rows = send_full(tn(place_any, middle_low).astype(bf16), experts, copies)
    head_parts = nt(branch_rows.reshape(-1, width), output_full).astype(bf16)
    head_home = home_join(head_parts.reshape(holders, capacity, -1), experts, copies)
    head_home = after(head_home, mlp_own, *down_sent)
    gate_grad = jnp.sum(middle_grad[None] * branch, axis=2).T
    logit_grad = gate_back(gates, hits, gate_grad)
    gate_column = gates.T.reshape(-1, 1)
    output_low_grad = nt(middle_low, output_upper)
    output_low_back = output_low_grad.astype(bf16)
    output_low_scaled = (jnp.tile(output_low_grad, (2, 1)) * gate_column).astype(bf16)
    output_lower_grad = tn(output_low_scaled, attended)
    output_low_sum = (output_low.astype(f32) * gate_column).reshape(2, rows, rank).sum(0)
    output_upper_grad = tn(output_low_sum.astype(bf16), middle_low)

    def over_sequences(arrays):
        joined = [a.reshape(rank, size, -1) for a in arrays]
        ends = [sum(a.shape[2] for a in joined[: k + 1]) for k in range(len(arrays) - 1)]
        joined = jnp.concatenate(joined, axis=2).transpose(1, 0, 2)
        mine = picked(joined, spot)
        for d in range(1, size):
            theirs = picked(joined, (spot + d) % size).astype(bf16)
            mine = mine + shifted(theirs, -d % size, size).astype(f32)
        every = lax.all_gather(mine.astype(bf16), ("seq", "dp"), axis=0, tiled=False)
        every = every.reshape(size, holders, rank, -1).astype(f32)
        chosen = (adapter_all[:, None] == jnp.arange(adapters)[None, :]).astype(f32)
        made = []
        for part in jnp.split(every, ends, axis=3):
            part = part.transpose(1, 2, 0, 3)
            total = sum(
                part[k][None] * chosen[k][:, None, None, None] for k in range(holders)
            )
            made.append(total.reshape(adapters, rank, -1))
        return made

    key_grad, value_grad, query_slots, query_sum = attend_back(
        query_rot,
        pairs,
        bias,
        totals,
        head_home,
        place,
        gate_column,
        output_low_back,
        output_lower,
        cosine,
        sine,
        cosine_all,
        sine_all,
    )
    query_back = send_cut(query_slots, experts, copies)
    half = key_grad.shape[1]
    pair_low_grad = nt(key_grad, pair_up[:, :half]) + nt(value_grad, pair_up[:, half:])
    pair_low_grad = pair_low_grad.astype(bf16)
    normed_grad = None
    for d in range(size - 1, -1, -1):
        block = slice(d * rows, (d + 1) * rows)
        back = nt(key_grad[block], pair_weight[:, :half]) + nt(value_grad[block], pair_weight[:, half:])
        back = back + nn(pair_low_grad[block], pair_down)
        if d:
            back = shifted(back.astype(bf16), -d % size, size).astype(f32)
        normed_grad = back if normed_grad is None else normed_grad + back
    pair_upper_grad = jnp.concatenate([tn(pair_low, key_grad), tn(pair_low, value_grad)], axis=1)
    pair_lower_grad = sum(
        tn(pair_low_grad[d * rows : (d + 1) * rows], normed_parts[d]) for d in range(size)
    )
    query_low_grad = nt(query_sum, query_upper).astype(bf16)
    query_upper_grad = tn(query_low, query_sum)
    query_lower_grad = tn(query_low_grad, normed)
    late = over_sequences(
        [
            after(pair_lower_grad, mlp_sums),
            pair_upper_grad,
            query_lower_grad,
            query_upper_grad,
            output_lower_grad,
            output_upper_grad,
        ]
    )
    input_parts = nt(query_back.reshape(holders * capacity, -1), query_full).astype(bf16)
    input_home = home_add(input_parts.reshape(holders, capacity, width), experts, copies)
    normed_grad = normed_grad + nn(place_any, input_home) + nn(query_low_grad, query_lower)
    normed_grad = normed_grad + nt(logit_grad.astype(bf16), router_weight)
    input_grad = norm_back(inputs, input_scale, norm_gain, normed_grad) + middle_grad

    down_near = sum(after(down, input_home).astype(f32) for down in down_near)
    down_near = down_near.astype(bf16).reshape(holders, capacity, width)
    down_total = nn(combines[0], home_add(down_near, experts, copies))
    for d, down in down_parts:
        down = after(down, query_back).reshape(holders, capacity, width)
        home = home_add(down, experts, copies)
        down_total = down_total + shifted(nn(combines[d], home).astype(bf16), -d % size, size).astype(f32)
    result = (middle + down_total).astype(bf16)

    return (
        result[None],
        input_grad[None],
        flat_down(late[0]),
        late[1],
        flat_down(late[2]),
        late[3],
        flat_down(late[4]),
        late[5],
        flat_down(inner_down_grad),
        inner_up_grad,
        flat_down(outer_down_grad),
        outer_up_grad,
    )


def solution(mesh):
    split = P("dp", "seq", None)
    placed = (
        (split, P(), P("seq", None), P(), split, split, P(), P(), split, split)
        + (P(),) * 10
        + (split, split, P("dp"), P("dp"), split)
    )
    return jax.shard_map(
        body,
        mesh=mesh,
        in_specs=placed,
        out_specs=(split, split) + (P(),) * 10,
        check_vma=False,
    )
```

```python
import functools
import math

import jax
import jax.numpy as jnp
import numpy as np
from jax import lax
from jax.experimental import pallas as pl
from jax.experimental.pallas import tpu as pltpu
from jax.sharding import PartitionSpec as P

KV_HEADS = 16
HD = 128

norm_eps = 1e-05
rope_base = 10000.0
masked_score = -1e30
vmem_bytes = 48 * 2**20

bf16 = jnp.bfloat16
f32 = jnp.float32


def product(left, right, left_dim, right_dim):
    return lax.dot_general(
        left, right, (((left_dim,), (right_dim,)), ((), ())), preferred_element_type=f32
    )


def nn(left, right):
    return product(left, right, 1, 0)


def nt(left, right):
    return product(left, right, 1, 1)


def tn(left, right):
    return product(left, right, 0, 0)


def pair_kernel(count, key_blocks, *refs):
    normed_refs = refs[:count]
    w_ref, down_ref, up_ref, cos_ref, sin_ref, out_ref, low_ref = refs[count:]
    rows = normed_refs[0].shape[0]
    step = pl.program_id(0)

    @pl.when(step == 0)
    def _():
        for k in range(count):
            low_ref[pl.ds(k * rows, rows), :] = nt(normed_refs[k][...], down_ref[...]).astype(bf16)

    for k in range(count):
        part = pl.ds(k * rows, rows)
        made = nn(normed_refs[k][...], w_ref[...]) + nn(low_ref[part, :], up_ref[...])

        @pl.when(step < key_blocks)
        def _():
            for start in range(0, made.shape[1], HD):
                head = made[:, start : start + HD]
                turned = head * cos_ref[part, :] + pltpu.roll(head, HD // 2, 1) * sin_ref[part, :]
                out_ref[part, start : start + HD] = turned.astype(bf16)

        @pl.when(step >= key_blocks)
        def _():
            out_ref[part, :] = made.astype(bf16)


def project_pairs(normed_parts, weight, down, upper, cosine, sine):
    count = len(normed_parts)
    rows, width = normed_parts[0].shape
    columns = weight.shape[1]
    block = 512
    whole = lambda array: pl.BlockSpec(array.shape, lambda i: (0, 0))
    return pl.pallas_call(
        functools.partial(pair_kernel, count, columns // 2 // block),
        grid=(columns // block,),
        in_specs=[whole(n) for n in normed_parts]
        + [
            pl.BlockSpec((width, block), lambda i: (0, i)),
            whole(down),
            pl.BlockSpec((upper.shape[0], block), lambda i: (0, i)),
            whole(cosine),
            whole(sine),
        ],
        out_specs=[
            pl.BlockSpec((count * rows, block), lambda i: (0, i)),
            pl.BlockSpec((count * rows, down.shape[0]), lambda i: (0, 0)),
        ],
        out_shape=[
            jax.ShapeDtypeStruct((count * rows, columns), bf16),
            jax.ShapeDtypeStruct((count * rows, down.shape[0]), bf16),
        ],
        compiler_params=pltpu.CompilerParams(vmem_limit_bytes=vmem_bytes),
        cost_estimate=pl.CostEstimate(
            flops=2 * count * rows * width * columns,
            bytes_accessed=2 * width * columns,
            transcendentals=0,
        ),
        name="pairs",
    )(*normed_parts, weight, down, upper, cosine, sine)


def attend_kernel(
    scale,
    home_ref,
    place_ref,
    low_ref,
    up_ref,
    cos_ref,
    sin_ref,
    key_ref,
    value_ref,
    bias_ref,
    attended_ref,
    slots_ref,
    query_ref,
    total_ref,
):
    rows = cos_ref.shape[0]
    base = nn(place_ref[...], home_ref[...])
    extra = nn(low_ref[...], up_ref[...])
    keys, values = key_ref[...], value_ref[...]
    for route in range(2):
        part = pl.ds(route * rows, rows)
        query = base[route * rows : (route + 1) * rows] + extra
        query = query * cos_ref[...] + pltpu.roll(query, HD // 2, 1) * sin_ref[...]
        query = query.astype(bf16)
        query_ref[part, :] = query
        scores = nt(query, keys) * scale + bias_ref[...]
        highest = jnp.max(scores, axis=1, keepdims=True)
        weights = jnp.exp(scores - highest)
        total = jnp.sum(weights, axis=1, keepdims=True)
        attended = nn(weights.astype(bf16), values) / total
        attended_ref[part, :] = attended.astype(bf16)
        total_ref[0, part, :] = highest + jnp.log(total)
    slots_ref[...] = tn(place_ref[...], attended_ref[...]).astype(bf16)


def attend(home, place, low, upper, cosine, sine, pairs, bias):
    rows2, slots = place.shape
    rows, length = bias.shape
    heads = home.shape[1] // HD
    kv_heads = pairs.shape[1] // (2 * HD)
    whole = lambda array: pl.BlockSpec(array.shape, lambda h: (0, 0))
    return pl.pallas_call(
        functools.partial(attend_kernel, 1.0 / math.sqrt(HD)),
        grid=(heads,),
        in_specs=[
            pl.BlockSpec((slots, HD), lambda h: (0, h)),
            whole(place),
            whole(low),
            pl.BlockSpec((upper.shape[0], HD), lambda h: (0, h)),
            whole(cosine),
            whole(sine),
            pl.BlockSpec((length, HD), lambda h: (0, h)),
            pl.BlockSpec((length, HD), lambda h: (0, kv_heads + h)),
            whole(bias),
        ],
        out_specs=[
            pl.BlockSpec((rows2, HD), lambda h: (0, h)),
            pl.BlockSpec((slots, HD), lambda h: (0, h)),
            pl.BlockSpec((rows2, HD), lambda h: (0, h)),
            pl.BlockSpec((1, rows2, 1), lambda h: (h, 0, 0)),
        ],
        out_shape=[
            jax.ShapeDtypeStruct((rows2, heads * HD), bf16),
            jax.ShapeDtypeStruct((slots, heads * HD), bf16),
            jax.ShapeDtypeStruct((rows2, heads * HD), bf16),
            jax.ShapeDtypeStruct((heads, rows2, 1), f32),
        ],
        compiler_params=pltpu.CompilerParams(vmem_limit_bytes=vmem_bytes),
        cost_estimate=pl.CostEstimate(
            flops=4 * heads * rows2 * length * HD,
            bytes_accessed=4 * length * heads * HD,
            transcendentals=heads * rows2 * length,
        ),
        name="attend",
    )(home, place, low, upper, cosine, sine, pairs, pairs, bias)


def attend_back_kernel(
    scale,
    query_ref,
    key_ref,
    value_ref,
    bias_ref,
    total_ref,
    home_ref,
    place_ref,
    gate_ref,
    low_ref,
    down_ref,
    cos_ref,
    sin_ref,
    cos_all_ref,
    sin_all_ref,
    key_grad_ref,
    value_grad_ref,
    slots_ref,
    sum_ref,
    turned_ref,
):
    rows = cos_ref.shape[0]
    base = nn(place_ref[...], home_ref[...])
    extra = nn(low_ref[...], down_ref[...])
    keys, values = key_ref[...], value_ref[...]
    key_grad = value_grad = None
    for route in range(2):
        part = pl.ds(route * rows, rows)
        query = query_ref[part, :]
        grad = (base[route * rows : (route + 1) * rows] + extra) * gate_ref[part, :]
        grad = grad.astype(bf16)
        scores = nt(query, keys) * scale + bias_ref[...]
        weights = jnp.exp(scores - total_ref[0, part, :])
        weight_grad = nt(grad, values)
        mean_grad = jnp.sum(weights * weight_grad, axis=1, keepdims=True)
        score_grad = (weights * (weight_grad - mean_grad)).astype(bf16)
        query_grad = nn(score_grad, keys) * scale
        query_grad = query_grad * cos_ref[...] - pltpu.roll(query_grad, HD // 2, 1) * sin_ref[...]
        turned_ref[part, :] = query_grad.astype(bf16)
        key_part = tn(score_grad, query)
        value_part = tn(weights.astype(bf16), grad)
        key_grad = key_part if route == 0 else key_grad + key_part
        value_grad = value_part if route == 0 else value_grad + value_part
    key_grad = key_grad * scale
    key_grad = key_grad * cos_all_ref[...] - pltpu.roll(key_grad, HD // 2, 1) * sin_all_ref[...]
    key_grad_ref[...] = key_grad.astype(bf16)
    value_grad_ref[...] = value_grad.astype(bf16)
    slots_ref[...] = tn(place_ref[...], turned_ref[...]).astype(bf16)
    first = turned_ref[pl.ds(0, rows), :].astype(f32)
    sum_ref[...] = (first + turned_ref[pl.ds(rows, rows), :].astype(f32)).astype(bf16)


def attend_back(query, pairs, bias, totals, home, place, gates, low, down, cosine, sine, cosine_all, sine_all):
    rows2, slots = place.shape
    rows, length = bias.shape
    heads = home.shape[1] // HD
    kv_heads = pairs.shape[1] // (2 * HD)
    whole = lambda array: pl.BlockSpec(array.shape, lambda h: (0, 0))
    return pl.pallas_call(
        functools.partial(attend_back_kernel, 1.0 / math.sqrt(HD)),
        grid=(heads,),
        in_specs=[
            pl.BlockSpec((rows2, HD), lambda h: (0, h)),
            pl.BlockSpec((length, HD), lambda h: (0, h)),
            pl.BlockSpec((length, HD), lambda h: (0, kv_heads + h)),
            whole(bias),
            pl.BlockSpec((1, rows2, 1), lambda h: (h, 0, 0)),
            pl.BlockSpec((slots, HD), lambda h: (0, h)),
            whole(place),
            whole(gates),
            whole(low),
            pl.BlockSpec((down.shape[0], HD), lambda h: (0, h)),
            whole(cosine),
            whole(sine),
            whole(cosine_all),
            whole(sine_all),
        ],
        out_specs=[
            pl.BlockSpec((length, HD), lambda h: (0, h)),
            pl.BlockSpec((length, HD), lambda h: (0, h)),
            pl.BlockSpec((slots, HD), lambda h: (0, h)),
            pl.BlockSpec((rows, HD), lambda h: (0, h)),
        ],
        out_shape=[
            jax.ShapeDtypeStruct((length, heads * HD), bf16),
            jax.ShapeDtypeStruct((length, heads * HD), bf16),
            jax.ShapeDtypeStruct((slots, heads * HD), bf16),
            jax.ShapeDtypeStruct((rows, heads * HD), bf16),
        ],
        scratch_shapes=[pltpu.VMEM((rows2, HD), bf16)],
        compiler_params=pltpu.CompilerParams(vmem_limit_bytes=vmem_bytes),
        cost_estimate=pl.CostEstimate(
            flops=10 * heads * rows2 * length * HD,
            bytes_accessed=8 * length * heads * HD,
            transcendentals=heads * rows2 * length,
        ),
        name="attend_back",
    )(query, pairs, pairs, bias, totals, home, place, gates, low, down, cosine, sine, cosine_all, sine_all)


def exchange(buffer):
    return lax.all_to_all(buffer, "dp", split_axis=0, concat_axis=0, tiled=True)


def shifted(array, shift, size):
    if shift == 0:
        return array
    return lax.ppermute(array, "seq", [(k, (k - shift) % size) for k in range(size)])


def send_full(slots, experts, copies):
    buffer = slots.reshape(experts, slots.shape[0] // experts, slots.shape[1])
    if copies > 1:
        buffer = jnp.repeat(buffer, copies, axis=0)
    return exchange(buffer)


def send_cut(slots, experts, copies):
    buffer = slots.reshape(experts, slots.shape[0] // experts, slots.shape[1])
    if copies > 1:
        _, rows, columns = buffer.shape
        buffer = buffer.reshape(experts, rows, copies, columns // copies).transpose(0, 2, 1, 3)
        buffer = buffer.reshape(experts * copies, rows, columns // copies)
    return exchange(buffer)


def home_join(parts, experts, copies):
    home = exchange(parts)
    _, rows, columns = home.shape
    if copies > 1:
        home = home.reshape(experts, copies, rows, columns).transpose(0, 2, 1, 3)
    return home.reshape(experts * rows, copies * columns)


def home_add(parts, experts, copies):
    home = exchange(parts)
    _, rows, columns = home.shape
    if copies > 1:
        home = home.reshape(experts, copies, rows, columns).astype(f32)
        home = jnp.sum(home, axis=1).astype(parts.dtype)
    return home.reshape(experts * rows, columns)


def slot_layout(route_ids, experts, capacity):
    flat = route_ids.T.reshape(-1)
    count = flat.shape[0]
    hits = flat[:, None] == jnp.arange(experts)[None, :]
    earlier = jnp.arange(count)[:, None] > jnp.arange(count)[None, :]
    before = nn(earlier.astype(bf16), hits.astype(bf16))
    rank = jnp.sum(jnp.where(hits, before, 0.0), axis=1).astype(jnp.int32)
    slot = flat * capacity + rank
    return (slot[:, None] == jnp.arange(experts * capacity)[None, :]).astype(bf16)


def either(place):
    rows = place.shape[0] // 2
    return place[:rows] + place[rows:]


def norm_back(values, scale, gain, grad):
    weighted = grad * gain
    mean = jnp.mean(weighted * values, axis=-1, keepdims=True)
    return weighted * scale - values * (scale * scale * scale * mean)


def norm_scale(values):
    return lax.rsqrt(jnp.mean(values * values, axis=-1, keepdims=True) + norm_eps)


def gate_pair(logits, route_ids):
    hits = (route_ids[:, :, None] == jnp.arange(logits.shape[1])).astype(f32)
    chosen = jnp.sum(hits * logits[:, None, :], axis=2)
    weights = jnp.exp(chosen - jnp.max(chosen, axis=1, keepdims=True))
    return weights / jnp.sum(weights, axis=1, keepdims=True), hits


def gate_back(gates, hits, grad):
    mean = jnp.sum(gates * grad, axis=1, keepdims=True)
    return jnp.sum((gates * (grad - mean))[:, :, None] * hits, axis=1)


def rope_full(length, start):
    half = HD // 2
    frequency = rope_base ** (-np.arange(half) / half)
    angles = np.arange(length)[:, None] * frequency[None, :]
    cosine, sine = np.cos(angles), np.sin(angles)
    tables = np.concatenate([cosine, cosine, -sine, sine], 1).astype(np.float32)
    tables = jnp.asarray(np.concatenate([tables, tables], 0))
    tables = lax.dynamic_slice_in_dim(tables, start, length, 0)
    return tables[:, :HD], tables[:, HD:]


def after(array, *earlier):
    return lax.optimization_barrier((array,) + earlier)[0]


def cut_kernel(target_ref, in_ref, out_ref):
    out_ref[...] = in_ref[...]


def cut_share(weight, target, size):
    rows, columns = weight.shape
    share = columns // 2 // size
    if share % 128:
        cut = weight.reshape(rows, 2, size, share)
        return lax.dynamic_index_in_dim(cut, target, 2, keepdims=False).reshape(rows, 2 * share)
    return pl.pallas_call(
        cut_kernel,
        grid_spec=pltpu.PrefetchScalarGridSpec(
            num_scalar_prefetch=1,
            grid=(2,),
            in_specs=[pl.BlockSpec((rows, share), lambda i, t: (0, i * size + t[0]))],
            out_specs=pl.BlockSpec((rows, share), lambda i, t: (0, i)),
        ),
        out_shape=jax.ShapeDtypeStruct((rows, 2 * share), bf16),
        compiler_params=pltpu.CompilerParams(vmem_limit_bytes=vmem_bytes),
        name="cut",
    )(target.reshape(1).astype(jnp.int32), weight)


def unpack_kernel(size, share, in_ref, inner_up_ref, outer_down_ref, inner_down_ref, outer_up_ref):
    spot = pl.program_id(1)
    got = in_ref[0, 0].astype(f32)
    hidden = size * share
    width = inner_down_ref.shape[2]
    start = pl.multiple_of(spot * share, 128)
    inner_up_ref[0, :, pl.ds(start, share)] = got[:, :share]
    inner_up_ref[0, :, pl.ds(pl.multiple_of(hidden + start, 128), share)] = got[:, share : 2 * share]
    outer_down_ref[0, :, pl.ds(start, share)] = got[:, 2 * share : 3 * share]
    inner_down = got[:, 3 * share : 3 * share + width]
    outer_up = got[:, 3 * share + width :]

    @pl.when(spot == 0)
    def _():
        inner_down_ref[0] = inner_down
        outer_up_ref[0] = outer_up

    @pl.when(spot > 0)
    def _():
        inner_down_ref[0] += inner_down
        outer_up_ref[0] += outer_up


def unpack_sums(sums, share, width):
    size, adapters, rank, columns = sums.shape
    hidden = size * share
    shapes = [2 * hidden, hidden, width, width]
    return pl.pallas_call(
        functools.partial(unpack_kernel, size, share),
        grid=(adapters, size),
        in_specs=[pl.BlockSpec((1, 1, rank, columns), lambda a, k: (k, a, 0, 0))],
        out_specs=[pl.BlockSpec((1, rank, n), lambda a, k: (a, 0, 0)) for n in shapes],
        out_shape=[jax.ShapeDtypeStruct((adapters, rank, n), f32) for n in shapes],
        compiler_params=pltpu.CompilerParams(vmem_limit_bytes=vmem_bytes),
        cost_estimate=pl.CostEstimate(
            flops=0, bytes_accessed=12 * adapters * rank * (3 * hidden + 2 * width), transcendentals=0
        ),
        name="unpack",
    )(sums)


def gather_adapters_kernel(adapters, ids_ref, in_ref, *out_refs):
    holders = in_ref.shape[1]
    start = 0
    for out_ref in out_refs:
        columns = out_ref.shape[2]
        parts = [in_ref[0, k, :, start : start + columns].astype(f32) for k in range(holders)]
        for a in range(adapters):
            total = None
            for k in range(holders):
                one = jnp.where(ids_ref[k] == a, parts[k], 0.0)
                total = one if total is None else total + one
            out_ref[a] = total
        start += columns


def gather_adapters(every, adapter_all, adapters, widths):
    size, holders, rank, columns = every.shape
    return pl.pallas_call(
        functools.partial(gather_adapters_kernel, adapters),
        grid_spec=pltpu.PrefetchScalarGridSpec(
            num_scalar_prefetch=1,
            grid=(size,),
            in_specs=[pl.BlockSpec((1, holders, rank, columns), lambda k, s: (k, 0, 0, 0))],
            out_specs=[
                pl.BlockSpec((adapters, rank, n // size), lambda k, s: (0, 0, k)) for n in widths
            ],
        ),
        out_shape=[jax.ShapeDtypeStruct((adapters, rank, n), f32) for n in widths],
        compiler_params=pltpu.CompilerParams(vmem_limit_bytes=vmem_bytes),
        name="gather_adapters",
    )(adapter_all, every)


def silu_parts(gate_part, up_part, hidden_grad):
    sigmoid = 1.0 / (1.0 + jnp.exp(-gate_part))
    active = gate_part * sigmoid
    activated = (active * up_part).astype(bf16)
    gate_grad = hidden_grad * up_part * sigmoid * (1.0 + gate_part * (1.0 - sigmoid))
    return activated, gate_grad.astype(bf16), (hidden_grad * active).astype(bf16)


def halves(value):
    high = value.astype(bf16)
    return high, (value - high.astype(f32)).astype(bf16)


def expert_kernel(size, share, spot_ref, x_ref, hidden_ref, mask_ref, up_ref, down_ref, *refs):
    w_refs = refs[:size]
    row_ref, active_ref, pre_ref, code_ref, back_ref = refs[size:]
    depth = w_refs[0].shape[0]
    width = size * depth
    columns = [pl.ds(pl.multiple_of((spot_ref[0] + k) % size * depth, 128), depth) for k in range(size)]
    code = nt(x_ref[...], down_ref[...]).astype(bf16) * mask_ref[...]
    code_ref[...] = code
    sums = None
    for start in range(0, share, 256):
        end = min(start + 256, share)

        def hidden(first, last):
            made = nn(code, up_ref[:, first:last])
            for k in range(size):
                made = made + nn(x_ref[:, columns[k]], w_refs[k][:, first:last])
            return made

        gate_part, up_part = hidden(start, end), hidden(share + start, share + end)
        hidden_grad = hidden_ref[:, start:end].astype(f32)
        activated, gate_grad, up_grad = silu_parts(gate_part, up_part, hidden_grad)
        active_ref[:, start:end] = activated
        pre_ref[:, start:end] = gate_grad
        pre_ref[:, share + start : share + end] = up_grad
        part = jnp.sum(activated.astype(f32) * hidden_grad, axis=1, keepdims=True)
        sums = part if sums is None else sums + part
    back = nt(pre_ref[...], up_ref[...]).astype(bf16) * mask_ref[...]
    back_ref[...] = back
    for k in range(size):
        base = (spot_ref[0] + k) % size * depth
        for start in range(0, depth, 256):
            end = min(start + 256, depth)
            here = pl.ds(pl.multiple_of(base + start, 128), end - start)
            made = nt(pre_ref[...], w_refs[k][start:end, :]) + nn(back, down_ref[:, here])
            row_ref[:, here] = made.astype(bf16)
    high, low = halves(sums)
    lane = lax.broadcasted_iota(jnp.int32, (sums.shape[0], 128), 1)
    packed = jnp.where(lane == 0, high.astype(f32), jnp.where(lane == 1, low.astype(f32), 0.0))
    row_ref[:, width:] = packed.astype(bf16)


def expert_block(got, hidden_grad, mask, inner_up, inner_down, inner_parts, spot):
    size = len(inner_parts)
    rows, width = got.shape
    share = hidden_grad.shape[1]
    codes = mask.shape[1]
    if share % 128 or width // size % 256:
        code = nt(got, inner_down).astype(bf16) * mask
        twice = jnp.concatenate(inner_parts + inner_parts, axis=0)
        first = (size - spot) % size * (width // size)
        inner_full = lax.dynamic_slice_in_dim(twice, first, width, 0)
        pre = nn(got, inner_full) + nn(code, inner_up)
        hidden_float = hidden_grad.astype(f32)
        activated, gate_grad, up_grad = silu_parts(pre[:, :share], pre[:, share:], hidden_float)
        pre_grad = jnp.concatenate([gate_grad, up_grad], axis=1)
        back = nt(pre_grad, inner_up).astype(bf16) * mask
        row_grad = (nt(pre_grad, inner_full) + nn(back, inner_down)).astype(bf16)
        sums = jnp.stack(halves(jnp.sum(activated.astype(f32) * hidden_float, axis=1)), axis=1)
        row_grad = jnp.concatenate([row_grad, jnp.pad(sums, ((0, 0), (0, 126)))], axis=1)
        return row_grad, activated, pre_grad, code, back
    block = rows // 2
    ahead = lambda n: pl.BlockSpec((block, n), lambda i, s: (i, 0))
    whole = lambda array: pl.BlockSpec(array.shape, lambda i, s: (0, 0), pipeline_mode=pl.Buffered(1))
    shapes = [width + 128, share, 2 * share, codes, codes]
    return pl.pallas_call(
        functools.partial(expert_kernel, size, share),
        grid_spec=pltpu.PrefetchScalarGridSpec(
            num_scalar_prefetch=1,
            grid=(2,),
            in_specs=[ahead(width), ahead(share), ahead(codes), whole(inner_up), whole(inner_down)]
            + [whole(part) for part in inner_parts],
            out_specs=[ahead(n) for n in shapes],
        ),
        out_shape=[jax.ShapeDtypeStruct((rows, n), bf16) for n in shapes],
        compiler_params=pltpu.CompilerParams(vmem_limit_bytes=vmem_bytes),
        cost_estimate=pl.CostEstimate(
            flops=8 * rows * width * share,
            bytes_accessed=4 * width * share + 10 * rows * width,
            transcendentals=rows * share,
        ),
        name="experts",
    )(spot.reshape(1).astype(jnp.int32), got, hidden_grad, mask, inner_up, inner_down, *inner_parts)


def picked(lookup, index):
    return lax.dynamic_index_in_dim(lookup, index, 0, keepdims=False)


def body(
    tokens,
    norm_gain,
    key_value_weight,
    router_weight,
    query_weight,
    output_weight,
    mlp_gain,
    mlp_router_weight,
    mlp_in_weight,
    mlp_out_weight,
    key_value_down,
    key_value_up,
    query_down,
    query_up,
    output_down,
    output_up,
    mlp_in_down,
    mlp_in_up,
    mlp_out_down,
    mlp_out_up,
    routes,
    mlp_routes,
    adapter_index,
    prefix_length,
    out_grad,
):
    seqs, rows, width = tokens.shape
    assert seqs == 1
    size, spot = lax.axis_size("seq"), lax.axis_index("seq")
    holders, holder = lax.axis_size("dp"), lax.axis_index("dp")
    experts = router_weight.shape[1]
    copies = holders // experts
    part = holder % copies
    capacity = 3 * rows // 8
    length = rows * size
    adapters, _, rank = key_value_down.shape
    codes = adapters * rank
    hidden = mlp_in_weight.shape[2] // 2
    share = hidden // size

    def flat_down(lookup):
        return lookup.transpose(0, 2, 1)

    adapter = adapter_index[0]
    adapter_all = exchange(jnp.broadcast_to(adapter_index[None], (holders, 128)))[:, 0]
    inputs = tokens[0].astype(f32)
    input_scale = norm_scale(inputs)
    normed = (inputs * input_scale * norm_gain).astype(bf16)

    gates, hits = gate_pair(nn(normed, router_weight), routes[0])
    place = slot_layout(routes[0], experts, capacity)
    place_any = either(place)
    query_rows = send_full(tn(place_any, normed).astype(bf16), experts, copies)
    query_full = lax.all_gather(query_weight[0], "seq", axis=0, tiled=True)
    normed_parts = [shifted(normed, d, size) for d in range(size)]
    piece = key_value_weight.shape[0] // holders
    pair_piece = lax.dynamic_slice_in_dim(key_value_weight, holder * piece, piece, 0)
    place_mlp = slot_layout(mlp_routes[0], experts, capacity)
    grad_own = send_full(tn(either(place_mlp), out_grad[0]).astype(bf16), experts, copies)
    pair_piece = after(
        pair_piece, query_full, query_rows, grad_own, adapter_all, *normed_parts[1:]
    )
    pair_weight = lax.all_gather(pair_piece, ("seq", "dp"), axis=0, tiled=True)
    lanes = jnp.pad(mlp_routes[0].astype(bf16), ((0, 0), (0, 126)))
    packet = jnp.concatenate([out_grad[0], lanes], axis=1)
    packet_late = after(packet, query_full)
    early = [packet] + [shifted(packet_late, d, size) for d in range(1, size)]
    output_own = after(output_weight[0], pair_weight, *early[1:])
    output_full = lax.all_gather(output_own, "seq", axis=0, tiled=True)
    grad_parts = [out_grad[0]] + [p[:, :width] for p in early[1:]]
    routes_there = [p[:, width : width + 2].astype(jnp.int32) for p in early]
    outer_full = mlp_out_weight[0]

    pair_down, pair_up = picked(flat_down(key_value_down), adapter), picked(key_value_up, adapter)
    query_lower, query_upper = picked(flat_down(query_down), adapter), picked(query_up, adapter)
    output_lower, output_upper = picked(flat_down(output_down), adapter), picked(output_up, adapter)
    query_low = nt(normed, query_lower).astype(bf16)
    positions = spot * rows + jnp.arange(rows)
    key_pos = (spot * rows + jnp.arange(length)) % length
    cosine_all, sine_all = rope_full(length, spot * rows)
    cosine, sine = cosine_all[:rows], sine_all[:rows]
    allowed = (key_pos[None, :] <= positions[:, None]) | (key_pos[None, :] < prefix_length[0])
    bias = jnp.where(allowed, 0.0, masked_score).astype(f32)

    mask = (jnp.arange(codes)[None, None, :] // rank == adapter_all[:, None, None]).astype(bf16)
    mask = jnp.broadcast_to(mask, (holders, capacity, codes)).reshape(-1, codes)
    inner_down = flat_down(mlp_in_down).reshape(codes, width)
    outer_up = mlp_out_up.reshape(codes, width)
    inner_up = mlp_in_up.reshape(codes, 2, copies, size, share)
    inner_up = lax.dynamic_index_in_dim(inner_up, part, 2, keepdims=False)
    inner_up = lax.dynamic_index_in_dim(inner_up, spot, 2, keepdims=False).reshape(codes, 2 * share)
    outer_down = flat_down(mlp_out_down).reshape(codes, copies, size, share)
    outer_down = lax.dynamic_index_in_dim(outer_down, part, 1, keepdims=False)
    outer_down = lax.dynamic_index_in_dim(outer_down, spot, 1, keepdims=False)

    places = [place_mlp] + [slot_layout(r, experts, capacity) for r in routes_there[1:]]
    grad_rows, hidden_grads, outer_codes = [], [], []
    for d in range(size):
        if d:
            got = send_full(tn(either(places[d]), grad_parts[d]).astype(bf16), experts, copies)
        else:
            got = grad_own
        got = got.reshape(-1, width)
        code = nt(got, outer_up).astype(bf16) * mask
        grad_rows.append(got)
        outer_codes.append(code)
        hidden_grads.append((nt(got, outer_full) + nn(code, outer_down)).astype(bf16))

    query_rows = after(query_rows, *normed_parts[1:])
    query_parts = nn(query_rows.reshape(-1, width), query_full).astype(bf16)
    query_home = home_join(query_parts.reshape(holders, capacity, -1), experts, copies)
    pairs, pair_low = project_pairs(
        normed_parts, pair_weight, pair_down, pair_up, cosine_all, sine_all
    )
    far = size // 2
    inner_sent = [cut_share(mlp_in_weight[0], (spot - d) % size, size) for d in range(size)]
    inner_parts = list(inner_sent)
    inner_parts[far] = shifted(after(inner_sent[far], *early[1:]), far, size)
    query_home = after(query_home, *early[1:], *grad_rows[:2])
    attended, output_slots, query_rot, totals = attend(
        query_home, place, query_low, query_upper, cosine, sine, pairs, bias
    )

    output_rows = send_cut(output_slots, experts, copies)
    output_rows = after(output_rows, inner_parts[far], *grad_rows[2:])
    output_parts = nn(output_rows.reshape(holders * capacity, -1), output_full).astype(bf16)
    distances = [d for d in range(1, size) if d != far]
    for d in distances:
        inner_parts[d] = shifted(after(inner_sent[d], output_full), d, size)
    output_home = home_add(output_parts.reshape(holders, capacity, width), experts, copies)
    output_low = nt(attended, output_lower).astype(bf16)
    branch = nn(place, output_home) + nn(output_low, output_upper)
    branch = branch.reshape(2, rows, width)
    middle = inputs + gates[:, :1] * branch[0] + gates[:, 1:] * branch[1]
    middle_scale = norm_scale(middle)
    normed_mlp = (middle * middle_scale * mlp_gain).astype(bf16)
    mlp_gates, mlp_hits = gate_pair(nn(normed_mlp, mlp_router_weight), mlp_routes[0])

    lanes = jnp.pad(jnp.concatenate(halves(mlp_gates), axis=1), ((0, 0), (0, 124)))
    packet = jnp.concatenate([normed_mlp, lanes], axis=1)
    packet = after(packet, *(inner_parts[d] for d in distances[:-1]))
    packets = [shifted(packet, d, size) for d in range(size)]
    gates_there = [
        (p[:, width : width + 2].astype(f32) + p[:, width + 2 : width + 4].astype(f32)).T.reshape(-1, 1)
        for p in packets
    ]
    combines = [either((places[d].astype(f32) * gates_there[d]).astype(bf16)) for d in range(size)]
    order = list(range(1, size)) + [0]
    got_rows = {}
    for d in order[-1:] + order[:-1]:
        rows_there = packets[d][:, :width]
        if d == order[0]:
            rows_there = after(rows_there, got_rows[0], *(inner_parts[k] for k in distances[-1:]))
        elif d:
            rows_there = after(rows_there, got_rows[d - 1])
        sent = tn(either(places[d]), rows_there).astype(bf16)
        got_rows[d] = send_full(sent, experts, copies)
    gate_slots = jnp.stack(
        [jnp.sum(places[d].astype(f32) * gates_there[d], axis=0) for d in range(size)]
    )
    gate_slots = gate_slots.reshape(size, experts, capacity).transpose(1, 0, 2)
    gate_slots = exchange(jnp.repeat(gate_slots, copies, axis=0))

    kept, row_total, backs = {}, None, []
    for turn, d in enumerate(order):
        if turn:
            got_rows[d] = after(got_rows[d], kept[order[turn - 1]][0])
        kept[d] = expert_block(
            got_rows[d].reshape(-1, width),
            hidden_grads[d],
            mask,
            inner_up,
            inner_down,
            inner_parts,
            spot,
        )
        row_grad = after(kept[d][0], backs[0]) if turn > 2 else kept[d][0]
        row_home = home_add(row_grad.reshape(holders, capacity, -1), experts, copies)
        row_sum = nn(combines[d], row_home[:, :width])
        gate_sum = nn(places[d], row_home[:, width:])
        lanes = gate_sum[:rows] + jnp.roll(gate_sum[rows:], 2, axis=1)
        row_back = jnp.concatenate([row_sum, lanes], axis=1)
        if d:
            row_back = shifted(row_back.astype(bf16), -d % size, size)
        backs.append(row_back)
        row_back = row_back.astype(f32)
        row_total = row_back if row_total is None else row_total + row_back
    gate_sum = row_total[:, width : width + 4]
    row_total = row_total[:, :width]
    mlp_gate_grad = gate_sum.reshape(rows, 2, 2).sum(2)
    mlp_logit_grad = gate_back(mlp_gates, mlp_hits, mlp_gate_grad)

    down_near, down_parts, down_sent, sums = [], [], [], None
    for d in order:
        _, activated, pre_grad, code, back = kept[d]
        outer_low = nt(activated, outer_down).astype(bf16) * mask
        down = (nn(activated, outer_full) + nn(outer_low, outer_up)).astype(bf16)
        if d in (0, 1, size - 1):
            if d:
                down_sent.append(down)
                down = shifted(after(down, row_home), -d % size, size)
            down_near.append(down)
        else:
            down_sent.append(down)
            down_parts.append((d, down))
        scale = gate_slots[:, d, :].reshape(-1, 1)

        def scaled(array):
            return (array.astype(f32) * scale).astype(bf16)

        new = (
            tn(scaled(code), pre_grad),
            tn(scaled(outer_codes[d]), activated),
            tn(scaled(back), got_rows[d].reshape(-1, width)),
            tn(scaled(outer_low), grad_rows[d]),
        )
        sums = new if sums is None else tuple(a + b for a, b in zip(sums, new))

    inner_up_sum, outer_down_sum, inner_down_sum, outer_up_sum = sums

    def widened(array):
        if copies == 1:
            return array
        whole = jnp.zeros((codes, copies, array.shape[1]), f32)
        whole = lax.dynamic_update_index_in_dim(whole, array, part, 1)
        return whole.reshape(codes, -1)

    wide = [widened(inner_up_sum), widened(outer_down_sum), inner_down_sum, outer_up_sum]
    ends = [sum(a.shape[1] for a in wide[: k + 1]) for k in range(3)]
    mlp_own = jnp.concatenate(wide, axis=1).astype(bf16)
    mlp_sums = lax.psum_scatter(mlp_own, "dp", scatter_dimension=0, tiled=True)
    mlp_sums = lax.all_gather(mlp_sums, ("seq", "dp"), axis=0, tiled=True)
    if copies == 1 and share % 128 == 0:
        inner_up_grad, outer_down_grad, inner_down_grad, outer_up_grad = unpack_sums(
            mlp_sums.reshape(size, adapters, rank, -1), share, width
        )
    else:
        mlp_sums = mlp_sums.astype(f32).reshape(size, codes, -1)
        inner_up_grad, outer_down_grad, inner_down_grad, outer_up_grad = jnp.split(mlp_sums, ends, axis=2)
        inner_up_grad = inner_up_grad.reshape(size, codes, copies, 2, share).transpose(1, 3, 2, 0, 4)
        inner_up_grad = inner_up_grad.reshape(adapters, rank, -1)
        outer_down_grad = outer_down_grad.reshape(size, codes, copies, share).transpose(1, 2, 0, 3)
        outer_down_grad = outer_down_grad.reshape(adapters, rank, -1)
        inner_down_grad = jnp.sum(inner_down_grad, 0).reshape(adapters, rank, width)
        outer_up_grad = jnp.sum(outer_up_grad, 0).reshape(adapters, rank, width)

    normed_mlp_grad = row_total + nt(mlp_logit_grad.astype(bf16), mlp_router_weight)
    middle_grad = norm_back(middle, middle_scale, mlp_gain, normed_mlp_grad)
    middle_grad = middle_grad + out_grad[0].astype(f32)
    middle_low = middle_grad.astype(bf16)
    branch_rows = send_full(tn(place_any, middle_low).astype(bf16), experts, copies)
    head_parts = nt(branch_rows.reshape(-1, width), output_full).astype(bf16)
    head_home = home_join(head_parts.reshape(holders, capacity, -1), experts, copies)
    head_home = after(head_home, mlp_own, *down_sent)
    gate_grad = jnp.sum(middle_grad[None] * branch, axis=2).T
    logit_grad = gate_back(gates, hits, gate_grad)
    gate_column = gates.T.reshape(-1, 1)
    output_low_grad = nt(middle_low, output_upper)
    output_low_back = output_low_grad.astype(bf16)
    output_low_scaled = (jnp.tile(output_low_grad, (2, 1)) * gate_column).astype(bf16)
    output_lower_grad = tn(output_low_scaled, attended)
    output_low_sum = (output_low.astype(f32) * gate_column).reshape(2, rows, rank).sum(0)
    output_upper_grad = tn(output_low_sum.astype(bf16), middle_low)

    def over_sequences(arrays):
        joined = [a.reshape(rank, size, -1) for a in arrays]
        joined = jnp.concatenate(joined, axis=2).transpose(1, 0, 2)
        mine = picked(joined, spot)
        for d in range(1, size):
            theirs = picked(joined, (spot + d) % size).astype(bf16)
            mine = mine + shifted(theirs, -d % size, size).astype(f32)
        every = lax.all_gather(mine.astype(bf16), ("seq", "dp"), axis=0, tiled=False)
        every = every.reshape(size, holders, rank, -1)
        return gather_adapters(every, adapter_all, adapters, [a.shape[1] for a in arrays])

    key_grad, value_grad, query_slots, query_sum = attend_back(
        query_rot,
        pairs,
        bias,
        totals,
        head_home,
        place,
        gate_column,
        output_low_back,
        output_lower,
        cosine,
        sine,
        cosine_all,
        sine_all,
    )
    query_back = send_cut(query_slots, experts, copies)
    half = key_grad.shape[1]
    pair_low_grad = nt(key_grad, pair_up[:, :half]) + nt(value_grad, pair_up[:, half:])
    pair_low_grad = pair_low_grad.astype(bf16)
    normed_grad = None
    for d in range(size - 1, -1, -1):
        block = slice(d * rows, (d + 1) * rows)
        back = nt(key_grad[block], pair_weight[:, :half]) + nt(value_grad[block], pair_weight[:, half:])
        back = back + nn(pair_low_grad[block], pair_down)
        if d:
            back = shifted(back.astype(bf16), -d % size, size).astype(f32)
        normed_grad = back if normed_grad is None else normed_grad + back
    pair_upper_grad = jnp.concatenate([tn(pair_low, key_grad), tn(pair_low, value_grad)], axis=1)
    pair_lower_grad = sum(
        tn(pair_low_grad[d * rows : (d + 1) * rows], normed_parts[d]) for d in range(size)
    )
    query_low_grad = nt(query_sum, query_upper).astype(bf16)
    query_upper_grad = tn(query_low, query_sum)
    query_lower_grad = tn(query_low_grad, normed)
    late = over_sequences(
        [
            after(pair_lower_grad, mlp_sums),
            pair_upper_grad,
            query_lower_grad,
            query_upper_grad,
            output_lower_grad,
            output_upper_grad,
        ]
    )
    input_parts = nt(query_back.reshape(holders * capacity, -1), query_full).astype(bf16)
    input_home = home_add(input_parts.reshape(holders, capacity, width), experts, copies)
    normed_grad = normed_grad + nn(place_any, input_home) + nn(query_low_grad, query_lower)
    normed_grad = normed_grad + nt(logit_grad.astype(bf16), router_weight)
    input_grad = norm_back(inputs, input_scale, norm_gain, normed_grad) + middle_grad

    down_near = sum(after(down, input_home).astype(f32) for down in down_near)
    down_near = down_near.astype(bf16).reshape(holders, capacity, width)
    down_total = nn(combines[0], home_add(down_near, experts, copies))
    for d, down in down_parts:
        down = after(down, query_back).reshape(holders, capacity, width)
        home = home_add(down, experts, copies)
        down_total = down_total + shifted(nn(combines[d], home).astype(bf16), -d % size, size).astype(f32)
    result = (middle + down_total).astype(bf16)

    return (
        result[None],
        input_grad[None],
        flat_down(late[0]),
        late[1],
        flat_down(late[2]),
        late[3],
        flat_down(late[4]),
        late[5],
        flat_down(inner_down_grad),
        inner_up_grad,
        flat_down(outer_down_grad),
        outer_up_grad,
    )


def solution(mesh):
    split = P("dp", "seq", None)
    placed = (
        (split, P(), P("seq", None), P(), split, split, P(), P(), split, split)
        + (P(),) * 10
        + (split, split, P("dp"), P("dp"), split)
    )
    return jax.shard_map(
        body,
        mesh=mesh,
        in_specs=placed,
        out_specs=(split, split) + (P(),) * 10,
        check_vma=False,
    )
```

```python
import functools
import math

import jax
import jax.numpy as jnp
import numpy as np
from jax import lax
from jax.experimental import pallas as pl
from jax.experimental.pallas import tpu as pltpu
from jax.sharding import PartitionSpec as P

KV_HEADS = 16
HD = 128

norm_eps = 1e-05
rope_base = 10000.0
masked_score = -1e30
vmem_bytes = 48 * 2**20

bf16 = jnp.bfloat16
f32 = jnp.float32


def product(left, right, left_dim, right_dim):
    return lax.dot_general(
        left, right, (((left_dim,), (right_dim,)), ((), ())), preferred_element_type=f32
    )


def nn(left, right):
    return product(left, right, 1, 0)


def nt(left, right):
    return product(left, right, 1, 1)


def tn(left, right):
    return product(left, right, 0, 0)


def pair_kernel(count, key_blocks, *refs):
    normed_refs = refs[:count]
    w_ref, down_ref, up_ref, cos_ref, sin_ref, out_ref, low_ref = refs[count:]
    rows = normed_refs[0].shape[0]
    step = pl.program_id(0)

    @pl.when(step == 0)
    def _():
        for k in range(count):
            low_ref[pl.ds(k * rows, rows), :] = nt(normed_refs[k][...], down_ref[...]).astype(bf16)

    for k in range(count):
        part = pl.ds(k * rows, rows)
        made = nn(normed_refs[k][...], w_ref[0]) + nn(low_ref[part, :], up_ref[...])

        @pl.when(step < key_blocks)
        def _():
            for start in range(0, made.shape[1], HD):
                head = made[:, start : start + HD]
                turned = head * cos_ref[part, :] + pltpu.roll(head, HD // 2, 1) * sin_ref[part, :]
                out_ref[part, start : start + HD] = turned.astype(bf16)

        @pl.when(step >= key_blocks)
        def _():
            out_ref[part, :] = made.astype(bf16)


def project_pairs(normed_parts, weight, down, upper, cosine, sine):
    count = len(normed_parts)
    rows, width = normed_parts[0].shape
    blocks, _, block = weight.shape
    columns = blocks * block
    whole = lambda array: pl.BlockSpec(array.shape, lambda i: (0, 0))
    return pl.pallas_call(
        functools.partial(pair_kernel, count, blocks // 2),
        grid=(blocks,),
        in_specs=[whole(n) for n in normed_parts]
        + [
            pl.BlockSpec((1, width, block), lambda i: (i, 0, 0)),
            whole(down),
            pl.BlockSpec((upper.shape[0], block), lambda i: (0, i)),
            whole(cosine),
            whole(sine),
        ],
        out_specs=[
            pl.BlockSpec((count * rows, block), lambda i: (0, i)),
            pl.BlockSpec((count * rows, down.shape[0]), lambda i: (0, 0)),
        ],
        out_shape=[
            jax.ShapeDtypeStruct((count * rows, columns), bf16),
            jax.ShapeDtypeStruct((count * rows, down.shape[0]), bf16),
        ],
        compiler_params=pltpu.CompilerParams(vmem_limit_bytes=vmem_bytes),
        cost_estimate=pl.CostEstimate(
            flops=2 * count * rows * width * columns,
            bytes_accessed=2 * width * columns,
            transcendentals=0,
        ),
        name="pairs",
    )(*normed_parts, weight, down, upper, cosine, sine)


def pair_back_kernel(key_blocks, key_ref, value_ref, w_ref, low_ref, down_ref, out_ref, sum_ref):
    step = pl.program_id(0)

    @pl.when(step == 0)
    def _():
        sum_ref[...] = nn(low_ref[...], down_ref[...])

    @pl.when(step < key_blocks)
    def _():
        sum_ref[...] += nt(key_ref[...], w_ref[0])

    @pl.when(step >= key_blocks)
    def _():
        sum_ref[...] += nt(value_ref[...], w_ref[0])

    @pl.when(step == pl.num_programs(0) - 1)
    def _():
        out_ref[...] = sum_ref[...].astype(bf16)


def pair_back(key_grad, value_grad, weight, low_grad, down):
    blocks, width, block = weight.shape
    rows = key_grad.shape[0]
    half = blocks // 2
    whole = lambda array: pl.BlockSpec(array.shape, lambda i: (0, 0))
    return pl.pallas_call(
        functools.partial(pair_back_kernel, half),
        grid=(blocks,),
        in_specs=[
            pl.BlockSpec((rows, block), lambda i: (0, jnp.minimum(i, half - 1))),
            pl.BlockSpec((rows, block), lambda i: (0, jnp.maximum(i - half, 0))),
            pl.BlockSpec((1, width, block), lambda i: (i, 0, 0)),
            whole(low_grad),
            whole(down),
        ],
        out_specs=pl.BlockSpec((rows, width), lambda i: (0, 0)),
        out_shape=jax.ShapeDtypeStruct((rows, width), bf16),
        scratch_shapes=[pltpu.VMEM((rows, width), f32)],
        compiler_params=pltpu.CompilerParams(vmem_limit_bytes=vmem_bytes),
        cost_estimate=pl.CostEstimate(
            flops=2 * rows * width * blocks * block,
            bytes_accessed=2 * width * blocks * block,
            transcendentals=0,
        ),
        name="pair_back",
    )(key_grad, value_grad, weight, low_grad, down)


def attend_kernel(
    scale,
    home_ref,
    place_ref,
    low_ref,
    up_ref,
    cos_ref,
    sin_ref,
    key_ref,
    value_ref,
    bias_ref,
    attended_ref,
    slots_ref,
    query_ref,
    total_ref,
):
    rows = cos_ref.shape[0]
    base = nn(place_ref[...], home_ref[...])
    extra = nn(low_ref[...], up_ref[...])
    keys, values = key_ref[...], value_ref[...]
    for route in range(2):
        part = pl.ds(route * rows, rows)
        query = base[route * rows : (route + 1) * rows] + extra
        query = query * cos_ref[...] + pltpu.roll(query, HD // 2, 1) * sin_ref[...]
        query = query.astype(bf16)
        query_ref[part, :] = query
        scores = nt(query, keys) * scale + bias_ref[...]
        highest = jnp.max(scores, axis=1, keepdims=True)
        weights = jnp.exp(scores - highest)
        total = jnp.sum(weights, axis=1, keepdims=True)
        attended = nn(weights.astype(bf16), values) / total
        attended_ref[part, :] = attended.astype(bf16)
        total_ref[0, part, :] = highest + jnp.log(total)
    slots_ref[...] = tn(place_ref[...], attended_ref[...]).astype(bf16)


def attend(home, place, low, upper, cosine, sine, pairs, bias):
    rows2, slots = place.shape
    rows, length = bias.shape
    heads = home.shape[1] // HD
    kv_heads = pairs.shape[1] // (2 * HD)
    whole = lambda array: pl.BlockSpec(array.shape, lambda h: (0, 0))
    return pl.pallas_call(
        functools.partial(attend_kernel, 1.0 / math.sqrt(HD)),
        grid=(heads,),
        in_specs=[
            pl.BlockSpec((slots, HD), lambda h: (0, h)),
            whole(place),
            whole(low),
            pl.BlockSpec((upper.shape[0], HD), lambda h: (0, h)),
            whole(cosine),
            whole(sine),
            pl.BlockSpec((length, HD), lambda h: (0, h)),
            pl.BlockSpec((length, HD), lambda h: (0, kv_heads + h)),
            whole(bias),
        ],
        out_specs=[
            pl.BlockSpec((rows2, HD), lambda h: (0, h)),
            pl.BlockSpec((slots, HD), lambda h: (0, h)),
            pl.BlockSpec((rows2, HD), lambda h: (0, h)),
            pl.BlockSpec((1, rows2, 1), lambda h: (h, 0, 0)),
        ],
        out_shape=[
            jax.ShapeDtypeStruct((rows2, heads * HD), bf16),
            jax.ShapeDtypeStruct((slots, heads * HD), bf16),
            jax.ShapeDtypeStruct((rows2, heads * HD), bf16),
            jax.ShapeDtypeStruct((heads, rows2, 1), f32),
        ],
        compiler_params=pltpu.CompilerParams(vmem_limit_bytes=vmem_bytes),
        cost_estimate=pl.CostEstimate(
            flops=4 * heads * rows2 * length * HD,
            bytes_accessed=4 * length * heads * HD,
            transcendentals=heads * rows2 * length,
        ),
        name="attend",
    )(home, place, low, upper, cosine, sine, pairs, pairs, bias)


def attend_back_kernel(
    scale,
    query_ref,
    key_ref,
    value_ref,
    bias_ref,
    total_ref,
    home_ref,
    place_ref,
    gate_ref,
    low_ref,
    down_ref,
    cos_ref,
    sin_ref,
    cos_all_ref,
    sin_all_ref,
    key_grad_ref,
    value_grad_ref,
    slots_ref,
    sum_ref,
    turned_ref,
):
    rows = cos_ref.shape[0]
    base = nn(place_ref[...], home_ref[...])
    extra = nn(low_ref[...], down_ref[...])
    keys, values = key_ref[...], value_ref[...]
    key_grad = value_grad = None
    for route in range(2):
        part = pl.ds(route * rows, rows)
        query = query_ref[part, :]
        grad = (base[route * rows : (route + 1) * rows] + extra) * gate_ref[part, :]
        grad = grad.astype(bf16)
        scores = nt(query, keys) * scale + bias_ref[...]
        weights = jnp.exp(scores - total_ref[0, part, :])
        weight_grad = nt(grad, values)
        mean_grad = jnp.sum(weights * weight_grad, axis=1, keepdims=True)
        score_grad = (weights * (weight_grad - mean_grad)).astype(bf16)
        query_grad = nn(score_grad, keys) * scale
        query_grad = query_grad * cos_ref[...] - pltpu.roll(query_grad, HD // 2, 1) * sin_ref[...]
        turned_ref[part, :] = query_grad.astype(bf16)
        key_part = tn(score_grad, query)
        value_part = tn(weights.astype(bf16), grad)
        key_grad = key_part if route == 0 else key_grad + key_part
        value_grad = value_part if route == 0 else value_grad + value_part
    key_grad = key_grad * scale
    key_grad = key_grad * cos_all_ref[...] - pltpu.roll(key_grad, HD // 2, 1) * sin_all_ref[...]
    key_grad_ref[...] = key_grad.astype(bf16)
    value_grad_ref[...] = value_grad.astype(bf16)
    slots_ref[...] = tn(place_ref[...], turned_ref[...]).astype(bf16)
    first = turned_ref[pl.ds(0, rows), :].astype(f32)
    sum_ref[...] = (first + turned_ref[pl.ds(rows, rows), :].astype(f32)).astype(bf16)


def attend_back(query, pairs, bias, totals, home, place, gates, low, down, cosine, sine, cosine_all, sine_all):
    rows2, slots = place.shape
    rows, length = bias.shape
    heads = home.shape[1] // HD
    kv_heads = pairs.shape[1] // (2 * HD)
    whole = lambda array: pl.BlockSpec(array.shape, lambda h: (0, 0))
    return pl.pallas_call(
        functools.partial(attend_back_kernel, 1.0 / math.sqrt(HD)),
        grid=(heads,),
        in_specs=[
            pl.BlockSpec((rows2, HD), lambda h: (0, h)),
            pl.BlockSpec((length, HD), lambda h: (0, h)),
            pl.BlockSpec((length, HD), lambda h: (0, kv_heads + h)),
            whole(bias),
            pl.BlockSpec((1, rows2, 1), lambda h: (h, 0, 0)),
            pl.BlockSpec((slots, HD), lambda h: (0, h)),
            whole(place),
            whole(gates),
            whole(low),
            pl.BlockSpec((down.shape[0], HD), lambda h: (0, h)),
            whole(cosine),
            whole(sine),
            whole(cosine_all),
            whole(sine_all),
        ],
        out_specs=[
            pl.BlockSpec((length, HD), lambda h: (0, h)),
            pl.BlockSpec((length, HD), lambda h: (0, h)),
            pl.BlockSpec((slots, HD), lambda h: (0, h)),
            pl.BlockSpec((rows, HD), lambda h: (0, h)),
        ],
        out_shape=[
            jax.ShapeDtypeStruct((length, heads * HD), bf16),
            jax.ShapeDtypeStruct((length, heads * HD), bf16),
            jax.ShapeDtypeStruct((slots, heads * HD), bf16),
            jax.ShapeDtypeStruct((rows, heads * HD), bf16),
        ],
        scratch_shapes=[pltpu.VMEM((rows2, HD), bf16)],
        compiler_params=pltpu.CompilerParams(vmem_limit_bytes=vmem_bytes),
        cost_estimate=pl.CostEstimate(
            flops=10 * heads * rows2 * length * HD,
            bytes_accessed=8 * length * heads * HD,
            transcendentals=heads * rows2 * length,
        ),
        name="attend_back",
    )(query, pairs, pairs, bias, totals, home, place, gates, low, down, cosine, sine, cosine_all, sine_all)


def exchange(buffer):
    return lax.all_to_all(buffer, "dp", split_axis=0, concat_axis=0, tiled=True)


def in_order(parts, spot):
    count = len(parts)
    twice = jnp.concatenate(parts + parts, axis=0)
    rows = parts[0].shape[0]
    return lax.dynamic_slice_in_dim(twice, (count - spot) % count * rows, count * rows, 0)


def shifted(array, shift, size):
    if shift == 0:
        return array
    return lax.ppermute(array, "seq", [(k, (k - shift) % size) for k in range(size)])


def send_full(slots, experts, copies):
    buffer = slots.reshape(experts, slots.shape[0] // experts, slots.shape[1])
    if copies > 1:
        buffer = jnp.repeat(buffer, copies, axis=0)
    return exchange(buffer)


def send_cut(slots, experts, copies):
    buffer = slots.reshape(experts, slots.shape[0] // experts, slots.shape[1])
    if copies > 1:
        _, rows, columns = buffer.shape
        buffer = buffer.reshape(experts, rows, copies, columns // copies).transpose(0, 2, 1, 3)
        buffer = buffer.reshape(experts * copies, rows, columns // copies)
    return exchange(buffer)


def home_join(parts, experts, copies):
    home = exchange(parts)
    _, rows, columns = home.shape
    if copies > 1:
        home = home.reshape(experts, copies, rows, columns).transpose(0, 2, 1, 3)
    return home.reshape(experts * rows, copies * columns)


def home_add(parts, experts, copies):
    home = exchange(parts)
    _, rows, columns = home.shape
    if copies > 1:
        home = home.reshape(experts, copies, rows, columns).astype(f32)
        home = jnp.sum(home, axis=1).astype(parts.dtype)
    return home.reshape(experts * rows, columns)


def slot_layout(route_ids, experts, capacity):
    flat = route_ids.T.reshape(-1)
    count = flat.shape[0]
    hits = flat[:, None] == jnp.arange(experts)[None, :]
    earlier = jnp.arange(count)[:, None] > jnp.arange(count)[None, :]
    before = nn(earlier.astype(bf16), hits.astype(bf16))
    rank = jnp.sum(jnp.where(hits, before, 0.0), axis=1).astype(jnp.int32)
    slot = flat * capacity + rank
    return (slot[:, None] == jnp.arange(experts * capacity)[None, :]).astype(bf16)


def either(place):
    rows = place.shape[0] // 2
    return place[:rows] + place[rows:]


def norm_back(values, scale, gain, grad):
    weighted = grad * gain
    mean = jnp.mean(weighted * values, axis=-1, keepdims=True)
    return weighted * scale - values * (scale * scale * scale * mean)


def norm_scale(values):
    return lax.rsqrt(jnp.mean(values * values, axis=-1, keepdims=True) + norm_eps)


def gate_pair(logits, route_ids):
    hits = (route_ids[:, :, None] == jnp.arange(logits.shape[1])).astype(f32)
    chosen = jnp.sum(hits * logits[:, None, :], axis=2)
    weights = jnp.exp(chosen - jnp.max(chosen, axis=1, keepdims=True))
    return weights / jnp.sum(weights, axis=1, keepdims=True), hits


def gate_back(gates, hits, grad):
    mean = jnp.sum(gates * grad, axis=1, keepdims=True)
    return jnp.sum((gates * (grad - mean))[:, :, None] * hits, axis=1)


def rope_full(length, start):
    half = HD // 2
    frequency = rope_base ** (-np.arange(half) / half)
    angles = np.arange(length)[:, None] * frequency[None, :]
    cosine, sine = np.cos(angles), np.sin(angles)
    tables = np.concatenate([cosine, cosine, -sine, sine], 1).astype(np.float32)
    tables = jnp.asarray(np.concatenate([tables, tables], 0))
    tables = lax.dynamic_slice_in_dim(tables, start, length, 0)
    return tables[:, :HD], tables[:, HD:]


def after(array, *earlier):
    return lax.optimization_barrier((array,) + earlier)[0]


def cut_kernel(target_ref, in_ref, out_ref):
    out_ref[...] = in_ref[...]


def cut_share(weight, target, size):
    rows, columns = weight.shape
    share = columns // 2 // size
    if share % 128:
        cut = weight.reshape(rows, 2, size, share)
        return lax.dynamic_index_in_dim(cut, target, 2, keepdims=False).reshape(rows, 2 * share)
    return pl.pallas_call(
        cut_kernel,
        grid_spec=pltpu.PrefetchScalarGridSpec(
            num_scalar_prefetch=1,
            grid=(2,),
            in_specs=[pl.BlockSpec((rows, share), lambda i, t: (0, i * size + t[0]))],
            out_specs=pl.BlockSpec((rows, share), lambda i, t: (0, i)),
        ),
        out_shape=jax.ShapeDtypeStruct((rows, 2 * share), bf16),
        compiler_params=pltpu.CompilerParams(vmem_limit_bytes=vmem_bytes),
        name="cut",
    )(target.reshape(1).astype(jnp.int32), weight)


def unpack_kernel(size, share, in_ref, inner_up_ref, outer_down_ref, inner_down_ref, outer_up_ref):
    spot = pl.program_id(1)
    got = in_ref[0, 0].astype(f32)
    hidden = size * share
    width = inner_down_ref.shape[2]
    start = pl.multiple_of(spot * share, 128)
    inner_up_ref[0, :, pl.ds(start, share)] = got[:, :share]
    inner_up_ref[0, :, pl.ds(pl.multiple_of(hidden + start, 128), share)] = got[:, share : 2 * share]
    outer_down_ref[0, :, pl.ds(start, share)] = got[:, 2 * share : 3 * share]
    inner_down = got[:, 3 * share : 3 * share + width]
    outer_up = got[:, 3 * share + width :]

    @pl.when(spot == 0)
    def _():
        inner_down_ref[0] = inner_down
        outer_up_ref[0] = outer_up

    @pl.when(spot > 0)
    def _():
        inner_down_ref[0] += inner_down
        outer_up_ref[0] += outer_up


def unpack_sums(sums, share, width):
    size, adapters, rank, columns = sums.shape
    hidden = size * share
    shapes = [2 * hidden, hidden, width, width]
    return pl.pallas_call(
        functools.partial(unpack_kernel, size, share),
        grid=(adapters, size),
        in_specs=[pl.BlockSpec((1, 1, rank, columns), lambda a, k: (k, a, 0, 0))],
        out_specs=[pl.BlockSpec((1, rank, n), lambda a, k: (a, 0, 0)) for n in shapes],
        out_shape=[jax.ShapeDtypeStruct((adapters, rank, n), f32) for n in shapes],
        compiler_params=pltpu.CompilerParams(vmem_limit_bytes=vmem_bytes),
        cost_estimate=pl.CostEstimate(
            flops=0, bytes_accessed=12 * adapters * rank * (3 * hidden + 2 * width), transcendentals=0
        ),
        name="unpack",
    )(sums)


def gather_adapters_kernel(adapters, ids_ref, in_ref, *out_refs):
    holders = in_ref.shape[1]
    start = 0
    for out_ref in out_refs:
        columns = out_ref.shape[2]
        parts = [in_ref[0, k, :, start : start + columns].astype(f32) for k in range(holders)]
        for a in range(adapters):
            total = None
            for k in range(holders):
                one = jnp.where(ids_ref[k] == a, parts[k], 0.0)
                total = one if total is None else total + one
            out_ref[a] = total
        start += columns


def gather_adapters(every, adapter_all, adapters, widths):
    size, holders, rank, columns = every.shape
    return pl.pallas_call(
        functools.partial(gather_adapters_kernel, adapters),
        grid_spec=pltpu.PrefetchScalarGridSpec(
            num_scalar_prefetch=1,
            grid=(size,),
            in_specs=[pl.BlockSpec((1, holders, rank, columns), lambda k, s: (k, 0, 0, 0))],
            out_specs=[
                pl.BlockSpec((adapters, rank, n // size), lambda k, s: (0, 0, k)) for n in widths
            ],
        ),
        out_shape=[jax.ShapeDtypeStruct((adapters, rank, n), f32) for n in widths],
        compiler_params=pltpu.CompilerParams(vmem_limit_bytes=vmem_bytes),
        name="gather_adapters",
    )(adapter_all, every)


def silu_parts(gate_part, up_part, hidden_grad):
    sigmoid = 1.0 / (1.0 + jnp.exp(-gate_part))
    active = gate_part * sigmoid
    activated = (active * up_part).astype(bf16)
    gate_grad = hidden_grad * up_part * sigmoid * (1.0 + gate_part * (1.0 - sigmoid))
    return activated, gate_grad.astype(bf16), (hidden_grad * active).astype(bf16)


def halves(value):
    high = value.astype(bf16)
    return high, (value - high.astype(f32)).astype(bf16)


def expert_kernel(size, share, spot_ref, x_ref, hidden_ref, mask_ref, up_ref, down_ref, *refs):
    w_refs = refs[:size]
    row_ref, active_ref, pre_ref, code_ref, back_ref = refs[size:]
    depth = w_refs[0].shape[0]
    width = size * depth
    columns = [pl.ds(pl.multiple_of((spot_ref[0] + k) % size * depth, 128), depth) for k in range(size)]
    code = nt(x_ref[...], down_ref[...]).astype(bf16) * mask_ref[...]
    code_ref[...] = code
    sums = None
    for start in range(0, share, 256):
        end = min(start + 256, share)

        def hidden(first, last):
            made = nn(code, up_ref[:, first:last])
            for k in range(size):
                made = made + nn(x_ref[:, columns[k]], w_refs[k][:, first:last])
            return made

        gate_part, up_part = hidden(start, end), hidden(share + start, share + end)
        hidden_grad = hidden_ref[:, start:end].astype(f32)
        activated, gate_grad, up_grad = silu_parts(gate_part, up_part, hidden_grad)
        active_ref[:, start:end] = activated
        pre_ref[:, start:end] = gate_grad
        pre_ref[:, share + start : share + end] = up_grad
        part = jnp.sum(activated.astype(f32) * hidden_grad, axis=1, keepdims=True)
        sums = part if sums is None else sums + part
    back = nt(pre_ref[...], up_ref[...]).astype(bf16) * mask_ref[...]
    back_ref[...] = back
    for k in range(size):
        base = (spot_ref[0] + k) % size * depth
        for start in range(0, depth, 256):
            end = min(start + 256, depth)
            here = pl.ds(pl.multiple_of(base + start, 128), end - start)
            made = nt(pre_ref[...], w_refs[k][start:end, :]) + nn(back, down_ref[:, here])
            row_ref[:, here] = made.astype(bf16)
    high, low = halves(sums)
    lane = lax.broadcasted_iota(jnp.int32, (sums.shape[0], 128), 1)
    packed = jnp.where(lane == 0, high.astype(f32), jnp.where(lane == 1, low.astype(f32), 0.0))
    row_ref[:, width:] = packed.astype(bf16)


def expert_block(got, hidden_grad, mask, inner_up, inner_down, inner_parts, spot):
    size = len(inner_parts)
    rows, width = got.shape
    share = hidden_grad.shape[1]
    codes = mask.shape[1]
    if share % 128 or width // size % 256:
        code = nt(got, inner_down).astype(bf16) * mask
        inner_full = in_order(inner_parts, spot)
        pre = nn(got, inner_full) + nn(code, inner_up)
        hidden_float = hidden_grad.astype(f32)
        activated, gate_grad, up_grad = silu_parts(pre[:, :share], pre[:, share:], hidden_float)
        pre_grad = jnp.concatenate([gate_grad, up_grad], axis=1)
        back = nt(pre_grad, inner_up).astype(bf16) * mask
        row_grad = (nt(pre_grad, inner_full) + nn(back, inner_down)).astype(bf16)
        sums = jnp.stack(halves(jnp.sum(activated.astype(f32) * hidden_float, axis=1)), axis=1)
        row_grad = jnp.concatenate([row_grad, jnp.pad(sums, ((0, 0), (0, 126)))], axis=1)
        return row_grad, activated, pre_grad, code, back
    block = rows // 2
    ahead = lambda n: pl.BlockSpec((block, n), lambda i, s: (i, 0))
    whole = lambda array: pl.BlockSpec(array.shape, lambda i, s: (0, 0), pipeline_mode=pl.Buffered(1))
    shapes = [width + 128, share, 2 * share, codes, codes]
    return pl.pallas_call(
        functools.partial(expert_kernel, size, share),
        grid_spec=pltpu.PrefetchScalarGridSpec(
            num_scalar_prefetch=1,
            grid=(2,),
            in_specs=[ahead(width), ahead(share), ahead(codes), whole(inner_up), whole(inner_down)]
            + [whole(part) for part in inner_parts],
            out_specs=[ahead(n) for n in shapes],
        ),
        out_shape=[jax.ShapeDtypeStruct((rows, n), bf16) for n in shapes],
        compiler_params=pltpu.CompilerParams(vmem_limit_bytes=vmem_bytes),
        cost_estimate=pl.CostEstimate(
            flops=8 * rows * width * share,
            bytes_accessed=4 * width * share + 10 * rows * width,
            transcendentals=rows * share,
        ),
        name="experts",
    )(spot.reshape(1).astype(jnp.int32), got, hidden_grad, mask, inner_up, inner_down, *inner_parts)


def picked(lookup, index):
    return lax.dynamic_index_in_dim(lookup, index, 0, keepdims=False)


def body(
    tokens,
    norm_gain,
    key_value_weight,
    router_weight,
    query_weight,
    output_weight,
    mlp_gain,
    mlp_router_weight,
    mlp_in_weight,
    mlp_out_weight,
    key_value_down,
    key_value_up,
    query_down,
    query_up,
    output_down,
    output_up,
    mlp_in_down,
    mlp_in_up,
    mlp_out_down,
    mlp_out_up,
    routes,
    mlp_routes,
    adapter_index,
    prefix_length,
    out_grad,
):
    seqs, rows, width = tokens.shape
    assert seqs == 1
    size, spot = lax.axis_size("seq"), lax.axis_index("seq")
    holders, holder = lax.axis_size("dp"), lax.axis_index("dp")
    experts = router_weight.shape[1]
    copies = holders // experts
    part = holder % copies
    capacity = 3 * rows // 8
    length = rows * size
    adapters, _, rank = key_value_down.shape
    codes = adapters * rank
    hidden = mlp_in_weight.shape[2] // 2
    share = hidden // size

    def flat_down(lookup):
        return lookup.transpose(0, 2, 1)

    adapter = adapter_index[0]
    adapter_all = exchange(jnp.broadcast_to(adapter_index[None], (holders, 128)))[:, 0]
    inputs = tokens[0].astype(f32)
    input_scale = norm_scale(inputs)
    normed = (inputs * input_scale * norm_gain).astype(bf16)

    gates, hits = gate_pair(nn(normed, router_weight), routes[0])
    place = slot_layout(routes[0], experts, capacity)
    place_any = either(place)
    query_rows = send_full(tn(place_any, normed).astype(bf16), experts, copies)
    query_full = lax.all_gather(query_weight[0], "seq", axis=0, tiled=True)
    block = key_value_weight.shape[1] // holders
    pair_piece = lax.dynamic_slice_in_dim(key_value_weight, holder * block, block, 1)
    packet = jnp.concatenate([normed, pair_piece.reshape(-1, width)], axis=0)
    packets = [packet] + [shifted(packet, d, size) for d in range(1, size)]
    normed_parts = [normed] + [p[:rows] for p in packets[1:]]
    pieces = [pair_piece] + [p[rows:].reshape(-1, block) for p in packets[1:]]
    place_mlp = slot_layout(mlp_routes[0], experts, capacity)
    grad_own = send_full(tn(either(place_mlp), out_grad[0]).astype(bf16), experts, copies)
    pair_own = in_order(pieces, spot)
    pair_own = after(pair_own, query_full, query_rows, grad_own, adapter_all)
    pair_weight = lax.all_gather(pair_own, "dp", axis=0, tiled=False)
    lanes = jnp.pad(mlp_routes[0].astype(bf16), ((0, 0), (0, 126)))
    packet = jnp.concatenate([out_grad[0], lanes], axis=1)
    packet_late = after(packet, query_full)
    early = [packet] + [shifted(packet_late, d, size) for d in range(1, size)]
    grad_parts = [out_grad[0]] + [p[:, :width] for p in early[1:]]
    routes_there = [p[:, width : width + 2].astype(jnp.int32) for p in early]
    outer_full = mlp_out_weight[0]

    pair_down, pair_up = picked(flat_down(key_value_down), adapter), picked(key_value_up, adapter)
    query_lower, query_upper = picked(flat_down(query_down), adapter), picked(query_up, adapter)
    output_lower, output_upper = picked(flat_down(output_down), adapter), picked(output_up, adapter)
    query_low = nt(normed, query_lower).astype(bf16)
    positions = spot * rows + jnp.arange(rows)
    key_pos = (spot * rows + jnp.arange(length)) % length
    cosine_all, sine_all = rope_full(length, spot * rows)
    cosine, sine = cosine_all[:rows], sine_all[:rows]
    allowed = (key_pos[None, :] <= positions[:, None]) | (key_pos[None, :] < prefix_length[0])
    bias = jnp.where(allowed, 0.0, masked_score).astype(f32)

    mask = (jnp.arange(codes)[None, None, :] // rank == adapter_all[:, None, None]).astype(bf16)
    mask = jnp.broadcast_to(mask, (holders, capacity, codes)).reshape(-1, codes)
    inner_down = flat_down(mlp_in_down).reshape(codes, width)
    outer_up = mlp_out_up.reshape(codes, width)
    inner_up = mlp_in_up.reshape(codes, 2, copies, size, share)
    inner_up = lax.dynamic_index_in_dim(inner_up, part, 2, keepdims=False)
    inner_up = lax.dynamic_index_in_dim(inner_up, spot, 2, keepdims=False).reshape(codes, 2 * share)
    outer_down = flat_down(mlp_out_down).reshape(codes, copies, size, share)
    outer_down = lax.dynamic_index_in_dim(outer_down, part, 1, keepdims=False)
    outer_down = lax.dynamic_index_in_dim(outer_down, spot, 1, keepdims=False)

    places = [place_mlp] + [slot_layout(r, experts, capacity) for r in routes_there[1:]]
    query_rows = after(query_rows, *normed_parts[1:])
    query_parts = nn(query_rows.reshape(-1, width), query_full).astype(bf16)
    query_home = home_join(query_parts.reshape(holders, capacity, -1), experts, copies)
    pairs, pair_low = project_pairs(
        normed_parts, pair_weight, pair_down, pair_up, cosine_all, sine_all
    )
    far = size // 2
    inner_sent = [cut_share(mlp_in_weight[0], (spot - d) % size, size) for d in range(size)]
    inner_parts = list(inner_sent)
    inner_parts[far] = shifted(after(inner_sent[far], *early[1:]), far, size)
    output_own = after(output_weight[0], pair_weight, query_home, *early[1:])
    output_full = lax.all_gather(output_own, "seq", axis=0, tiled=True)
    attended, output_slots, query_rot, totals = attend(
        query_home, place, query_low, query_upper, cosine, sine, pairs, bias
    )

    output_rows = send_cut(output_slots, experts, copies)
    output_rows = after(output_rows, inner_parts[far])
    output_parts = nn(output_rows.reshape(holders * capacity, -1), output_full).astype(bf16)
    distances = [d for d in range(1, size) if d != far]
    before = output_full
    for d in distances:
        before = inner_parts[d] = shifted(after(inner_sent[d], before), d, size)
    output_home = home_add(output_parts.reshape(holders, capacity, width), experts, copies)
    output_low = nt(attended, output_lower).astype(bf16)
    branch = nn(place, output_home) + nn(output_low, output_upper)
    branch = branch.reshape(2, rows, width)
    middle = inputs + gates[:, :1] * branch[0] + gates[:, 1:] * branch[1]
    middle_scale = norm_scale(middle)
    normed_mlp = (middle * middle_scale * mlp_gain).astype(bf16)
    mlp_gates, mlp_hits = gate_pair(nn(normed_mlp, mlp_router_weight), mlp_routes[0])

    lanes = jnp.pad(jnp.concatenate(halves(mlp_gates), axis=1), ((0, 0), (0, 124)))
    packet = jnp.concatenate([normed_mlp, lanes], axis=1)
    packet = after(packet, *(inner_parts[d] for d in distances[:1]))
    packets = [shifted(packet, d, size) for d in range(size)]
    gates_there = [
        (p[:, width : width + 2].astype(f32) + p[:, width + 2 : width + 4].astype(f32)).T.reshape(-1, 1)
        for p in packets
    ]
    combines = [either((places[d].astype(f32) * gates_there[d]).astype(bf16)) for d in range(size)]
    order = list(range(size))
    grad_rows = [grad_own.reshape(-1, width)]
    for d in order[1:]:
        sent = tn(either(places[d]), after(grad_parts[d], output_home)).astype(bf16)
        grad_rows.append(send_full(sent, experts, copies).reshape(-1, width))
    outer_codes = [nt(got, outer_up).astype(bf16) * mask for got in grad_rows]
    hidden_grads = [
        (nt(got, outer_full) + nn(code, outer_down)).astype(bf16)
        for got, code in zip(grad_rows, outer_codes)
    ]
    gate_slots = jnp.stack(
        [jnp.sum(places[d].astype(f32) * gates_there[d], axis=0) for d in range(size)]
    )
    gate_slots = gate_slots.reshape(size, experts, capacity).transpose(1, 0, 2)
    gate_slots = exchange(jnp.repeat(gate_slots, copies, axis=0))

    def send_rows(d, *earlier):
        sent = tn(either(places[d]), after(packets[d][:, :width], *earlier)).astype(bf16)
        return send_full(sent, experts, copies).reshape(-1, width)

    def work(d, got):
        return expert_block(got, hidden_grads[d], mask, inner_up, inner_down, inner_parts, spot)

    def rows_home(d, row_grad):
        home = home_add(row_grad.reshape(holders, capacity, -1), experts, copies)
        row_sum = nn(combines[d], home[:, :width])
        gate_sum = nn(places[d], home[:, width:])
        lanes = gate_sum[:rows] + jnp.roll(gate_sum[rows:], 2, axis=1)
        row_back = jnp.concatenate([row_sum, lanes], axis=1)
        return home, shifted(row_back.astype(bf16), -d % size, size) if d else row_back

    got_rows = [send_rows(0, *grad_rows[:2])]
    kept = [work(0, got_rows[0])]
    row_home, row_total = rows_home(0, kept[0][0])
    row_backs = [row_total]
    for d in order[1:]:
        earlier = grad_rows[2:] + [inner_parts[k] for k in distances] if d == 1 else [got_rows[-1]]
        got_rows.append(send_rows(d, row_home, *earlier))
    for d in order[1:]:
        kept.append(work(d, after(got_rows[d], kept[-1][0])))
        row_grad = kept[d][0]
        if d > 2:
            row_grad = after(row_grad, row_backs[d - 2])
        row_home, row_back = rows_home(d, row_grad)
        row_backs.append(row_back)
        row_total = row_total + row_back.astype(f32)
    gate_sum = row_total[:, width : width + 4]
    row_total = row_total[:, :width]
    mlp_gate_grad = gate_sum.reshape(rows, 2, 2).sum(2)
    mlp_logit_grad = gate_back(mlp_gates, mlp_hits, mlp_gate_grad)

    down_near, down_parts, down_sent, sums = [], [], [], None
    for d in order:
        _, activated, pre_grad, code, back = kept[d]
        outer_low = nt(activated, outer_down).astype(bf16) * mask
        down = (nn(activated, outer_full) + nn(outer_low, outer_up)).astype(bf16)
        if d in (0, 1, size - 1):
            if d:
                down_sent.append(down)
                down = shifted(after(down, row_home), -d % size, size)
            down_near.append(down)
        else:
            down_sent.append(down)
            down_parts.append((d, down))
        scale = gate_slots[:, d, :].reshape(-1, 1)

        def scaled(array):
            return (array.astype(f32) * scale).astype(bf16)

        new = (
            tn(scaled(code), pre_grad),
            tn(scaled(outer_codes[d]), activated),
            tn(scaled(back), got_rows[d]),
            tn(scaled(outer_low), grad_rows[d]),
        )
        sums = new if sums is None else tuple(a + b for a, b in zip(sums, new))

    inner_up_sum, outer_down_sum, inner_down_sum, outer_up_sum = sums

    def widened(array):
        if copies == 1:
            return array
        whole = jnp.zeros((codes, copies, array.shape[1]), f32)
        whole = lax.dynamic_update_index_in_dim(whole, array, part, 1)
        return whole.reshape(codes, -1)

    wide = [widened(inner_up_sum), widened(outer_down_sum), inner_down_sum, outer_up_sum]
    ends = [sum(a.shape[1] for a in wide[: k + 1]) for k in range(3)]
    mlp_own = jnp.concatenate(wide, axis=1).astype(bf16)
    mlp_sums = lax.psum_scatter(mlp_own, "dp", scatter_dimension=0, tiled=True)
    mlp_sums = lax.all_gather(mlp_sums, ("seq", "dp"), axis=0, tiled=True)
    if copies == 1 and share % 128 == 0:
        inner_up_grad, outer_down_grad, inner_down_grad, outer_up_grad = unpack_sums(
            mlp_sums.reshape(size, adapters, rank, -1), share, width
        )
    else:
        mlp_sums = mlp_sums.astype(f32).reshape(size, codes, -1)
        inner_up_grad, outer_down_grad, inner_down_grad, outer_up_grad = jnp.split(mlp_sums, ends, axis=2)
        inner_up_grad = inner_up_grad.reshape(size, codes, copies, 2, share).transpose(1, 3, 2, 0, 4)
        inner_up_grad = inner_up_grad.reshape(adapters, rank, -1)
        outer_down_grad = outer_down_grad.reshape(size, codes, copies, share).transpose(1, 2, 0, 3)
        outer_down_grad = outer_down_grad.reshape(adapters, rank, -1)
        inner_down_grad = jnp.sum(inner_down_grad, 0).reshape(adapters, rank, width)
        outer_up_grad = jnp.sum(outer_up_grad, 0).reshape(adapters, rank, width)

    normed_mlp_grad = row_total + nt(mlp_logit_grad.astype(bf16), mlp_router_weight)
    middle_grad = norm_back(middle, middle_scale, mlp_gain, normed_mlp_grad)
    middle_grad = middle_grad + out_grad[0].astype(f32)
    middle_low = middle_grad.astype(bf16)
    branch_rows = send_full(tn(place_any, middle_low).astype(bf16), experts, copies)
    head_parts = nt(branch_rows.reshape(-1, width), output_full).astype(bf16)
    head_home = home_join(head_parts.reshape(holders, capacity, -1), experts, copies)
    head_home = after(head_home, mlp_own, *down_sent)
    gate_grad = jnp.sum(middle_grad[None] * branch, axis=2).T
    logit_grad = gate_back(gates, hits, gate_grad)
    gate_column = gates.T.reshape(-1, 1)
    output_low_grad = nt(middle_low, output_upper)
    output_low_back = output_low_grad.astype(bf16)
    output_low_scaled = (jnp.tile(output_low_grad, (2, 1)) * gate_column).astype(bf16)
    output_lower_grad = tn(output_low_scaled, attended)
    output_low_sum = (output_low.astype(f32) * gate_column).reshape(2, rows, rank).sum(0)
    output_upper_grad = tn(output_low_sum.astype(bf16), middle_low)

    def own_part(arrays):
        joined = [a.reshape(rank, size, -1) for a in arrays]
        joined = jnp.concatenate(joined, axis=2).transpose(1, 0, 2)
        mine = picked(joined, spot)
        for d in range(1, size):
            theirs = picked(joined, (spot + d) % size).astype(bf16)
            mine = mine + shifted(theirs, -d % size, size).astype(f32)
        return joined, mine.astype(bf16)

    def over_sequences(mine, widths):
        every = lax.all_gather(mine, ("seq", "dp"), axis=0, tiled=False)
        every = every.reshape(size, holders, rank, -1)
        return gather_adapters(every, adapter_all, adapters, widths)

    key_grad, value_grad, query_slots, query_sum = attend_back(
        query_rot,
        pairs,
        bias,
        totals,
        head_home,
        place,
        gate_column,
        output_low_back,
        output_lower,
        cosine,
        sine,
        cosine_all,
        sine_all,
    )
    query_back = send_cut(query_slots, experts, copies)
    half = key_grad.shape[1]
    pair_low_grad = nt(key_grad, pair_up[:, :half]) + nt(value_grad, pair_up[:, half:])
    pair_low_grad = pair_low_grad.astype(bf16)
    pair_upper_grad = jnp.concatenate([tn(pair_low, key_grad), tn(pair_low, value_grad)], axis=1)
    pair_lower_grad = sum(
        tn(pair_low_grad[d * rows : (d + 1) * rows], normed_parts[d]) for d in range(size)
    )
    query_low_grad = nt(query_sum, query_upper).astype(bf16)
    query_upper_grad = tn(query_low, query_sum)
    query_lower_grad = tn(query_low_grad, normed)
    sequence_grads = [
        pair_lower_grad,
        pair_upper_grad,
        query_lower_grad,
        query_upper_grad,
        output_lower_grad,
        output_upper_grad,
    ]
    joined, mine = own_part(sequence_grads)
    normed_grads = pair_back(
        after(key_grad, joined), value_grad, pair_weight, pair_low_grad, pair_down
    )
    mine = after(mine, mlp_sums, normed_grads)
    late = over_sequences(mine, [a.shape[1] for a in sequence_grads])
    back_parts = [
        shifted(normed_grads[d * rows : (d + 1) * rows], -d % size, size) for d in range(1, size)
    ]
    normed_grad = normed_grads[:rows].astype(f32) + sum(back.astype(f32) for back in back_parts)
    input_parts = nt(query_back.reshape(holders * capacity, -1), query_full).astype(bf16)
    input_home = home_add(input_parts.reshape(holders, capacity, width), experts, copies)
    normed_grad = normed_grad + nn(place_any, input_home) + nn(query_low_grad, query_lower)
    normed_grad = normed_grad + nt(logit_grad.astype(bf16), router_weight)
    input_grad = norm_back(inputs, input_scale, norm_gain, normed_grad) + middle_grad

    down_near = sum(after(down, input_home, *back_parts).astype(f32) for down in down_near)
    down_near = down_near.astype(bf16).reshape(holders, capacity, width)
    down_total = nn(combines[0], home_add(down_near, experts, copies))
    for d, down in down_parts:
        down = after(down, query_back).reshape(holders, capacity, width)
        home = home_add(down, experts, copies)
        down_total = down_total + shifted(nn(combines[d], home).astype(bf16), -d % size, size).astype(f32)
    result = (middle + down_total).astype(bf16)

    return (
        result[None],
        input_grad[None],
        flat_down(late[0]),
        late[1],
        flat_down(late[2]),
        late[3],
        flat_down(late[4]),
        late[5],
        flat_down(inner_down_grad),
        inner_up_grad,
        flat_down(outer_down_grad),
        outer_up_grad,
    )


def solution(mesh):
    split = P("dp", "seq", None)
    placed = (
        (split, P(), P("seq", None), P(), split, split, P(), P(), split, split)
        + (P(),) * 10
        + (split, split, P("dp"), P("dp"), split)
    )
    return jax.shard_map(
        body,
        mesh=mesh,
        in_specs=placed,
        out_specs=(split, split) + (P(),) * 10,
        check_vma=False,
    )
```

```python
import functools
import math

import jax
import jax.numpy as jnp
import numpy as np
from jax import lax
from jax.experimental import pallas as pl
from jax.experimental.pallas import tpu as pltpu
from jax.sharding import PartitionSpec as P

KV_HEADS = 16
HD = 128

norm_eps = 1e-05
rope_base = 10000.0
masked_score = -1e30
vmem_bytes = 48 * 2**20

bf16 = jnp.bfloat16
f32 = jnp.float32


def product(left, right, left_dim, right_dim):
    return lax.dot_general(
        left, right, (((left_dim,), (right_dim,)), ((), ())), preferred_element_type=f32
    )


def nn(left, right):
    return product(left, right, 1, 0)


def nt(left, right):
    return product(left, right, 1, 1)


def tn(left, right):
    return product(left, right, 0, 0)


def pair_kernel(count, key_blocks, *refs):
    normed_refs = refs[:count]
    w_ref, down_ref, up_ref, cos_ref, sin_ref, out_ref, low_ref = refs[count:]
    rows = normed_refs[0].shape[0]
    step = pl.program_id(0)

    @pl.when(step == 0)
    def _():
        for k in range(count):
            low_ref[pl.ds(k * rows, rows), :] = nt(normed_refs[k][...], down_ref[...]).astype(bf16)

    for k in range(count):
        part = pl.ds(k * rows, rows)
        made = nn(normed_refs[k][...], w_ref[0]) + nn(low_ref[part, :], up_ref[...])

        @pl.when(step < key_blocks)
        def _():
            for start in range(0, made.shape[1], HD):
                head = made[:, start : start + HD]
                turned = head * cos_ref[part, :] + pltpu.roll(head, HD // 2, 1) * sin_ref[part, :]
                out_ref[part, start : start + HD] = turned.astype(bf16)

        @pl.when(step >= key_blocks)
        def _():
            out_ref[part, :] = made.astype(bf16)


def project_pairs(normed_parts, weight, down, upper, cosine, sine):
    count = len(normed_parts)
    rows, width = normed_parts[0].shape
    blocks, _, block = weight.shape
    columns = blocks * block
    whole = lambda array: pl.BlockSpec(array.shape, lambda i: (0, 0))
    return pl.pallas_call(
        functools.partial(pair_kernel, count, blocks // 2),
        grid=(blocks,),
        in_specs=[whole(n) for n in normed_parts]
        + [
            pl.BlockSpec((1, width, block), lambda i: (i, 0, 0)),
            whole(down),
            pl.BlockSpec((upper.shape[0], block), lambda i: (0, i)),
            whole(cosine),
            whole(sine),
        ],
        out_specs=[
            pl.BlockSpec((count * rows, block), lambda i: (0, i)),
            pl.BlockSpec((count * rows, down.shape[0]), lambda i: (0, 0)),
        ],
        out_shape=[
            jax.ShapeDtypeStruct((count * rows, columns), bf16),
            jax.ShapeDtypeStruct((count * rows, down.shape[0]), bf16),
        ],
        compiler_params=pltpu.CompilerParams(vmem_limit_bytes=vmem_bytes),
        cost_estimate=pl.CostEstimate(
            flops=2 * count * rows * width * columns,
            bytes_accessed=2 * width * columns,
            transcendentals=0,
        ),
        name="pairs",
    )(*normed_parts, weight, down, upper, cosine, sine)


def pair_back_kernel(key_blocks, key_ref, value_ref, w_ref, low_ref, down_ref, out_ref, sum_ref):
    step = pl.program_id(0)

    @pl.when(step == 0)
    def _():
        sum_ref[...] = nn(low_ref[...], down_ref[...])

    @pl.when(step < key_blocks)
    def _():
        sum_ref[...] += nt(key_ref[...], w_ref[0])

    @pl.when(step >= key_blocks)
    def _():
        sum_ref[...] += nt(value_ref[...], w_ref[0])

    @pl.when(step == pl.num_programs(0) - 1)
    def _():
        out_ref[...] = sum_ref[...].astype(bf16)


def pair_back(key_grad, value_grad, weight, low_grad, down):
    blocks, width, block = weight.shape
    rows = key_grad.shape[0]
    half = blocks // 2
    whole = lambda array: pl.BlockSpec(array.shape, lambda i: (0, 0))
    return pl.pallas_call(
        functools.partial(pair_back_kernel, half),
        grid=(blocks,),
        in_specs=[
            pl.BlockSpec((rows, block), lambda i: (0, jnp.minimum(i, half - 1))),
            pl.BlockSpec((rows, block), lambda i: (0, jnp.maximum(i - half, 0))),
            pl.BlockSpec((1, width, block), lambda i: (i, 0, 0)),
            whole(low_grad),
            whole(down),
        ],
        out_specs=pl.BlockSpec((rows, width), lambda i: (0, 0)),
        out_shape=jax.ShapeDtypeStruct((rows, width), bf16),
        scratch_shapes=[pltpu.VMEM((rows, width), f32)],
        compiler_params=pltpu.CompilerParams(vmem_limit_bytes=vmem_bytes),
        cost_estimate=pl.CostEstimate(
            flops=2 * rows * width * blocks * block,
            bytes_accessed=2 * width * blocks * block,
            transcendentals=0,
        ),
        name="pair_back",
    )(key_grad, value_grad, weight, low_grad, down)


def attend_kernel(
    scale,
    home_ref,
    place_ref,
    low_ref,
    up_ref,
    cos_ref,
    sin_ref,
    key_ref,
    value_ref,
    bias_ref,
    attended_ref,
    slots_ref,
    query_ref,
    total_ref,
):
    rows = cos_ref.shape[0]
    base = nn(place_ref[...], home_ref[...])
    extra = nn(low_ref[...], up_ref[...])
    keys, values = key_ref[...], value_ref[...]
    for route in range(2):
        part = pl.ds(route * rows, rows)
        query = base[route * rows : (route + 1) * rows] + extra
        query = query * cos_ref[...] + pltpu.roll(query, HD // 2, 1) * sin_ref[...]
        query = query.astype(bf16)
        query_ref[part, :] = query
        scores = nt(query, keys) * scale + bias_ref[...]
        highest = jnp.max(scores, axis=1, keepdims=True)
        weights = jnp.exp(scores - highest)
        total = jnp.sum(weights, axis=1, keepdims=True)
        attended = nn(weights.astype(bf16), values) / total
        attended_ref[part, :] = attended.astype(bf16)
        total_ref[0, part, :] = highest + jnp.log(total)
    slots_ref[...] = tn(place_ref[...], attended_ref[...]).astype(bf16)


def attend(home, place, low, upper, cosine, sine, pairs, bias):
    rows2, slots = place.shape
    rows, length = bias.shape
    heads = home.shape[1] // HD
    kv_heads = pairs.shape[1] // (2 * HD)
    whole = lambda array: pl.BlockSpec(array.shape, lambda h: (0, 0))
    return pl.pallas_call(
        functools.partial(attend_kernel, 1.0 / math.sqrt(HD)),
        grid=(heads,),
        in_specs=[
            pl.BlockSpec((slots, HD), lambda h: (0, h)),
            whole(place),
            whole(low),
            pl.BlockSpec((upper.shape[0], HD), lambda h: (0, h)),
            whole(cosine),
            whole(sine),
            pl.BlockSpec((length, HD), lambda h: (0, h)),
            pl.BlockSpec((length, HD), lambda h: (0, kv_heads + h)),
            whole(bias),
        ],
        out_specs=[
            pl.BlockSpec((rows2, HD), lambda h: (0, h)),
            pl.BlockSpec((slots, HD), lambda h: (0, h)),
            pl.BlockSpec((rows2, HD), lambda h: (0, h)),
            pl.BlockSpec((1, rows2, 1), lambda h: (h, 0, 0)),
        ],
        out_shape=[
            jax.ShapeDtypeStruct((rows2, heads * HD), bf16),
            jax.ShapeDtypeStruct((slots, heads * HD), bf16),
            jax.ShapeDtypeStruct((rows2, heads * HD), bf16),
            jax.ShapeDtypeStruct((heads, rows2, 1), f32),
        ],
        compiler_params=pltpu.CompilerParams(vmem_limit_bytes=vmem_bytes),
        cost_estimate=pl.CostEstimate(
            flops=4 * heads * rows2 * length * HD,
            bytes_accessed=4 * length * heads * HD,
            transcendentals=heads * rows2 * length,
        ),
        name="attend",
    )(home, place, low, upper, cosine, sine, pairs, pairs, bias)


def attend_back_kernel(
    scale,
    query_ref,
    key_ref,
    value_ref,
    bias_ref,
    total_ref,
    home_ref,
    place_ref,
    gate_ref,
    low_ref,
    down_ref,
    cos_ref,
    sin_ref,
    cos_all_ref,
    sin_all_ref,
    key_grad_ref,
    value_grad_ref,
    slots_ref,
    sum_ref,
    turned_ref,
):
    rows = cos_ref.shape[0]
    base = nn(place_ref[...], home_ref[...])
    extra = nn(low_ref[...], down_ref[...])
    keys, values = key_ref[...], value_ref[...]
    key_grad = value_grad = None
    for route in range(2):
        part = pl.ds(route * rows, rows)
        query = query_ref[part, :]
        grad = (base[route * rows : (route + 1) * rows] + extra) * gate_ref[part, :]
        grad = grad.astype(bf16)
        scores = nt(query, keys) * scale + bias_ref[...]
        weights = jnp.exp(scores - total_ref[0, part, :])
        weight_grad = nt(grad, values)
        mean_grad = jnp.sum(weights * weight_grad, axis=1, keepdims=True)
        score_grad = (weights * (weight_grad - mean_grad)).astype(bf16)
        query_grad = nn(score_grad, keys) * scale
        query_grad = query_grad * cos_ref[...] - pltpu.roll(query_grad, HD // 2, 1) * sin_ref[...]
        turned_ref[part, :] = query_grad.astype(bf16)
        key_part = tn(score_grad, query)
        value_part = tn(weights.astype(bf16), grad)
        key_grad = key_part if route == 0 else key_grad + key_part
        value_grad = value_part if route == 0 else value_grad + value_part
    key_grad = key_grad * scale
    key_grad = key_grad * cos_all_ref[...] - pltpu.roll(key_grad, HD // 2, 1) * sin_all_ref[...]
    key_grad_ref[...] = key_grad.astype(bf16)
    value_grad_ref[...] = value_grad.astype(bf16)
    slots_ref[...] = tn(place_ref[...], turned_ref[...]).astype(bf16)
    first = turned_ref[pl.ds(0, rows), :].astype(f32)
    sum_ref[...] = (first + turned_ref[pl.ds(rows, rows), :].astype(f32)).astype(bf16)


def attend_back(query, pairs, bias, totals, home, place, gates, low, down, cosine, sine, cosine_all, sine_all):
    rows2, slots = place.shape
    rows, length = bias.shape
    heads = home.shape[1] // HD
    kv_heads = pairs.shape[1] // (2 * HD)
    whole = lambda array: pl.BlockSpec(array.shape, lambda h: (0, 0))
    return pl.pallas_call(
        functools.partial(attend_back_kernel, 1.0 / math.sqrt(HD)),
        grid=(heads,),
        in_specs=[
            pl.BlockSpec((rows2, HD), lambda h: (0, h)),
            pl.BlockSpec((length, HD), lambda h: (0, h)),
            pl.BlockSpec((length, HD), lambda h: (0, kv_heads + h)),
            whole(bias),
            pl.BlockSpec((1, rows2, 1), lambda h: (h, 0, 0)),
            pl.BlockSpec((slots, HD), lambda h: (0, h)),
            whole(place),
            whole(gates),
            whole(low),
            pl.BlockSpec((down.shape[0], HD), lambda h: (0, h)),
            whole(cosine),
            whole(sine),
            whole(cosine_all),
            whole(sine_all),
        ],
        out_specs=[
            pl.BlockSpec((length, HD), lambda h: (0, h)),
            pl.BlockSpec((length, HD), lambda h: (0, h)),
            pl.BlockSpec((slots, HD), lambda h: (0, h)),
            pl.BlockSpec((rows, HD), lambda h: (0, h)),
        ],
        out_shape=[
            jax.ShapeDtypeStruct((length, heads * HD), bf16),
            jax.ShapeDtypeStruct((length, heads * HD), bf16),
            jax.ShapeDtypeStruct((slots, heads * HD), bf16),
            jax.ShapeDtypeStruct((rows, heads * HD), bf16),
        ],
        scratch_shapes=[pltpu.VMEM((rows2, HD), bf16)],
        compiler_params=pltpu.CompilerParams(vmem_limit_bytes=vmem_bytes),
        cost_estimate=pl.CostEstimate(
            flops=10 * heads * rows2 * length * HD,
            bytes_accessed=8 * length * heads * HD,
            transcendentals=heads * rows2 * length,
        ),
        name="attend_back",
    )(query, pairs, pairs, bias, totals, home, place, gates, low, down, cosine, sine, cosine_all, sine_all)


def exchange(buffer):
    return lax.all_to_all(buffer, "dp", split_axis=0, concat_axis=0, tiled=True)


def in_order(parts, spot):
    count = len(parts)
    twice = jnp.concatenate(parts + parts, axis=0)
    rows = parts[0].shape[0]
    return lax.dynamic_slice_in_dim(twice, (count - spot) % count * rows, count * rows, 0)


def shifted(array, shift, size):
    if shift == 0:
        return array
    return lax.ppermute(array, "seq", [(k, (k - shift) % size) for k in range(size)])


def send_full(slots, experts, copies):
    buffer = slots.reshape(experts, slots.shape[0] // experts, slots.shape[1])
    if copies > 1:
        buffer = jnp.repeat(buffer, copies, axis=0)
    return exchange(buffer)


def send_cut(slots, experts, copies):
    buffer = slots.reshape(experts, slots.shape[0] // experts, slots.shape[1])
    if copies > 1:
        _, rows, columns = buffer.shape
        buffer = buffer.reshape(experts, rows, copies, columns // copies).transpose(0, 2, 1, 3)
        buffer = buffer.reshape(experts * copies, rows, columns // copies)
    return exchange(buffer)


def home_join(parts, experts, copies):
    home = exchange(parts)
    _, rows, columns = home.shape
    if copies > 1:
        home = home.reshape(experts, copies, rows, columns).transpose(0, 2, 1, 3)
    return home.reshape(experts * rows, copies * columns)


def home_add(parts, experts, copies):
    home = exchange(parts)
    _, rows, columns = home.shape
    if copies > 1:
        home = home.reshape(experts, copies, rows, columns).astype(f32)
        home = jnp.sum(home, axis=1).astype(parts.dtype)
    return home.reshape(experts * rows, columns)


def slot_layout(route_ids, experts, capacity):
    flat = route_ids.T.reshape(-1)
    count = flat.shape[0]
    hits = flat[:, None] == jnp.arange(experts)[None, :]
    earlier = jnp.arange(count)[:, None] > jnp.arange(count)[None, :]
    before = nn(earlier.astype(bf16), hits.astype(bf16))
    rank = jnp.sum(jnp.where(hits, before, 0.0), axis=1).astype(jnp.int32)
    slot = flat * capacity + rank
    return (slot[:, None] == jnp.arange(experts * capacity)[None, :]).astype(bf16)


def either(place):
    rows = place.shape[0] // 2
    return place[:rows] + place[rows:]


def norm_back(values, scale, gain, grad):
    weighted = grad * gain
    mean = jnp.mean(weighted * values, axis=-1, keepdims=True)
    return weighted * scale - values * (scale * scale * scale * mean)


def norm_scale(values):
    return lax.rsqrt(jnp.mean(values * values, axis=-1, keepdims=True) + norm_eps)


def gate_pair(logits, route_ids):
    hits = (route_ids[:, :, None] == jnp.arange(logits.shape[1])).astype(f32)
    chosen = jnp.sum(hits * logits[:, None, :], axis=2)
    weights = jnp.exp(chosen - jnp.max(chosen, axis=1, keepdims=True))
    return weights / jnp.sum(weights, axis=1, keepdims=True), hits


def gate_back(gates, hits, grad):
    mean = jnp.sum(gates * grad, axis=1, keepdims=True)
    return jnp.sum((gates * (grad - mean))[:, :, None] * hits, axis=1)


def rope_full(length, start):
    half = HD // 2
    frequency = rope_base ** (-np.arange(half) / half)
    angles = np.arange(length)[:, None] * frequency[None, :]
    cosine, sine = np.cos(angles), np.sin(angles)
    tables = np.concatenate([cosine, cosine, -sine, sine], 1).astype(np.float32)
    tables = jnp.asarray(np.concatenate([tables, tables], 0))
    tables = lax.dynamic_slice_in_dim(tables, start, length, 0)
    return tables[:, :HD], tables[:, HD:]


def after(array, *earlier):
    return lax.optimization_barrier((array,) + earlier)[0]


def cut_kernel(target_ref, in_ref, out_ref):
    out_ref[...] = in_ref[...]


def cut_share(weight, target, size):
    rows, columns = weight.shape
    share = columns // 2 // size
    if share % 128:
        cut = weight.reshape(rows, 2, size, share)
        return lax.dynamic_index_in_dim(cut, target, 2, keepdims=False).reshape(rows, 2 * share)
    return pl.pallas_call(
        cut_kernel,
        grid_spec=pltpu.PrefetchScalarGridSpec(
            num_scalar_prefetch=1,
            grid=(2,),
            in_specs=[pl.BlockSpec((rows, share), lambda i, t: (0, i * size + t[0]))],
            out_specs=pl.BlockSpec((rows, share), lambda i, t: (0, i)),
        ),
        out_shape=jax.ShapeDtypeStruct((rows, 2 * share), bf16),
        compiler_params=pltpu.CompilerParams(vmem_limit_bytes=vmem_bytes),
        name="cut",
    )(target.reshape(1).astype(jnp.int32), weight)


def unpack_kernel(size, share, in_ref, inner_up_ref, outer_down_ref, inner_down_ref, outer_up_ref):
    spot = pl.program_id(1)
    got = in_ref[0, 0].astype(f32)
    hidden = size * share
    width = inner_down_ref.shape[2]
    start = pl.multiple_of(spot * share, 128)
    inner_up_ref[0, :, pl.ds(start, share)] = got[:, :share]
    inner_up_ref[0, :, pl.ds(pl.multiple_of(hidden + start, 128), share)] = got[:, share : 2 * share]
    outer_down_ref[0, :, pl.ds(start, share)] = got[:, 2 * share : 3 * share]
    inner_down = got[:, 3 * share : 3 * share + width]
    outer_up = got[:, 3 * share + width :]

    @pl.when(spot == 0)
    def _():
        inner_down_ref[0] = inner_down
        outer_up_ref[0] = outer_up

    @pl.when(spot > 0)
    def _():
        inner_down_ref[0] += inner_down
        outer_up_ref[0] += outer_up


def unpack_sums(sums, share, width):
    size, adapters, rank, columns = sums.shape
    hidden = size * share
    shapes = [2 * hidden, hidden, width, width]
    return pl.pallas_call(
        functools.partial(unpack_kernel, size, share),
        grid=(adapters, size),
        in_specs=[pl.BlockSpec((1, 1, rank, columns), lambda a, k: (k, a, 0, 0))],
        out_specs=[pl.BlockSpec((1, rank, n), lambda a, k: (a, 0, 0)) for n in shapes],
        out_shape=[jax.ShapeDtypeStruct((adapters, rank, n), f32) for n in shapes],
        compiler_params=pltpu.CompilerParams(vmem_limit_bytes=vmem_bytes),
        cost_estimate=pl.CostEstimate(
            flops=0, bytes_accessed=12 * adapters * rank * (3 * hidden + 2 * width), transcendentals=0
        ),
        name="unpack",
    )(sums)


def gather_adapters_kernel(adapters, ids_ref, in_ref, *out_refs):
    holders = in_ref.shape[1]
    start = 0
    for out_ref in out_refs:
        columns = out_ref.shape[2]
        parts = [in_ref[0, k, :, start : start + columns].astype(f32) for k in range(holders)]
        for a in range(adapters):
            total = None
            for k in range(holders):
                one = jnp.where(ids_ref[k] == a, parts[k], 0.0)
                total = one if total is None else total + one
            out_ref[a] = total
        start += columns


def gather_adapters(every, adapter_all, adapters, widths):
    size, holders, rank, columns = every.shape
    return pl.pallas_call(
        functools.partial(gather_adapters_kernel, adapters),
        grid_spec=pltpu.PrefetchScalarGridSpec(
            num_scalar_prefetch=1,
            grid=(size,),
            in_specs=[pl.BlockSpec((1, holders, rank, columns), lambda k, s: (k, 0, 0, 0))],
            out_specs=[
                pl.BlockSpec((adapters, rank, n // size), lambda k, s: (0, 0, k)) for n in widths
            ],
        ),
        out_shape=[jax.ShapeDtypeStruct((adapters, rank, n), f32) for n in widths],
        compiler_params=pltpu.CompilerParams(vmem_limit_bytes=vmem_bytes),
        name="gather_adapters",
    )(adapter_all, every)


def silu_parts(gate_part, up_part, hidden_grad):
    sigmoid = 1.0 / (1.0 + jnp.exp(-gate_part))
    active = gate_part * sigmoid
    activated = (active * up_part).astype(bf16)
    gate_grad = hidden_grad * up_part * sigmoid * (1.0 + gate_part * (1.0 - sigmoid))
    return activated, gate_grad.astype(bf16), (hidden_grad * active).astype(bf16)


def halves(value):
    high = value.astype(bf16)
    return high, (value - high.astype(f32)).astype(bf16)


def expert_kernel(size, share, spot_ref, x_ref, hidden_ref, mask_ref, up_ref, down_ref, *refs):
    w_refs = refs[:size]
    row_ref, active_ref, pre_ref, code_ref, back_ref = refs[size:]
    depth = w_refs[0].shape[0]
    width = size * depth
    columns = [pl.ds(pl.multiple_of((spot_ref[0] + k) % size * depth, 128), depth) for k in range(size)]
    code = nt(x_ref[...], down_ref[...]).astype(bf16) * mask_ref[...]
    code_ref[...] = code
    sums = None
    for start in range(0, share, 256):
        end = min(start + 256, share)

        def hidden(first, last):
            made = nn(code, up_ref[:, first:last])
            for k in range(size):
                made = made + nn(x_ref[:, columns[k]], w_refs[k][:, first:last])
            return made

        gate_part, up_part = hidden(start, end), hidden(share + start, share + end)
        hidden_grad = hidden_ref[:, start:end].astype(f32)
        activated, gate_grad, up_grad = silu_parts(gate_part, up_part, hidden_grad)
        active_ref[:, start:end] = activated
        pre_ref[:, start:end] = gate_grad
        pre_ref[:, share + start : share + end] = up_grad
        part = jnp.sum(activated.astype(f32) * hidden_grad, axis=1, keepdims=True)
        sums = part if sums is None else sums + part
    back = nt(pre_ref[...], up_ref[...]).astype(bf16) * mask_ref[...]
    back_ref[...] = back
    for k in range(size):
        base = (spot_ref[0] + k) % size * depth
        for start in range(0, depth, 256):
            end = min(start + 256, depth)
            here = pl.ds(pl.multiple_of(base + start, 128), end - start)
            made = nt(pre_ref[...], w_refs[k][start:end, :]) + nn(back, down_ref[:, here])
            row_ref[:, here] = made.astype(bf16)
    high, low = halves(sums)
    lane = lax.broadcasted_iota(jnp.int32, (sums.shape[0], 128), 1)
    packed = jnp.where(lane == 0, high.astype(f32), jnp.where(lane == 1, low.astype(f32), 0.0))
    row_ref[:, width:] = packed.astype(bf16)


def expert_block(got, hidden_grad, mask, inner_up, inner_down, inner_parts, spot):
    size = len(inner_parts)
    rows, width = got.shape
    share = hidden_grad.shape[1]
    codes = mask.shape[1]
    if share % 128 or width // size % 256:
        code = nt(got, inner_down).astype(bf16) * mask
        inner_full = in_order(inner_parts, spot)
        pre = nn(got, inner_full) + nn(code, inner_up)
        hidden_float = hidden_grad.astype(f32)
        activated, gate_grad, up_grad = silu_parts(pre[:, :share], pre[:, share:], hidden_float)
        pre_grad = jnp.concatenate([gate_grad, up_grad], axis=1)
        back = nt(pre_grad, inner_up).astype(bf16) * mask
        row_grad = (nt(pre_grad, inner_full) + nn(back, inner_down)).astype(bf16)
        sums = jnp.stack(halves(jnp.sum(activated.astype(f32) * hidden_float, axis=1)), axis=1)
        row_grad = jnp.concatenate([row_grad, jnp.pad(sums, ((0, 0), (0, 126)))], axis=1)
        return row_grad, activated, pre_grad, code, back
    block = rows // 2
    ahead = lambda n: pl.BlockSpec((block, n), lambda i, s: (i, 0))
    whole = lambda array: pl.BlockSpec(array.shape, lambda i, s: (0, 0), pipeline_mode=pl.Buffered(1))
    shapes = [width + 128, share, 2 * share, codes, codes]
    return pl.pallas_call(
        functools.partial(expert_kernel, size, share),
        grid_spec=pltpu.PrefetchScalarGridSpec(
            num_scalar_prefetch=1,
            grid=(2,),
            in_specs=[ahead(width), ahead(share), ahead(codes), whole(inner_up), whole(inner_down)]
            + [whole(part) for part in inner_parts],
            out_specs=[ahead(n) for n in shapes],
        ),
        out_shape=[jax.ShapeDtypeStruct((rows, n), bf16) for n in shapes],
        compiler_params=pltpu.CompilerParams(vmem_limit_bytes=vmem_bytes),
        cost_estimate=pl.CostEstimate(
            flops=8 * rows * width * share,
            bytes_accessed=4 * width * share + 10 * rows * width,
            transcendentals=rows * share,
        ),
        name="experts",
    )(spot.reshape(1).astype(jnp.int32), got, hidden_grad, mask, inner_up, inner_down, *inner_parts)


def picked(lookup, index):
    return lax.dynamic_index_in_dim(lookup, index, 0, keepdims=False)


def body(
    tokens,
    norm_gain,
    key_value_weight,
    router_weight,
    query_weight,
    output_weight,
    mlp_gain,
    mlp_router_weight,
    mlp_in_weight,
    mlp_out_weight,
    key_value_down,
    key_value_up,
    query_down,
    query_up,
    output_down,
    output_up,
    mlp_in_down,
    mlp_in_up,
    mlp_out_down,
    mlp_out_up,
    routes,
    mlp_routes,
    adapter_index,
    prefix_length,
    out_grad,
):
    seqs, rows, width = tokens.shape
    assert seqs == 1
    size, spot = lax.axis_size("seq"), lax.axis_index("seq")
    holders, holder = lax.axis_size("dp"), lax.axis_index("dp")
    experts = router_weight.shape[1]
    copies = holders // experts
    part = holder % copies
    capacity = 3 * rows // 8
    length = rows * size
    adapters, _, rank = key_value_down.shape
    codes = adapters * rank
    hidden = mlp_in_weight.shape[2] // 2
    share = hidden // size

    def flat_down(lookup):
        return lookup.transpose(0, 2, 1)

    adapter = adapter_index[0]
    adapter_all = exchange(jnp.broadcast_to(adapter_index[None], (holders, 128)))[:, 0]
    inputs = tokens[0].astype(f32)
    input_scale = norm_scale(inputs)
    normed = (inputs * input_scale * norm_gain).astype(bf16)

    gates, hits = gate_pair(nn(normed, router_weight), routes[0])
    place = slot_layout(routes[0], experts, capacity)
    place_any = either(place)
    query_rows = send_full(tn(place_any, normed).astype(bf16), experts, copies)
    query_full = lax.all_gather(query_weight[0], "seq", axis=0, tiled=True)
    block = key_value_weight.shape[1] // holders
    pair_piece = lax.dynamic_slice_in_dim(key_value_weight, holder * block, block, 1)
    packet = jnp.concatenate([normed, pair_piece.reshape(-1, width)], axis=0)
    packets = [packet] + [shifted(packet, d, size) for d in range(1, size)]
    normed_parts = [normed] + [p[:rows] for p in packets[1:]]
    pieces = [pair_piece] + [p[rows:].reshape(-1, block) for p in packets[1:]]
    place_mlp = slot_layout(mlp_routes[0], experts, capacity)
    grad_own = send_full(tn(either(place_mlp), out_grad[0]).astype(bf16), experts, copies)
    pair_own = in_order(pieces, spot)
    pair_own = after(pair_own, query_full, query_rows, grad_own, adapter_all)
    pair_weight = lax.all_gather(pair_own, "dp", axis=0, tiled=False)
    lanes = jnp.pad(mlp_routes[0].astype(bf16), ((0, 0), (0, 126)))
    packet = jnp.concatenate([out_grad[0], lanes], axis=1)
    packet_late = after(packet, query_full)
    early = [packet] + [shifted(packet_late, d, size) for d in range(1, size)]
    grad_parts = [out_grad[0]] + [p[:, :width] for p in early[1:]]
    routes_there = [p[:, width : width + 2].astype(jnp.int32) for p in early]
    outer_full = mlp_out_weight[0]

    pair_down, pair_up = picked(flat_down(key_value_down), adapter), picked(key_value_up, adapter)
    query_lower, query_upper = picked(flat_down(query_down), adapter), picked(query_up, adapter)
    output_lower, output_upper = picked(flat_down(output_down), adapter), picked(output_up, adapter)
    query_low = nt(normed, query_lower).astype(bf16)
    positions = spot * rows + jnp.arange(rows)
    key_pos = (spot * rows + jnp.arange(length)) % length
    cosine_all, sine_all = rope_full(length, spot * rows)
    cosine, sine = cosine_all[:rows], sine_all[:rows]
    allowed = (key_pos[None, :] <= positions[:, None]) | (key_pos[None, :] < prefix_length[0])
    bias = jnp.where(allowed, 0.0, masked_score).astype(f32)

    mask = (jnp.arange(codes)[None, None, :] // rank == adapter_all[:, None, None]).astype(bf16)
    mask = jnp.broadcast_to(mask, (holders, capacity, codes)).reshape(-1, codes)
    inner_down = flat_down(mlp_in_down).reshape(codes, width)
    outer_up = mlp_out_up.reshape(codes, width)
    inner_up = mlp_in_up.reshape(codes, 2, copies, size, share)
    inner_up = lax.dynamic_index_in_dim(inner_up, part, 2, keepdims=False)
    inner_up = lax.dynamic_index_in_dim(inner_up, spot, 2, keepdims=False).reshape(codes, 2 * share)
    outer_down = flat_down(mlp_out_down).reshape(codes, copies, size, share)
    outer_down = lax.dynamic_index_in_dim(outer_down, part, 1, keepdims=False)
    outer_down = lax.dynamic_index_in_dim(outer_down, spot, 1, keepdims=False)

    places = [place_mlp] + [slot_layout(r, experts, capacity) for r in routes_there[1:]]
    query_rows = after(query_rows, *normed_parts[1:])
    query_parts = nn(query_rows.reshape(-1, width), query_full).astype(bf16)
    query_home = home_join(query_parts.reshape(holders, capacity, -1), experts, copies)
    pairs, pair_low = project_pairs(
        normed_parts, pair_weight, pair_down, pair_up, cosine_all, sine_all
    )
    output_own = after(output_weight[0], pair_weight, query_home, *early[1:])
    output_full = lax.all_gather(output_own, "seq", axis=0, tiled=True)
    grad_rows = [grad_own.reshape(-1, width)]
    for d in range(1, size):
        sent = grad_parts[d] if d < 2 else after(grad_parts[d], pairs)
        sent = tn(either(places[d]), sent).astype(bf16)
        grad_rows.append(send_full(sent, experts, copies).reshape(-1, width))
    attended, output_slots, query_rot, totals = attend(
        query_home, place, query_low, query_upper, cosine, sine, pairs, bias
    )

    output_rows = send_cut(output_slots, experts, copies)
    output_rows = after(output_rows, *grad_rows[:3])
    output_parts = nn(output_rows.reshape(holders * capacity, -1), output_full).astype(bf16)
    far = size // 2
    distances = [d for d in range(1, size) if d != far] + ([far] if size > 1 else [])
    inner_sent = [cut_share(mlp_in_weight[0], (spot - d) % size, size) for d in range(size)]
    inner_parts = list(inner_sent)
    before = output_full
    for d in distances:
        before = inner_parts[d] = shifted(after(inner_sent[d], before), d, size)
    output_home = home_add(output_parts.reshape(holders, capacity, width), experts, copies)
    output_low = nt(attended, output_lower).astype(bf16)
    branch = nn(place, output_home) + nn(output_low, output_upper)
    branch = branch.reshape(2, rows, width)
    middle = inputs + gates[:, :1] * branch[0] + gates[:, 1:] * branch[1]
    middle_scale = norm_scale(middle)
    normed_mlp = (middle * middle_scale * mlp_gain).astype(bf16)
    mlp_gates, mlp_hits = gate_pair(nn(normed_mlp, mlp_router_weight), mlp_routes[0])

    lanes = jnp.pad(jnp.concatenate(halves(mlp_gates), axis=1), ((0, 0), (0, 124)))
    packet = jnp.concatenate([normed_mlp, lanes], axis=1)
    packet = after(packet, *(inner_parts[d] for d in distances[:1]))
    packet_all = lax.all_gather(packet, "seq", axis=0, tiled=True)
    packets = [packet] + [
        lax.dynamic_slice_in_dim(packet_all, (spot + d) % size * rows, rows, 0)
        for d in range(1, size)
    ]
    gates_there = [
        (p[:, width : width + 2].astype(f32) + p[:, width + 2 : width + 4].astype(f32)).T.reshape(-1, 1)
        for p in packets
    ]
    combines = [either((places[d].astype(f32) * gates_there[d]).astype(bf16)) for d in range(size)]
    order = list(range(size))
    outer_codes = [nt(got, outer_up).astype(bf16) * mask for got in grad_rows]
    hidden_grads = [
        (nt(got, outer_full) + nn(code, outer_down)).astype(bf16)
        for got, code in zip(grad_rows, outer_codes)
    ]
    gate_slots = jnp.stack(
        [jnp.sum(places[d].astype(f32) * gates_there[d], axis=0) for d in range(size)]
    )
    gate_slots = gate_slots.reshape(size, experts, capacity).transpose(1, 0, 2)
    gate_slots = exchange(jnp.repeat(gate_slots, copies, axis=0))

    def send_rows(d, *earlier):
        sent = tn(either(places[d]), after(packets[d][:, :width], *earlier)).astype(bf16)
        return send_full(sent, experts, copies).reshape(-1, width)

    def work(d, got):
        return expert_block(got, hidden_grads[d], mask, inner_up, inner_down, inner_parts, spot)

    def rows_home(d, row_grad):
        home = home_add(row_grad.reshape(holders, capacity, -1), experts, copies)
        row_sum = nn(combines[d], home[:, :width])
        gate_sum = nn(places[d], home[:, width:])
        lanes = gate_sum[:rows] + jnp.roll(gate_sum[rows:], 2, axis=1)
        row_back = jnp.concatenate([row_sum, lanes], axis=1)
        return home, shifted(row_back.astype(bf16), -d % size, size) if d else row_back

    got_rows = [send_rows(0)]
    for d in order[1:]:
        earlier = [inner_parts[k] for k in distances[:-1]] if d == 1 else []
        got_rows.append(send_rows(d, got_rows[-1], *earlier))
    kept = [work(0, got_rows[0])]
    row_home, row_total = rows_home(0, kept[0][0])
    row_backs = [row_total]
    for d in order[1:]:
        kept.append(work(d, after(got_rows[d], kept[-1][0])))
        row_grad = kept[d][0]
        if d > 2:
            row_grad = after(row_grad, row_backs[d - 2])
        row_home, row_back = rows_home(d, row_grad)
        row_backs.append(row_back)
        row_total = row_total + row_back.astype(f32)
    gate_sum = row_total[:, width : width + 4]
    row_total = row_total[:, :width]
    mlp_gate_grad = gate_sum.reshape(rows, 2, 2).sum(2)
    mlp_logit_grad = gate_back(mlp_gates, mlp_hits, mlp_gate_grad)

    down_near, down_parts, down_made, sums = [], [], [], None
    for d in order:
        _, activated, pre_grad, code, back = kept[d]
        outer_low = nt(activated, outer_down).astype(bf16) * mask
        down = (nn(activated, outer_full) + nn(outer_low, outer_up)).astype(bf16)
        down_made.append(down)
        if d in (0, 1, size - 1):
            if d:
                down = shifted(after(down, row_home), -d % size, size)
            down_near.append(down)
        else:
            down_parts.append((d, down))
        scale = gate_slots[:, d, :].reshape(-1, 1)

        def scaled(array):
            return (array.astype(f32) * scale).astype(bf16)

        new = (
            tn(scaled(code), pre_grad),
            tn(scaled(outer_codes[d]), activated),
            tn(scaled(back), got_rows[d]),
            tn(scaled(outer_low), grad_rows[d]),
        )
        sums = new if sums is None else tuple(a + b for a, b in zip(sums, new))

    inner_up_sum, outer_down_sum, inner_down_sum, outer_up_sum = sums

    def widened(array):
        if copies == 1:
            return array
        whole = jnp.zeros((codes, copies, array.shape[1]), f32)
        whole = lax.dynamic_update_index_in_dim(whole, array, part, 1)
        return whole.reshape(codes, -1)

    wide = [widened(inner_up_sum), widened(outer_down_sum), inner_down_sum, outer_up_sum]
    ends = [sum(a.shape[1] for a in wide[: k + 1]) for k in range(3)]
    mlp_own = jnp.concatenate(wide, axis=1).astype(bf16)
    mlp_sums = lax.psum_scatter(mlp_own, "dp", scatter_dimension=0, tiled=True)
    mlp_sums = lax.all_gather(mlp_sums, ("seq", "dp"), axis=0, tiled=True)
    if copies == 1 and share % 128 == 0:
        inner_up_grad, outer_down_grad, inner_down_grad, outer_up_grad = unpack_sums(
            mlp_sums.reshape(size, adapters, rank, -1), share, width
        )
    else:
        mlp_sums = mlp_sums.astype(f32).reshape(size, codes, -1)
        inner_up_grad, outer_down_grad, inner_down_grad, outer_up_grad = jnp.split(mlp_sums, ends, axis=2)
        inner_up_grad = inner_up_grad.reshape(size, codes, copies, 2, share).transpose(1, 3, 2, 0, 4)
        inner_up_grad = inner_up_grad.reshape(adapters, rank, -1)
        outer_down_grad = outer_down_grad.reshape(size, codes, copies, share).transpose(1, 2, 0, 3)
        outer_down_grad = outer_down_grad.reshape(adapters, rank, -1)
        inner_down_grad = jnp.sum(inner_down_grad, 0).reshape(adapters, rank, width)
        outer_up_grad = jnp.sum(outer_up_grad, 0).reshape(adapters, rank, width)

    normed_mlp_grad = row_total + nt(mlp_logit_grad.astype(bf16), mlp_router_weight)
    middle_grad = norm_back(middle, middle_scale, mlp_gain, normed_mlp_grad)
    middle_grad = middle_grad + out_grad[0].astype(f32)
    middle_low = after(middle_grad.astype(bf16), *down_made)
    branch_rows = send_full(tn(place_any, middle_low).astype(bf16), experts, copies)
    head_parts = nt(branch_rows.reshape(-1, width), output_full).astype(bf16)
    head_home = home_join(head_parts.reshape(holders, capacity, -1), experts, copies)
    head_home = after(head_home, mlp_own)
    gate_grad = jnp.sum(middle_grad[None] * branch, axis=2).T
    logit_grad = gate_back(gates, hits, gate_grad)
    gate_column = gates.T.reshape(-1, 1)
    output_low_grad = nt(middle_low, output_upper)
    output_low_back = output_low_grad.astype(bf16)
    output_low_scaled = (jnp.tile(output_low_grad, (2, 1)) * gate_column).astype(bf16)
    output_lower_grad = tn(output_low_scaled, attended)
    output_low_sum = (output_low.astype(f32) * gate_column).reshape(2, rows, rank).sum(0)
    output_upper_grad = tn(output_low_sum.astype(bf16), middle_low)

    def own_part(arrays):
        joined = [a.reshape(rank, size, -1) for a in arrays]
        joined = jnp.concatenate(joined, axis=2).transpose(1, 0, 2)
        mine = picked(joined, spot)
        for d in range(1, size):
            theirs = picked(joined, (spot + d) % size).astype(bf16)
            mine = mine + shifted(theirs, -d % size, size).astype(f32)
        return joined, mine.astype(bf16)

    def over_sequences(mine, widths):
        every = lax.all_gather(mine, ("seq", "dp"), axis=0, tiled=False)
        every = every.reshape(size, holders, rank, -1)
        return gather_adapters(every, adapter_all, adapters, widths)

    key_grad, value_grad, query_slots, query_sum = attend_back(
        query_rot,
        pairs,
        bias,
        totals,
        head_home,
        place,
        gate_column,
        output_low_back,
        output_lower,
        cosine,
        sine,
        cosine_all,
        sine_all,
    )
    query_back = send_cut(query_slots, experts, copies)
    half = key_grad.shape[1]
    pair_low_grad = nt(key_grad, pair_up[:, :half]) + nt(value_grad, pair_up[:, half:])
    pair_low_grad = pair_low_grad.astype(bf16)
    pair_upper_grad = jnp.concatenate([tn(pair_low, key_grad), tn(pair_low, value_grad)], axis=1)
    pair_lower_grad = sum(
        tn(pair_low_grad[d * rows : (d + 1) * rows], normed_parts[d]) for d in range(size)
    )
    query_low_grad = nt(query_sum, query_upper).astype(bf16)
    query_upper_grad = tn(query_low, query_sum)
    query_lower_grad = tn(query_low_grad, normed)
    sequence_grads = [
        pair_lower_grad,
        pair_upper_grad,
        query_lower_grad,
        query_upper_grad,
        output_lower_grad,
        output_upper_grad,
    ]
    joined, mine = own_part(sequence_grads)
    normed_grads = pair_back(
        after(key_grad, joined), value_grad, pair_weight, pair_low_grad, pair_down
    )
    mine = after(mine, mlp_sums, normed_grads)
    late = over_sequences(mine, [a.shape[1] for a in sequence_grads])
    back_parts = [
        shifted(normed_grads[d * rows : (d + 1) * rows], -d % size, size) for d in range(1, size)
    ]
    down_near = sum(after(down, *back_parts).astype(f32) for down in down_near).astype(bf16)
    down_near = after(down_near, query_back).reshape(holders, capacity, width)
    down_home = home_add(down_near, experts, copies)
    own_back = after(normed_grads[:rows], inner_up_grad)
    normed_grad = own_back.astype(f32) + sum(back.astype(f32) for back in back_parts)
    input_parts = nt(query_back.reshape(holders * capacity, -1), query_full).astype(bf16)
    input_home = home_add(input_parts.reshape(holders, capacity, width), experts, copies)
    normed_grad = normed_grad + nn(place_any, input_home) + nn(query_low_grad, query_lower)
    normed_grad = normed_grad + nt(logit_grad.astype(bf16), router_weight)
    input_grad = norm_back(inputs, input_scale, norm_gain, normed_grad) + middle_grad

    down_total = nn(combines[0], down_home)
    for d, down in down_parts:
        down = after(down, input_home).reshape(holders, capacity, width)
        home = home_add(down, experts, copies)
        down_total = down_total + shifted(nn(combines[d], home).astype(bf16), -d % size, size).astype(f32)
    result = (middle + down_total).astype(bf16)

    return (
        result[None],
        input_grad[None],
        flat_down(late[0]),
        late[1],
        flat_down(late[2]),
        late[3],
        flat_down(late[4]),
        late[5],
        flat_down(inner_down_grad),
        inner_up_grad,
        flat_down(outer_down_grad),
        outer_up_grad,
    )


def solution(mesh):
    split = P("dp", "seq", None)
    placed = (
        (split, P(), P("seq", None), P(), split, split, P(), P(), split, split)
        + (P(),) * 10
        + (split, split, P("dp"), P("dp"), split)
    )
    return jax.shard_map(
        body,
        mesh=mesh,
        in_specs=placed,
        out_specs=(split, split) + (P(),) * 10,
        check_vma=False,
    )
```

```python
import functools
import math

import jax
import jax.numpy as jnp
import numpy as np
from jax import lax
from jax.experimental import pallas as pl
from jax.experimental.pallas import tpu as pltpu
from jax.sharding import PartitionSpec as P

KV_HEADS = 16
HD = 128

norm_eps = 1e-05
rope_base = 10000.0
masked_score = -1e30
vmem_bytes = 48 * 2**20

bf16 = jnp.bfloat16
f32 = jnp.float32


def product(left, right, left_dim, right_dim):
    return lax.dot_general(
        left, right, (((left_dim,), (right_dim,)), ((), ())), preferred_element_type=f32
    )


def nn(left, right):
    return product(left, right, 1, 0)


def nt(left, right):
    return product(left, right, 1, 1)


def tn(left, right):
    return product(left, right, 0, 0)


def pair_kernel(count, key_blocks, *refs):
    normed_refs = refs[:count]
    w_ref, down_ref, up_ref, cos_ref, sin_ref, out_ref, low_ref = refs[count:]
    rows = normed_refs[0].shape[0]
    step = pl.program_id(0)

    @pl.when(step == 0)
    def _():
        for k in range(count):
            low_ref[pl.ds(k * rows, rows), :] = nt(normed_refs[k][...], down_ref[...]).astype(bf16)

    for k in range(count):
        part = pl.ds(k * rows, rows)
        made = nn(normed_refs[k][...], w_ref[0]) + nn(low_ref[part, :], up_ref[...])

        @pl.when(step < key_blocks)
        def _():
            for start in range(0, made.shape[1], HD):
                head = made[:, start : start + HD]
                turned = head * cos_ref[part, :] + pltpu.roll(head, HD // 2, 1) * sin_ref[part, :]
                out_ref[part, start : start + HD] = turned.astype(bf16)

        @pl.when(step >= key_blocks)
        def _():
            out_ref[part, :] = made.astype(bf16)


def project_pairs(normed_parts, weight, down, upper, cosine, sine):
    count = len(normed_parts)
    rows, width = normed_parts[0].shape
    blocks, _, block = weight.shape
    columns = blocks * block
    whole = lambda array: pl.BlockSpec(array.shape, lambda i: (0, 0))
    return pl.pallas_call(
        functools.partial(pair_kernel, count, blocks // 2),
        grid=(blocks,),
        in_specs=[whole(n) for n in normed_parts]
        + [
            pl.BlockSpec((1, width, block), lambda i: (i, 0, 0)),
            whole(down),
            pl.BlockSpec((upper.shape[0], block), lambda i: (0, i)),
            whole(cosine),
            whole(sine),
        ],
        out_specs=[
            pl.BlockSpec((count * rows, block), lambda i: (0, i)),
            pl.BlockSpec((count * rows, down.shape[0]), lambda i: (0, 0)),
        ],
        out_shape=[
            jax.ShapeDtypeStruct((count * rows, columns), bf16),
            jax.ShapeDtypeStruct((count * rows, down.shape[0]), bf16),
        ],
        compiler_params=pltpu.CompilerParams(vmem_limit_bytes=vmem_bytes),
        cost_estimate=pl.CostEstimate(
            flops=2 * count * rows * width * columns,
            bytes_accessed=2 * width * columns,
            transcendentals=0,
        ),
        name="pairs",
    )(*normed_parts, weight, down, upper, cosine, sine)


def pair_back_kernel(key_blocks, key_ref, value_ref, w_ref, low_ref, down_ref, out_ref, sum_ref):
    step = pl.program_id(0)

    @pl.when(step == 0)
    def _():
        sum_ref[...] = nn(low_ref[...], down_ref[...])

    @pl.when(step < key_blocks)
    def _():
        sum_ref[...] += nt(key_ref[...], w_ref[0])

    @pl.when(step >= key_blocks)
    def _():
        sum_ref[...] += nt(value_ref[...], w_ref[0])

    @pl.when(step == pl.num_programs(0) - 1)
    def _():
        out_ref[...] = sum_ref[...].astype(bf16)


def pair_back(key_grad, value_grad, weight, low_grad, down):
    blocks, width, block = weight.shape
    rows = key_grad.shape[0]
    half = blocks // 2
    whole = lambda array: pl.BlockSpec(array.shape, lambda i: (0, 0))
    return pl.pallas_call(
        functools.partial(pair_back_kernel, half),
        grid=(blocks,),
        in_specs=[
            pl.BlockSpec((rows, block), lambda i: (0, jnp.minimum(i, half - 1))),
            pl.BlockSpec((rows, block), lambda i: (0, jnp.maximum(i - half, 0))),
            pl.BlockSpec((1, width, block), lambda i: (i, 0, 0)),
            whole(low_grad),
            whole(down),
        ],
        out_specs=pl.BlockSpec((rows, width), lambda i: (0, 0)),
        out_shape=jax.ShapeDtypeStruct((rows, width), bf16),
        scratch_shapes=[pltpu.VMEM((rows, width), f32)],
        compiler_params=pltpu.CompilerParams(vmem_limit_bytes=vmem_bytes),
        cost_estimate=pl.CostEstimate(
            flops=2 * rows * width * blocks * block,
            bytes_accessed=2 * width * blocks * block,
            transcendentals=0,
        ),
        name="pair_back",
    )(key_grad, value_grad, weight, low_grad, down)


def attend_kernel(
    scale,
    home_ref,
    place_ref,
    low_ref,
    up_ref,
    cos_ref,
    sin_ref,
    key_ref,
    value_ref,
    bias_ref,
    attended_ref,
    slots_ref,
    query_ref,
    total_ref,
):
    rows = cos_ref.shape[0]
    base = nn(place_ref[...], home_ref[...])
    extra = nn(low_ref[...], up_ref[...])
    keys, values = key_ref[...], value_ref[...]
    for route in range(2):
        part = pl.ds(route * rows, rows)
        query = base[route * rows : (route + 1) * rows] + extra
        query = query * cos_ref[...] + pltpu.roll(query, HD // 2, 1) * sin_ref[...]
        query = query.astype(bf16)
        query_ref[part, :] = query
        scores = nt(query, keys) * scale + bias_ref[...]
        highest = jnp.max(scores, axis=1, keepdims=True)
        weights = jnp.exp(scores - highest)
        total = jnp.sum(weights, axis=1, keepdims=True)
        attended = nn(weights.astype(bf16), values) / total
        attended_ref[part, :] = attended.astype(bf16)
        total_ref[0, part, :] = highest + jnp.log(total)
    slots_ref[...] = tn(place_ref[...], attended_ref[...]).astype(bf16)


def attend(home, place, low, upper, cosine, sine, pairs, bias):
    rows2, slots = place.shape
    rows, length = bias.shape
    heads = home.shape[1] // HD
    kv_heads = pairs.shape[1] // (2 * HD)
    whole = lambda array: pl.BlockSpec(array.shape, lambda h: (0, 0))
    return pl.pallas_call(
        functools.partial(attend_kernel, 1.0 / math.sqrt(HD)),
        grid=(heads,),
        in_specs=[
            pl.BlockSpec((slots, HD), lambda h: (0, h)),
            whole(place),
            whole(low),
            pl.BlockSpec((upper.shape[0], HD), lambda h: (0, h)),
            whole(cosine),
            whole(sine),
            pl.BlockSpec((length, HD), lambda h: (0, h)),
            pl.BlockSpec((length, HD), lambda h: (0, kv_heads + h)),
            whole(bias),
        ],
        out_specs=[
            pl.BlockSpec((rows2, HD), lambda h: (0, h)),
            pl.BlockSpec((slots, HD), lambda h: (0, h)),
            pl.BlockSpec((rows2, HD), lambda h: (0, h)),
            pl.BlockSpec((1, rows2, 1), lambda h: (h, 0, 0)),
        ],
        out_shape=[
            jax.ShapeDtypeStruct((rows2, heads * HD), bf16),
            jax.ShapeDtypeStruct((slots, heads * HD), bf16),
            jax.ShapeDtypeStruct((rows2, heads * HD), bf16),
            jax.ShapeDtypeStruct((heads, rows2, 1), f32),
        ],
        compiler_params=pltpu.CompilerParams(vmem_limit_bytes=vmem_bytes),
        cost_estimate=pl.CostEstimate(
            flops=4 * heads * rows2 * length * HD,
            bytes_accessed=4 * length * heads * HD,
            transcendentals=heads * rows2 * length,
        ),
        name="attend",
    )(home, place, low, upper, cosine, sine, pairs, pairs, bias)


def attend_back_kernel(
    scale,
    query_ref,
    key_ref,
    value_ref,
    bias_ref,
    total_ref,
    home_ref,
    place_ref,
    gate_ref,
    low_ref,
    down_ref,
    cos_ref,
    sin_ref,
    cos_all_ref,
    sin_all_ref,
    key_grad_ref,
    value_grad_ref,
    slots_ref,
    sum_ref,
    turned_ref,
):
    rows = cos_ref.shape[0]
    base = nn(place_ref[...], home_ref[...])
    extra = nn(low_ref[...], down_ref[...])
    keys, values = key_ref[...], value_ref[...]
    key_grad = value_grad = None
    for route in range(2):
        part = pl.ds(route * rows, rows)
        query = query_ref[part, :]
        grad = (base[route * rows : (route + 1) * rows] + extra) * gate_ref[part, :]
        grad = grad.astype(bf16)
        scores = nt(query, keys) * scale + bias_ref[...]
        weights = jnp.exp(scores - total_ref[0, part, :])
        weight_grad = nt(grad, values)
        mean_grad = jnp.sum(weights * weight_grad, axis=1, keepdims=True)
        score_grad = (weights * (weight_grad - mean_grad)).astype(bf16)
        query_grad = nn(score_grad, keys) * scale
        query_grad = query_grad * cos_ref[...] - pltpu.roll(query_grad, HD // 2, 1) * sin_ref[...]
        turned_ref[part, :] = query_grad.astype(bf16)
        key_part = tn(score_grad, query)
        value_part = tn(weights.astype(bf16), grad)
        key_grad = key_part if route == 0 else key_grad + key_part
        value_grad = value_part if route == 0 else value_grad + value_part
    key_grad = key_grad * scale
    key_grad = key_grad * cos_all_ref[...] - pltpu.roll(key_grad, HD // 2, 1) * sin_all_ref[...]
    key_grad_ref[...] = key_grad.astype(bf16)
    value_grad_ref[...] = value_grad.astype(bf16)
    slots_ref[...] = tn(place_ref[...], turned_ref[...]).astype(bf16)
    first = turned_ref[pl.ds(0, rows), :].astype(f32)
    sum_ref[...] = (first + turned_ref[pl.ds(rows, rows), :].astype(f32)).astype(bf16)


def attend_back(query, pairs, bias, totals, home, place, gates, low, down, cosine, sine, cosine_all, sine_all):
    rows2, slots = place.shape
    rows, length = bias.shape
    heads = home.shape[1] // HD
    kv_heads = pairs.shape[1] // (2 * HD)
    whole = lambda array: pl.BlockSpec(array.shape, lambda h: (0, 0))
    return pl.pallas_call(
        functools.partial(attend_back_kernel, 1.0 / math.sqrt(HD)),
        grid=(heads,),
        in_specs=[
            pl.BlockSpec((rows2, HD), lambda h: (0, h)),
            pl.BlockSpec((length, HD), lambda h: (0, h)),
            pl.BlockSpec((length, HD), lambda h: (0, kv_heads + h)),
            whole(bias),
            pl.BlockSpec((1, rows2, 1), lambda h: (h, 0, 0)),
            pl.BlockSpec((slots, HD), lambda h: (0, h)),
            whole(place),
            whole(gates),
            whole(low),
            pl.BlockSpec((down.shape[0], HD), lambda h: (0, h)),
            whole(cosine),
            whole(sine),
            whole(cosine_all),
            whole(sine_all),
        ],
        out_specs=[
            pl.BlockSpec((length, HD), lambda h: (0, h)),
            pl.BlockSpec((length, HD), lambda h: (0, h)),
            pl.BlockSpec((slots, HD), lambda h: (0, h)),
            pl.BlockSpec((rows, HD), lambda h: (0, h)),
        ],
        out_shape=[
            jax.ShapeDtypeStruct((length, heads * HD), bf16),
            jax.ShapeDtypeStruct((length, heads * HD), bf16),
            jax.ShapeDtypeStruct((slots, heads * HD), bf16),
            jax.ShapeDtypeStruct((rows, heads * HD), bf16),
        ],
        scratch_shapes=[pltpu.VMEM((rows2, HD), bf16)],
        compiler_params=pltpu.CompilerParams(vmem_limit_bytes=vmem_bytes),
        cost_estimate=pl.CostEstimate(
            flops=10 * heads * rows2 * length * HD,
            bytes_accessed=8 * length * heads * HD,
            transcendentals=heads * rows2 * length,
        ),
        name="attend_back",
    )(query, pairs, pairs, bias, totals, home, place, gates, low, down, cosine, sine, cosine_all, sine_all)


def exchange(buffer):
    return lax.all_to_all(buffer, "dp", split_axis=0, concat_axis=0, tiled=True)


def in_order(parts, spot):
    count = len(parts)
    twice = jnp.concatenate(parts + parts, axis=0)
    rows = parts[0].shape[0]
    return lax.dynamic_slice_in_dim(twice, (count - spot) % count * rows, count * rows, 0)


def shifted(array, shift, size):
    if shift == 0:
        return array
    return lax.ppermute(array, "seq", [(k, (k - shift) % size) for k in range(size)])


def send_full(slots, experts, copies):
    buffer = slots.reshape(experts, slots.shape[0] // experts, slots.shape[1])
    if copies > 1:
        buffer = jnp.repeat(buffer, copies, axis=0)
    return exchange(buffer)


def send_cut(slots, experts, copies):
    buffer = slots.reshape(experts, slots.shape[0] // experts, slots.shape[1])
    if copies > 1:
        _, rows, columns = buffer.shape
        buffer = buffer.reshape(experts, rows, copies, columns // copies).transpose(0, 2, 1, 3)
        buffer = buffer.reshape(experts * copies, rows, columns // copies)
    return exchange(buffer)


def home_join(parts, experts, copies):
    home = exchange(parts)
    _, rows, columns = home.shape
    if copies > 1:
        home = home.reshape(experts, copies, rows, columns).transpose(0, 2, 1, 3)
    return home.reshape(experts * rows, copies * columns)


def home_add(parts, experts, copies):
    home = exchange(parts)
    _, rows, columns = home.shape
    if copies > 1:
        home = home.reshape(experts, copies, rows, columns).astype(f32)
        home = jnp.sum(home, axis=1).astype(parts.dtype)
    return home.reshape(experts * rows, columns)


def slot_layout(route_ids, experts, capacity):
    flat = route_ids.T.reshape(-1)
    count = flat.shape[0]
    hits = flat[:, None] == jnp.arange(experts)[None, :]
    earlier = jnp.arange(count)[:, None] > jnp.arange(count)[None, :]
    before = nn(earlier.astype(bf16), hits.astype(bf16))
    rank = jnp.sum(jnp.where(hits, before, 0.0), axis=1).astype(jnp.int32)
    slot = flat * capacity + rank
    return (slot[:, None] == jnp.arange(experts * capacity)[None, :]).astype(bf16)


def either(place):
    rows = place.shape[0] // 2
    return place[:rows] + place[rows:]


def norm_back(values, scale, gain, grad):
    weighted = grad * gain
    mean = jnp.mean(weighted * values, axis=-1, keepdims=True)
    return weighted * scale - values * (scale * scale * scale * mean)


def norm_scale(values):
    return lax.rsqrt(jnp.mean(values * values, axis=-1, keepdims=True) + norm_eps)


def gate_pair(logits, route_ids):
    hits = (route_ids[:, :, None] == jnp.arange(logits.shape[1])).astype(f32)
    chosen = jnp.sum(hits * logits[:, None, :], axis=2)
    weights = jnp.exp(chosen - jnp.max(chosen, axis=1, keepdims=True))
    return weights / jnp.sum(weights, axis=1, keepdims=True), hits


def gate_back(gates, hits, grad):
    mean = jnp.sum(gates * grad, axis=1, keepdims=True)
    return jnp.sum((gates * (grad - mean))[:, :, None] * hits, axis=1)


def rope_full(length, start):
    half = HD // 2
    frequency = rope_base ** (-np.arange(half) / half)
    angles = np.arange(length)[:, None] * frequency[None, :]
    cosine, sine = np.cos(angles), np.sin(angles)
    tables = np.concatenate([cosine, cosine, -sine, sine], 1).astype(np.float32)
    tables = jnp.asarray(np.concatenate([tables, tables], 0))
    tables = lax.dynamic_slice_in_dim(tables, start, length, 0)
    return tables[:, :HD], tables[:, HD:]


def after(array, *earlier):
    return lax.optimization_barrier((array,) + earlier)[0]


def cut_kernel(target_ref, in_ref, out_ref):
    out_ref[...] = in_ref[...]


def cut_share(weight, target, size):
    rows, columns = weight.shape
    share = columns // 2 // size
    if share % 128:
        cut = weight.reshape(rows, 2, size, share)
        return lax.dynamic_index_in_dim(cut, target, 2, keepdims=False).reshape(rows, 2 * share)
    return pl.pallas_call(
        cut_kernel,
        grid_spec=pltpu.PrefetchScalarGridSpec(
            num_scalar_prefetch=1,
            grid=(2,),
            in_specs=[pl.BlockSpec((rows, share), lambda i, t: (0, i * size + t[0]))],
            out_specs=pl.BlockSpec((rows, share), lambda i, t: (0, i)),
        ),
        out_shape=jax.ShapeDtypeStruct((rows, 2 * share), bf16),
        compiler_params=pltpu.CompilerParams(vmem_limit_bytes=vmem_bytes),
        name="cut",
    )(target.reshape(1).astype(jnp.int32), weight)


def unpack_kernel(size, share, in_ref, inner_up_ref, outer_down_ref, inner_down_ref, outer_up_ref):
    spot = pl.program_id(1)
    got = in_ref[0, 0].astype(f32)
    hidden = size * share
    width = inner_down_ref.shape[2]
    start = pl.multiple_of(spot * share, 128)
    inner_up_ref[0, :, pl.ds(start, share)] = got[:, :share]
    inner_up_ref[0, :, pl.ds(pl.multiple_of(hidden + start, 128), share)] = got[:, share : 2 * share]
    outer_down_ref[0, :, pl.ds(start, share)] = got[:, 2 * share : 3 * share]
    inner_down = got[:, 3 * share : 3 * share + width]
    outer_up = got[:, 3 * share + width :]

    @pl.when(spot == 0)
    def _():
        inner_down_ref[0] = inner_down
        outer_up_ref[0] = outer_up

    @pl.when(spot > 0)
    def _():
        inner_down_ref[0] += inner_down
        outer_up_ref[0] += outer_up


def unpack_sums(sums, share, width):
    size, adapters, rank, columns = sums.shape
    hidden = size * share
    shapes = [2 * hidden, hidden, width, width]
    return pl.pallas_call(
        functools.partial(unpack_kernel, size, share),
        grid=(adapters, size),
        in_specs=[pl.BlockSpec((1, 1, rank, columns), lambda a, k: (k, a, 0, 0))],
        out_specs=[pl.BlockSpec((1, rank, n), lambda a, k: (a, 0, 0)) for n in shapes],
        out_shape=[jax.ShapeDtypeStruct((adapters, rank, n), f32) for n in shapes],
        compiler_params=pltpu.CompilerParams(vmem_limit_bytes=vmem_bytes),
        cost_estimate=pl.CostEstimate(
            flops=0, bytes_accessed=12 * adapters * rank * (3 * hidden + 2 * width), transcendentals=0
        ),
        name="unpack",
    )(sums)


def gather_adapters_kernel(adapters, ids_ref, in_ref, *out_refs):
    holders = in_ref.shape[1]
    start = 0
    for out_ref in out_refs:
        columns = out_ref.shape[2]
        parts = [in_ref[0, k, :, start : start + columns].astype(f32) for k in range(holders)]
        for a in range(adapters):
            total = None
            for k in range(holders):
                one = jnp.where(ids_ref[k] == a, parts[k], 0.0)
                total = one if total is None else total + one
            out_ref[a] = total
        start += columns


def gather_adapters(every, adapter_all, adapters, widths):
    size, holders, rank, columns = every.shape
    return pl.pallas_call(
        functools.partial(gather_adapters_kernel, adapters),
        grid_spec=pltpu.PrefetchScalarGridSpec(
            num_scalar_prefetch=1,
            grid=(size,),
            in_specs=[pl.BlockSpec((1, holders, rank, columns), lambda k, s: (k, 0, 0, 0))],
            out_specs=[
                pl.BlockSpec((adapters, rank, n // size), lambda k, s: (0, 0, k)) for n in widths
            ],
        ),
        out_shape=[jax.ShapeDtypeStruct((adapters, rank, n), f32) for n in widths],
        compiler_params=pltpu.CompilerParams(vmem_limit_bytes=vmem_bytes),
        name="gather_adapters",
    )(adapter_all, every)


def silu_parts(gate_part, up_part, hidden_grad):
    sigmoid = 1.0 / (1.0 + jnp.exp(-gate_part))
    active = gate_part * sigmoid
    activated = (active * up_part).astype(bf16)
    gate_grad = hidden_grad * up_part * sigmoid * (1.0 + gate_part * (1.0 - sigmoid))
    return activated, gate_grad.astype(bf16), (hidden_grad * active).astype(bf16)


def halves(value):
    high = value.astype(bf16)
    return high, (value - high.astype(f32)).astype(bf16)


def expert_kernel(size, share, spot_ref, x_ref, hidden_ref, mask_ref, up_ref, down_ref, *refs):
    w_refs = refs[:size]
    row_ref, active_ref, pre_ref, code_ref, back_ref = refs[size:]
    depth = w_refs[0].shape[0]
    width = size * depth
    columns = [pl.ds(pl.multiple_of((spot_ref[0] + k) % size * depth, 128), depth) for k in range(size)]
    code = nt(x_ref[...], down_ref[...]).astype(bf16) * mask_ref[...]
    code_ref[...] = code
    sums = None
    for start in range(0, share, 256):
        end = min(start + 256, share)

        def hidden(first, last):
            made = nn(code, up_ref[:, first:last])
            for k in range(size):
                made = made + nn(x_ref[:, columns[k]], w_refs[k][:, first:last])
            return made

        gate_part, up_part = hidden(start, end), hidden(share + start, share + end)
        hidden_grad = hidden_ref[:, start:end].astype(f32)
        activated, gate_grad, up_grad = silu_parts(gate_part, up_part, hidden_grad)
        active_ref[:, start:end] = activated
        pre_ref[:, start:end] = gate_grad
        pre_ref[:, share + start : share + end] = up_grad
        part = jnp.sum(activated.astype(f32) * hidden_grad, axis=1, keepdims=True)
        sums = part if sums is None else sums + part
    back = nt(pre_ref[...], up_ref[...]).astype(bf16) * mask_ref[...]
    back_ref[...] = back
    for k in range(size):
        base = (spot_ref[0] + k) % size * depth
        for start in range(0, depth, 256):
            end = min(start + 256, depth)
            here = pl.ds(pl.multiple_of(base + start, 128), end - start)
            made = nt(pre_ref[...], w_refs[k][start:end, :]) + nn(back, down_ref[:, here])
            row_ref[:, here] = made.astype(bf16)
    high, low = halves(sums)
    lane = lax.broadcasted_iota(jnp.int32, (sums.shape[0], 128), 1)
    packed = jnp.where(lane == 0, high.astype(f32), jnp.where(lane == 1, low.astype(f32), 0.0))
    row_ref[:, width:] = packed.astype(bf16)


def expert_block(got, hidden_grad, mask, inner_up, inner_down, inner_parts, spot):
    size = len(inner_parts)
    rows, width = got.shape
    share = hidden_grad.shape[1]
    codes = mask.shape[1]
    if share % 128 or width // size % 256:
        code = nt(got, inner_down).astype(bf16) * mask
        inner_full = in_order(inner_parts, spot)
        pre = nn(got, inner_full) + nn(code, inner_up)
        hidden_float = hidden_grad.astype(f32)
        activated, gate_grad, up_grad = silu_parts(pre[:, :share], pre[:, share:], hidden_float)
        pre_grad = jnp.concatenate([gate_grad, up_grad], axis=1)
        back = nt(pre_grad, inner_up).astype(bf16) * mask
        row_grad = (nt(pre_grad, inner_full) + nn(back, inner_down)).astype(bf16)
        sums = jnp.stack(halves(jnp.sum(activated.astype(f32) * hidden_float, axis=1)), axis=1)
        row_grad = jnp.concatenate([row_grad, jnp.pad(sums, ((0, 0), (0, 126)))], axis=1)
        return row_grad, activated, pre_grad, code, back
    block = rows // 2
    ahead = lambda n: pl.BlockSpec((block, n), lambda i, s: (i, 0))
    whole = lambda array: pl.BlockSpec(array.shape, lambda i, s: (0, 0), pipeline_mode=pl.Buffered(1))
    shapes = [width + 128, share, 2 * share, codes, codes]
    return pl.pallas_call(
        functools.partial(expert_kernel, size, share),
        grid_spec=pltpu.PrefetchScalarGridSpec(
            num_scalar_prefetch=1,
            grid=(2,),
            in_specs=[ahead(width), ahead(share), ahead(codes), whole(inner_up), whole(inner_down)]
            + [whole(part) for part in inner_parts],
            out_specs=[ahead(n) for n in shapes],
        ),
        out_shape=[jax.ShapeDtypeStruct((rows, n), bf16) for n in shapes],
        compiler_params=pltpu.CompilerParams(vmem_limit_bytes=vmem_bytes),
        cost_estimate=pl.CostEstimate(
            flops=8 * rows * width * share,
            bytes_accessed=4 * width * share + 10 * rows * width,
            transcendentals=rows * share,
        ),
        name="experts",
    )(spot.reshape(1).astype(jnp.int32), got, hidden_grad, mask, inner_up, inner_down, *inner_parts)


def picked(lookup, index):
    return lax.dynamic_index_in_dim(lookup, index, 0, keepdims=False)


def body(
    tokens,
    norm_gain,
    key_value_weight,
    router_weight,
    query_weight,
    output_weight,
    mlp_gain,
    mlp_router_weight,
    mlp_in_weight,
    mlp_out_weight,
    key_value_down,
    key_value_up,
    query_down,
    query_up,
    output_down,
    output_up,
    mlp_in_down,
    mlp_in_up,
    mlp_out_down,
    mlp_out_up,
    routes,
    mlp_routes,
    adapter_index,
    prefix_length,
    out_grad,
):
    seqs, rows, width = tokens.shape
    assert seqs == 1
    size, spot = lax.axis_size("seq"), lax.axis_index("seq")
    holders, holder = lax.axis_size("dp"), lax.axis_index("dp")
    experts = router_weight.shape[1]
    copies = holders // experts
    part = holder % copies
    capacity = 3 * rows // 8
    length = rows * size
    adapters, _, rank = key_value_down.shape
    codes = adapters * rank
    hidden = mlp_in_weight.shape[2] // 2
    share = hidden // size

    def flat_down(lookup):
        return lookup.transpose(0, 2, 1)

    adapter = adapter_index[0]
    adapter_all = exchange(jnp.broadcast_to(adapter_index[None], (holders, 128)))[:, 0]
    inputs = tokens[0].astype(f32)
    input_scale = norm_scale(inputs)
    normed = (inputs * input_scale * norm_gain).astype(bf16)

    gates, hits = gate_pair(nn(normed, router_weight), routes[0])
    place = slot_layout(routes[0], experts, capacity)
    place_any = either(place)
    query_rows = send_full(tn(place_any, normed).astype(bf16), experts, copies)
    query_full = lax.all_gather(query_weight[0], "seq", axis=0, tiled=True)
    block = key_value_weight.shape[1] // holders
    pair_piece = lax.dynamic_slice_in_dim(key_value_weight, holder * block, block, 1)
    packet = jnp.concatenate([normed, pair_piece.reshape(-1, width)], axis=0)
    packets = [packet] + [shifted(packet, d, size) for d in range(1, size)]
    normed_parts = [normed] + [p[:rows] for p in packets[1:]]
    pieces = [pair_piece] + [p[rows:].reshape(-1, block) for p in packets[1:]]
    place_mlp = slot_layout(mlp_routes[0], experts, capacity)
    grad_own = send_full(tn(either(place_mlp), out_grad[0]).astype(bf16), experts, copies)
    pair_own = in_order(pieces, spot)
    pair_own = after(pair_own, query_full, query_rows, grad_own, adapter_all)
    pair_weight = lax.all_gather(pair_own, "dp", axis=0, tiled=False)
    lanes = jnp.pad(mlp_routes[0].astype(bf16), ((0, 0), (0, 126)))
    packet = jnp.concatenate([out_grad[0], lanes], axis=1)
    packet_late = after(packet, query_full)
    early = [packet] + [shifted(packet_late, d, size) for d in range(1, size)]
    grad_parts = [out_grad[0]] + [p[:, :width] for p in early[1:]]
    routes_there = [p[:, width : width + 2].astype(jnp.int32) for p in early]
    outer_full = mlp_out_weight[0]

    pair_down, pair_up = picked(flat_down(key_value_down), adapter), picked(key_value_up, adapter)
    query_lower, query_upper = picked(flat_down(query_down), adapter), picked(query_up, adapter)
    output_lower, output_upper = picked(flat_down(output_down), adapter), picked(output_up, adapter)
    query_low = nt(normed, query_lower).astype(bf16)
    positions = spot * rows + jnp.arange(rows)
    key_pos = (spot * rows + jnp.arange(length)) % length
    cosine_all, sine_all = rope_full(length, spot * rows)
    cosine, sine = cosine_all[:rows], sine_all[:rows]
    allowed = (key_pos[None, :] <= positions[:, None]) | (key_pos[None, :] < prefix_length[0])
    bias = jnp.where(allowed, 0.0, masked_score).astype(f32)

    mask = (jnp.arange(codes)[None, None, :] // rank == adapter_all[:, None, None]).astype(bf16)
    mask = jnp.broadcast_to(mask, (holders, capacity, codes)).reshape(-1, codes)
    inner_down = flat_down(mlp_in_down).reshape(codes, width)
    outer_up = mlp_out_up.reshape(codes, width)
    inner_up = mlp_in_up.reshape(codes, 2, copies, size, share)
    inner_up = lax.dynamic_index_in_dim(inner_up, part, 2, keepdims=False)
    inner_up = lax.dynamic_index_in_dim(inner_up, spot, 2, keepdims=False).reshape(codes, 2 * share)
    outer_down = flat_down(mlp_out_down).reshape(codes, copies, size, share)
    outer_down = lax.dynamic_index_in_dim(outer_down, part, 1, keepdims=False)
    outer_down = lax.dynamic_index_in_dim(outer_down, spot, 1, keepdims=False)

    places = [place_mlp] + [slot_layout(r, experts, capacity) for r in routes_there[1:]]
    query_rows = after(query_rows, *normed_parts[1:])
    query_parts = nn(query_rows.reshape(-1, width), query_full).astype(bf16)
    query_home = home_join(query_parts.reshape(holders, capacity, -1), experts, copies)
    pairs, pair_low = project_pairs(
        normed_parts, pair_weight, pair_down, pair_up, cosine_all, sine_all
    )
    output_own = after(output_weight[0], pair_weight, query_home, *early[1:])
    output_full = lax.all_gather(output_own, "seq", axis=0, tiled=True)
    grad_rows = [grad_own.reshape(-1, width)]
    for d in range(1, size):
        sent = grad_parts[d] if d < 2 else after(grad_parts[d], pairs)
        sent = tn(either(places[d]), sent).astype(bf16)
        grad_rows.append(send_full(sent, experts, copies).reshape(-1, width))
    attended, output_slots, query_rot, totals = attend(
        query_home, place, query_low, query_upper, cosine, sine, pairs, bias
    )

    output_rows = send_cut(output_slots, experts, copies)
    inner_sent = [cut_share(mlp_in_weight[0], (spot - d) % size, size) for d in range(size)]
    output_rows = after(output_rows, *grad_rows[:3], *inner_sent)
    output_parts = nn(output_rows.reshape(holders * capacity, -1), output_full).astype(bf16)
    far = size // 2
    distances = [d for d in range(1, size) if d != far] + ([far] if size > 1 else [])
    inner_parts = list(inner_sent)
    before = output_full
    for d in distances:
        before = inner_parts[d] = shifted(after(inner_sent[d], before), d, size)
    output_home = home_add(output_parts.reshape(holders, capacity, width), experts, copies)
    output_low = nt(attended, output_lower).astype(bf16)
    branch = nn(place, output_home) + nn(output_low, output_upper)
    branch = branch.reshape(2, rows, width)
    middle = inputs + gates[:, :1] * branch[0] + gates[:, 1:] * branch[1]
    middle_scale = norm_scale(middle)
    normed_mlp = (middle * middle_scale * mlp_gain).astype(bf16)
    mlp_gates, mlp_hits = gate_pair(nn(normed_mlp, mlp_router_weight), mlp_routes[0])

    lanes = jnp.pad(jnp.concatenate(halves(mlp_gates), axis=1), ((0, 0), (0, 124)))
    packet = jnp.concatenate([normed_mlp, lanes], axis=1)
    packet = after(packet, *(inner_parts[d] for d in distances[:1]))
    packet_all = lax.all_gather(packet, "seq", axis=0, tiled=True)
    packets = [packet] + [
        lax.dynamic_slice_in_dim(packet_all, (spot + d) % size * rows, rows, 0)
        for d in range(1, size)
    ]
    gates_there = [
        (p[:, width : width + 2].astype(f32) + p[:, width + 2 : width + 4].astype(f32)).T.reshape(-1, 1)
        for p in packets
    ]
    combines = [either((places[d].astype(f32) * gates_there[d]).astype(bf16)) for d in range(size)]
    order = list(range(size))
    outer_codes = [nt(got, outer_up).astype(bf16) * mask for got in grad_rows]
    hidden_grads = [
        (nt(got, outer_full) + nn(code, outer_down)).astype(bf16)
        for got, code in zip(grad_rows, outer_codes)
    ]
    gate_slots = jnp.stack(
        [jnp.sum(places[d].astype(f32) * gates_there[d], axis=0) for d in range(size)]
    )
    gate_slots = gate_slots.reshape(size, experts, capacity).transpose(1, 0, 2)
    gate_slots = exchange(jnp.repeat(gate_slots, copies, axis=0))

    def send_rows(d, *earlier):
        sent = tn(either(places[d]), after(packets[d][:, :width], *earlier)).astype(bf16)
        return send_full(sent, experts, copies).reshape(-1, width)

    def work(d, got):
        return expert_block(got, hidden_grads[d], mask, inner_up, inner_down, inner_parts, spot)

    def rows_home(d, row_grad):
        home = home_add(row_grad.reshape(holders, capacity, -1), experts, copies)
        row_sum = nn(combines[d], home[:, :width])
        gate_sum = nn(places[d], home[:, width:])
        lanes = gate_sum[:rows] + jnp.roll(gate_sum[rows:], 2, axis=1)
        row_back = jnp.concatenate([row_sum, lanes], axis=1)
        return home, shifted(row_back.astype(bf16), -d % size, size) if d else row_back

    got_rows = [send_rows(0)]
    for d in order[1:]:
        earlier = [inner_parts[k] for k in distances[:-1]] if d == 1 else []
        got_rows.append(send_rows(d, got_rows[-1], *earlier))
    kept = [work(0, after(got_rows[0], got_rows[-1]))]
    row_home, row_total = rows_home(0, kept[0][0])
    row_backs, row_homes = [row_total], [row_home]
    for d in order[1:]:
        kept.append(work(d, after(got_rows[d], kept[-1][0])))
        row_grad = kept[d][0]
        if d > 2:
            row_grad = after(row_grad, row_backs[d - 2])
        row_home, row_back = rows_home(d, row_grad)
        row_backs.append(row_back)
        row_homes.append(row_home)
        row_total = row_total + row_back.astype(f32)
    gate_sum = row_total[:, width : width + 4]
    row_total = row_total[:, :width]
    mlp_gate_grad = gate_sum.reshape(rows, 2, 2).sum(2)
    mlp_logit_grad = gate_back(mlp_gates, mlp_hits, mlp_gate_grad)

    outer_lows, sums = [], None
    for d in order:
        _, activated, pre_grad, code, back = kept[d]
        there = row_homes[min(d, size - 2)] if size > 1 else row_homes[0]
        activated, pre_grad = after(activated, there), after(pre_grad, there)
        outer_low = nt(activated, outer_down).astype(bf16) * mask
        outer_lows.append(outer_low)
        scale = gate_slots[:, d, :].reshape(-1, 1)

        def scaled(array):
            return (array.astype(f32) * scale).astype(bf16)

        new = (
            tn(scaled(code), pre_grad),
            tn(scaled(outer_codes[d]), activated),
            tn(scaled(back), got_rows[d]),
            tn(scaled(outer_low), grad_rows[d]),
        )
        sums = new if sums is None else tuple(a + b for a, b in zip(sums, new))


    inner_up_sum, outer_down_sum, inner_down_sum, outer_up_sum = sums

    def widened(array):
        if copies == 1:
            return array
        whole = jnp.zeros((codes, copies, array.shape[1]), f32)
        whole = lax.dynamic_update_index_in_dim(whole, array, part, 1)
        return whole.reshape(codes, -1)

    wide = [widened(inner_up_sum), widened(outer_down_sum), inner_down_sum, outer_up_sum]
    ends = [sum(a.shape[1] for a in wide[: k + 1]) for k in range(3)]
    mlp_own = after(jnp.concatenate(wide, axis=1).astype(bf16), row_home)
    mlp_sums = lax.psum_scatter(mlp_own, "dp", scatter_dimension=0, tiled=True)

    def down_back(d, before_matmul, before_sending):
        activated = after(kept[d][1], before_matmul)
        down = (nn(activated, outer_full) + nn(outer_lows[d], outer_up)).astype(bf16)
        down = after(down, before_sending).reshape(holders, capacity, width)
        home = home_add(down, experts, copies)
        made = nn(combines[d], home)
        return home, shifted(made.astype(bf16), -d % size, size).astype(f32) if d else made

    down_turns = order[1:] + [0]
    down_home, down_total = down_back(down_turns[0], row_homes[-2], row_home)

    normed_mlp_grad = row_total + nt(mlp_logit_grad.astype(bf16), mlp_router_weight)
    middle_grad = norm_back(middle, middle_scale, mlp_gain, normed_mlp_grad)
    middle_grad = middle_grad + out_grad[0].astype(f32)
    middle_low = middle_grad.astype(bf16)
    branch_sent = tn(place_any, after(middle_low, down_home)).astype(bf16)
    branch_rows = send_full(branch_sent, experts, copies)
    mlp_sums = lax.all_gather(after(mlp_sums, branch_rows), ("seq", "dp"), axis=0, tiled=True)
    if copies == 1 and share % 128 == 0:
        inner_up_grad, outer_down_grad, inner_down_grad, outer_up_grad = unpack_sums(
            mlp_sums.reshape(size, adapters, rank, -1), share, width
        )
    else:
        mlp_sums = mlp_sums.astype(f32).reshape(size, codes, -1)
        inner_up_grad, outer_down_grad, inner_down_grad, outer_up_grad = jnp.split(mlp_sums, ends, axis=2)
        inner_up_grad = inner_up_grad.reshape(size, codes, copies, 2, share).transpose(1, 3, 2, 0, 4)
        inner_up_grad = inner_up_grad.reshape(adapters, rank, -1)
        outer_down_grad = outer_down_grad.reshape(size, codes, copies, share).transpose(1, 2, 0, 3)
        outer_down_grad = outer_down_grad.reshape(adapters, rank, -1)
        inner_down_grad = jnp.sum(inner_down_grad, 0).reshape(adapters, rank, width)
        outer_up_grad = jnp.sum(outer_up_grad, 0).reshape(adapters, rank, width)
    head_parts = nt(branch_rows.reshape(-1, width), output_full).astype(bf16)
    head_home = home_join(head_parts.reshape(holders, capacity, -1), experts, copies)
    down_home, made = down_back(down_turns[1], head_parts, head_home)
    down_total = down_total + made
    head_home = after(head_home, mlp_own)
    gate_grad = jnp.sum(middle_grad[None] * branch, axis=2).T
    logit_grad = gate_back(gates, hits, gate_grad)
    gate_column = gates.T.reshape(-1, 1)
    output_low_grad = nt(middle_low, output_upper)
    output_low_back = output_low_grad.astype(bf16)
    output_low_scaled = (jnp.tile(output_low_grad, (2, 1)) * gate_column).astype(bf16)
    output_lower_grad = tn(output_low_scaled, attended)
    output_low_sum = (output_low.astype(f32) * gate_column).reshape(2, rows, rank).sum(0)
    output_upper_grad = tn(output_low_sum.astype(bf16), middle_low)

    def own_part(arrays):
        joined = [a.reshape(rank, size, -1) for a in arrays]
        joined = jnp.concatenate(joined, axis=2).transpose(1, 0, 2)
        mine = picked(joined, spot)
        for d in range(1, size):
            theirs = picked(joined, (spot + d) % size).astype(bf16)
            mine = mine + shifted(theirs, -d % size, size).astype(f32)
        return joined, mine.astype(bf16)

    def over_sequences(mine, widths):
        every = lax.all_gather(mine, ("seq", "dp"), axis=0, tiled=False)
        every = every.reshape(size, holders, rank, -1)
        return gather_adapters(every, adapter_all, adapters, widths)

    key_grad, value_grad, query_slots, query_sum = attend_back(
        query_rot,
        pairs,
        bias,
        totals,
        head_home,
        place,
        gate_column,
        output_low_back,
        output_lower,
        cosine,
        sine,
        cosine_all,
        sine_all,
    )
    query_back = send_cut(after(query_slots, down_home), experts, copies)
    half = key_grad.shape[1]
    pair_low_grad = nt(key_grad, pair_up[:, :half]) + nt(value_grad, pair_up[:, half:])
    pair_low_grad = pair_low_grad.astype(bf16)
    pair_upper_grad = jnp.concatenate([tn(pair_low, key_grad), tn(pair_low, value_grad)], axis=1)
    pair_lower_grad = sum(
        tn(pair_low_grad[d * rows : (d + 1) * rows], normed_parts[d]) for d in range(size)
    )
    query_low_grad = nt(query_sum, query_upper).astype(bf16)
    query_upper_grad = tn(query_low, query_sum)
    query_lower_grad = tn(query_low_grad, normed)
    sequence_grads = [
        pair_lower_grad,
        pair_upper_grad,
        query_lower_grad,
        query_upper_grad,
        output_lower_grad,
        output_upper_grad,
    ]
    joined, mine = own_part(sequence_grads)
    normed_grads = pair_back(
        after(key_grad, joined), value_grad, pair_weight, pair_low_grad, pair_down
    )
    mine = after(mine, mlp_sums, normed_grads)
    late = over_sequences(mine, [a.shape[1] for a in sequence_grads])
    back_parts = [
        shifted(normed_grads[d * rows : (d + 1) * rows], -d % size, size) for d in range(1, size)
    ]
    normed_grad = normed_grads[:rows].astype(f32) + sum(back.astype(f32) for back in back_parts)
    input_parts = nt(query_back.reshape(holders * capacity, -1), query_full).astype(bf16)
    input_home = home_add(input_parts.reshape(holders, capacity, width), experts, copies)
    input_home = after(input_home, inner_up_grad)
    normed_grad = normed_grad + nn(place_any, input_home) + nn(query_low_grad, query_lower)
    normed_grad = normed_grad + nt(logit_grad.astype(bf16), router_weight)
    input_grad = norm_back(inputs, input_scale, norm_gain, normed_grad) + middle_grad

    for d in down_turns[2:]:
        down_home, made = down_back(d, query_slots, input_home)
        down_total = down_total + made
    result = (middle + down_total).astype(bf16)

    return (
        result[None],
        input_grad[None],
        flat_down(late[0]),
        late[1],
        flat_down(late[2]),
        late[3],
        flat_down(late[4]),
        late[5],
        flat_down(inner_down_grad),
        inner_up_grad,
        flat_down(outer_down_grad),
        outer_up_grad,
    )


def solution(mesh):
    split = P("dp", "seq", None)
    placed = (
        (split, P(), P("seq", None), P(), split, split, P(), P(), split, split)
        + (P(),) * 10
        + (split, split, P("dp"), P("dp"), split)
    )
    return jax.shard_map(
        body,
        mesh=mesh,
        in_specs=placed,
        out_specs=(split, split) + (P(),) * 10,
        check_vma=False,
    )
```

```python
import functools
import math

import jax
import jax.numpy as jnp
import numpy as np
from jax import lax
from jax.experimental import pallas as pl
from jax.experimental.pallas import tpu as pltpu
from jax.sharding import PartitionSpec as P

KV_HEADS = 16
HD = 128

norm_eps = 1e-05
rope_base = 10000.0
masked_score = -1e30
vmem_bytes = 48 * 2**20

bf16 = jnp.bfloat16
f32 = jnp.float32


def product(left, right, left_dim, right_dim):
    return lax.dot_general(
        left, right, (((left_dim,), (right_dim,)), ((), ())), preferred_element_type=f32
    )


def nn(left, right):
    return product(left, right, 1, 0)


def nt(left, right):
    return product(left, right, 1, 1)


def tn(left, right):
    return product(left, right, 0, 0)


def pair_kernel(count, key_blocks, *refs):
    normed_refs = refs[:count]
    w_ref, down_ref, up_ref, cos_ref, sin_ref, out_ref, low_ref = refs[count:]
    rows = normed_refs[0].shape[0]
    step = pl.program_id(0)

    @pl.when(step == 0)
    def _():
        for k in range(count):
            low_ref[pl.ds(k * rows, rows), :] = nt(normed_refs[k][...], down_ref[...]).astype(bf16)

    for k in range(count):
        part = pl.ds(k * rows, rows)
        made = nn(normed_refs[k][...], w_ref[0]) + nn(low_ref[part, :], up_ref[...])

        @pl.when(step < key_blocks)
        def _():
            for start in range(0, made.shape[1], HD):
                head = made[:, start : start + HD]
                turned = head * cos_ref[part, :] + pltpu.roll(head, HD // 2, 1) * sin_ref[part, :]
                out_ref[part, start : start + HD] = turned.astype(bf16)

        @pl.when(step >= key_blocks)
        def _():
            out_ref[part, :] = made.astype(bf16)


def project_pairs(normed_parts, weight, down, upper, cosine, sine):
    count = len(normed_parts)
    rows, width = normed_parts[0].shape
    blocks, _, block = weight.shape
    columns = blocks * block
    whole = lambda array: pl.BlockSpec(array.shape, lambda i: (0, 0))
    return pl.pallas_call(
        functools.partial(pair_kernel, count, blocks // 2),
        grid=(blocks,),
        in_specs=[whole(n) for n in normed_parts]
        + [
            pl.BlockSpec((1, width, block), lambda i: (i, 0, 0)),
            whole(down),
            pl.BlockSpec((upper.shape[0], block), lambda i: (0, i)),
            whole(cosine),
            whole(sine),
        ],
        out_specs=[
            pl.BlockSpec((count * rows, block), lambda i: (0, i)),
            pl.BlockSpec((count * rows, down.shape[0]), lambda i: (0, 0)),
        ],
        out_shape=[
            jax.ShapeDtypeStruct((count * rows, columns), bf16),
            jax.ShapeDtypeStruct((count * rows, down.shape[0]), bf16),
        ],
        compiler_params=pltpu.CompilerParams(vmem_limit_bytes=vmem_bytes),
        cost_estimate=pl.CostEstimate(
            flops=2 * count * rows * width * columns,
            bytes_accessed=2 * width * columns,
            transcendentals=0,
        ),
        name="pairs",
    )(*normed_parts, weight, down, upper, cosine, sine)


def pair_back_kernel(key_blocks, key_ref, value_ref, w_ref, low_ref, down_ref, out_ref, sum_ref):
    step = pl.program_id(0)

    @pl.when(step == 0)
    def _():
        sum_ref[...] = nn(low_ref[...], down_ref[...])

    @pl.when(step < key_blocks)
    def _():
        sum_ref[...] += nt(key_ref[...], w_ref[0])

    @pl.when(step >= key_blocks)
    def _():
        sum_ref[...] += nt(value_ref[...], w_ref[0])

    @pl.when(step == pl.num_programs(0) - 1)
    def _():
        out_ref[...] = sum_ref[...].astype(bf16)


def pair_back(key_grad, value_grad, weight, low_grad, down):
    blocks, width, block = weight.shape
    rows = key_grad.shape[0]
    half = blocks // 2
    whole = lambda array: pl.BlockSpec(array.shape, lambda i: (0, 0))
    return pl.pallas_call(
        functools.partial(pair_back_kernel, half),
        grid=(blocks,),
        in_specs=[
            pl.BlockSpec((rows, block), lambda i: (0, jnp.minimum(i, half - 1))),
            pl.BlockSpec((rows, block), lambda i: (0, jnp.maximum(i - half, 0))),
            pl.BlockSpec((1, width, block), lambda i: (i, 0, 0)),
            whole(low_grad),
            whole(down),
        ],
        out_specs=pl.BlockSpec((rows, width), lambda i: (0, 0)),
        out_shape=jax.ShapeDtypeStruct((rows, width), bf16),
        scratch_shapes=[pltpu.VMEM((rows, width), f32)],
        compiler_params=pltpu.CompilerParams(vmem_limit_bytes=vmem_bytes),
        cost_estimate=pl.CostEstimate(
            flops=2 * rows * width * blocks * block,
            bytes_accessed=2 * width * blocks * block,
            transcendentals=0,
        ),
        name="pair_back",
    )(key_grad, value_grad, weight, low_grad, down)


def attend_kernel(
    scale,
    home_ref,
    place_ref,
    low_ref,
    up_ref,
    cos_ref,
    sin_ref,
    key_ref,
    value_ref,
    bias_ref,
    attended_ref,
    slots_ref,
    query_ref,
    total_ref,
):
    rows = cos_ref.shape[0]
    base = nn(place_ref[...], home_ref[...])
    extra = nn(low_ref[...], up_ref[...])
    keys, values = key_ref[...], value_ref[...]
    for route in range(2):
        part = pl.ds(route * rows, rows)
        query = base[route * rows : (route + 1) * rows] + extra
        query = query * cos_ref[...] + pltpu.roll(query, HD // 2, 1) * sin_ref[...]
        query = query.astype(bf16)
        query_ref[part, :] = query
        scores = nt(query, keys) * scale + bias_ref[...]
        highest = jnp.max(scores, axis=1, keepdims=True)
        weights = jnp.exp(scores - highest)
        total = jnp.sum(weights, axis=1, keepdims=True)
        attended = nn(weights.astype(bf16), values) / total
        attended_ref[part, :] = attended.astype(bf16)
        total_ref[0, part, :] = highest + jnp.log(total)
    slots_ref[...] = tn(place_ref[...], attended_ref[...]).astype(bf16)


def attend(home, place, low, upper, cosine, sine, pairs, bias):
    rows2, slots = place.shape
    rows, length = bias.shape
    heads = home.shape[1] // HD
    kv_heads = pairs.shape[1] // (2 * HD)
    whole = lambda array: pl.BlockSpec(array.shape, lambda h: (0, 0))
    return pl.pallas_call(
        functools.partial(attend_kernel, 1.0 / math.sqrt(HD)),
        grid=(heads,),
        in_specs=[
            pl.BlockSpec((slots, HD), lambda h: (0, h)),
            whole(place),
            whole(low),
            pl.BlockSpec((upper.shape[0], HD), lambda h: (0, h)),
            whole(cosine),
            whole(sine),
            pl.BlockSpec((length, HD), lambda h: (0, h)),
            pl.BlockSpec((length, HD), lambda h: (0, kv_heads + h)),
            whole(bias),
        ],
        out_specs=[
            pl.BlockSpec((rows2, HD), lambda h: (0, h)),
            pl.BlockSpec((slots, HD), lambda h: (0, h)),
            pl.BlockSpec((rows2, HD), lambda h: (0, h)),
            pl.BlockSpec((1, rows2, 1), lambda h: (h, 0, 0)),
        ],
        out_shape=[
            jax.ShapeDtypeStruct((rows2, heads * HD), bf16),
            jax.ShapeDtypeStruct((slots, heads * HD), bf16),
            jax.ShapeDtypeStruct((rows2, heads * HD), bf16),
            jax.ShapeDtypeStruct((heads, rows2, 1), f32),
        ],
        compiler_params=pltpu.CompilerParams(vmem_limit_bytes=vmem_bytes),
        cost_estimate=pl.CostEstimate(
            flops=4 * heads * rows2 * length * HD,
            bytes_accessed=4 * length * heads * HD,
            transcendentals=heads * rows2 * length,
        ),
        name="attend",
    )(home, place, low, upper, cosine, sine, pairs, pairs, bias)


def attend_back_kernel(
    scale,
    query_ref,
    key_ref,
    value_ref,
    bias_ref,
    total_ref,
    home_ref,
    place_ref,
    gate_ref,
    low_ref,
    down_ref,
    cos_ref,
    sin_ref,
    cos_all_ref,
    sin_all_ref,
    key_grad_ref,
    value_grad_ref,
    slots_ref,
    sum_ref,
    turned_ref,
):
    rows = cos_ref.shape[0]
    base = nn(place_ref[...], home_ref[...])
    extra = nn(low_ref[...], down_ref[...])
    keys, values = key_ref[...], value_ref[...]
    key_grad = value_grad = None
    for route in range(2):
        part = pl.ds(route * rows, rows)
        query = query_ref[part, :]
        grad = (base[route * rows : (route + 1) * rows] + extra) * gate_ref[part, :]
        grad = grad.astype(bf16)
        scores = nt(query, keys) * scale + bias_ref[...]
        weights = jnp.exp(scores - total_ref[0, part, :])
        weight_grad = nt(grad, values)
        mean_grad = jnp.sum(weights * weight_grad, axis=1, keepdims=True)
        score_grad = (weights * (weight_grad - mean_grad)).astype(bf16)
        query_grad = nn(score_grad, keys) * scale
        query_grad = query_grad * cos_ref[...] - pltpu.roll(query_grad, HD // 2, 1) * sin_ref[...]
        turned_ref[part, :] = query_grad.astype(bf16)
        key_part = tn(score_grad, query)
        value_part = tn(weights.astype(bf16), grad)
        key_grad = key_part if route == 0 else key_grad + key_part
        value_grad = value_part if route == 0 else value_grad + value_part
    key_grad = key_grad * scale
    key_grad = key_grad * cos_all_ref[...] - pltpu.roll(key_grad, HD // 2, 1) * sin_all_ref[...]
    key_grad_ref[...] = key_grad.astype(bf16)
    value_grad_ref[...] = value_grad.astype(bf16)
    slots_ref[...] = tn(place_ref[...], turned_ref[...]).astype(bf16)
    first = turned_ref[pl.ds(0, rows), :].astype(f32)
    sum_ref[...] = (first + turned_ref[pl.ds(rows, rows), :].astype(f32)).astype(bf16)


def attend_back(query, pairs, bias, totals, home, place, gates, low, down, cosine, sine, cosine_all, sine_all):
    rows2, slots = place.shape
    rows, length = bias.shape
    heads = home.shape[1] // HD
    kv_heads = pairs.shape[1] // (2 * HD)
    whole = lambda array: pl.BlockSpec(array.shape, lambda h: (0, 0))
    return pl.pallas_call(
        functools.partial(attend_back_kernel, 1.0 / math.sqrt(HD)),
        grid=(heads,),
        in_specs=[
            pl.BlockSpec((rows2, HD), lambda h: (0, h)),
            pl.BlockSpec((length, HD), lambda h: (0, h)),
            pl.BlockSpec((length, HD), lambda h: (0, kv_heads + h)),
            whole(bias),
            pl.BlockSpec((1, rows2, 1), lambda h: (h, 0, 0)),
            pl.BlockSpec((slots, HD), lambda h: (0, h)),
            whole(place),
            whole(gates),
            whole(low),
            pl.BlockSpec((down.shape[0], HD), lambda h: (0, h)),
            whole(cosine),
            whole(sine),
            whole(cosine_all),
            whole(sine_all),
        ],
        out_specs=[
            pl.BlockSpec((length, HD), lambda h: (0, h)),
            pl.BlockSpec((length, HD), lambda h: (0, h)),
            pl.BlockSpec((slots, HD), lambda h: (0, h)),
            pl.BlockSpec((rows, HD), lambda h: (0, h)),
        ],
        out_shape=[
            jax.ShapeDtypeStruct((length, heads * HD), bf16),
            jax.ShapeDtypeStruct((length, heads * HD), bf16),
            jax.ShapeDtypeStruct((slots, heads * HD), bf16),
            jax.ShapeDtypeStruct((rows, heads * HD), bf16),
        ],
        scratch_shapes=[pltpu.VMEM((rows2, HD), bf16)],
        compiler_params=pltpu.CompilerParams(vmem_limit_bytes=vmem_bytes),
        cost_estimate=pl.CostEstimate(
            flops=10 * heads * rows2 * length * HD,
            bytes_accessed=8 * length * heads * HD,
            transcendentals=heads * rows2 * length,
        ),
        name="attend_back",
    )(query, pairs, pairs, bias, totals, home, place, gates, low, down, cosine, sine, cosine_all, sine_all)


def exchange(buffer):
    return lax.all_to_all(buffer, "dp", split_axis=0, concat_axis=0, tiled=True)


def in_order(parts, spot):
    count = len(parts)
    twice = jnp.concatenate(parts + parts, axis=0)
    rows = parts[0].shape[0]
    return lax.dynamic_slice_in_dim(twice, (count - spot) % count * rows, count * rows, 0)


def shifted(array, shift, size):
    if shift == 0:
        return array
    return lax.ppermute(array, "seq", [(k, (k - shift) % size) for k in range(size)])


def send_full(slots, experts, copies):
    buffer = slots.reshape(experts, slots.shape[0] // experts, slots.shape[1])
    if copies > 1:
        buffer = jnp.repeat(buffer, copies, axis=0)
    return exchange(buffer)


def send_cut(slots, experts, copies):
    buffer = slots.reshape(experts, slots.shape[0] // experts, slots.shape[1])
    if copies > 1:
        _, rows, columns = buffer.shape
        buffer = buffer.reshape(experts, rows, copies, columns // copies).transpose(0, 2, 1, 3)
        buffer = buffer.reshape(experts * copies, rows, columns // copies)
    return exchange(buffer)


def home_join(parts, experts, copies):
    home = exchange(parts)
    _, rows, columns = home.shape
    if copies > 1:
        home = home.reshape(experts, copies, rows, columns).transpose(0, 2, 1, 3)
    return home.reshape(experts * rows, copies * columns)


def home_add(parts, experts, copies):
    home = exchange(parts)
    _, rows, columns = home.shape
    if copies > 1:
        home = home.reshape(experts, copies, rows, columns).astype(f32)
        home = jnp.sum(home, axis=1).astype(parts.dtype)
    return home.reshape(experts * rows, columns)


def slot_layout(route_ids, experts, capacity):
    flat = route_ids.T.reshape(-1)
    count = flat.shape[0]
    hits = flat[:, None] == jnp.arange(experts)[None, :]
    earlier = jnp.arange(count)[:, None] > jnp.arange(count)[None, :]
    before = nn(earlier.astype(bf16), hits.astype(bf16))
    rank = jnp.sum(jnp.where(hits, before, 0.0), axis=1).astype(jnp.int32)
    slot = flat * capacity + rank
    return (slot[:, None] == jnp.arange(experts * capacity)[None, :]).astype(bf16)


def either(place):
    rows = place.shape[0] // 2
    return place[:rows] + place[rows:]


def norm_back(values, scale, gain, grad):
    weighted = grad * gain
    mean = jnp.mean(weighted * values, axis=-1, keepdims=True)
    return weighted * scale - values * (scale * scale * scale * mean)


def norm_scale(values):
    return lax.rsqrt(jnp.mean(values * values, axis=-1, keepdims=True) + norm_eps)


def gate_pair(logits, route_ids):
    hits = (route_ids[:, :, None] == jnp.arange(logits.shape[1])).astype(f32)
    chosen = jnp.sum(hits * logits[:, None, :], axis=2)
    weights = jnp.exp(chosen - jnp.max(chosen, axis=1, keepdims=True))
    return weights / jnp.sum(weights, axis=1, keepdims=True), hits


def gate_back(gates, hits, grad):
    mean = jnp.sum(gates * grad, axis=1, keepdims=True)
    return jnp.sum((gates * (grad - mean))[:, :, None] * hits, axis=1)


def rope_full(length, start):
    half = HD // 2
    frequency = rope_base ** (-np.arange(half) / half)
    angles = np.arange(length)[:, None] * frequency[None, :]
    cosine, sine = np.cos(angles), np.sin(angles)
    tables = np.concatenate([cosine, cosine, -sine, sine], 1).astype(np.float32)
    tables = jnp.asarray(np.concatenate([tables, tables], 0))
    tables = lax.dynamic_slice_in_dim(tables, start, length, 0)
    return tables[:, :HD], tables[:, HD:]


def after(array, *earlier):
    return lax.optimization_barrier((array,) + earlier)[0]


def cut_kernel(target_ref, in_ref, out_ref):
    out_ref[...] = in_ref[...]


def cut_share(weight, target, size):
    rows, columns = weight.shape
    share = columns // 2 // size
    if share % 128:
        cut = weight.reshape(rows, 2, size, share)
        return lax.dynamic_index_in_dim(cut, target, 2, keepdims=False).reshape(rows, 2 * share)
    return pl.pallas_call(
        cut_kernel,
        grid_spec=pltpu.PrefetchScalarGridSpec(
            num_scalar_prefetch=1,
            grid=(2,),
            in_specs=[pl.BlockSpec((rows, share), lambda i, t: (0, i * size + t[0]))],
            out_specs=pl.BlockSpec((rows, share), lambda i, t: (0, i)),
        ),
        out_shape=jax.ShapeDtypeStruct((rows, 2 * share), bf16),
        compiler_params=pltpu.CompilerParams(vmem_limit_bytes=vmem_bytes),
        name="cut",
    )(target.reshape(1).astype(jnp.int32), weight)


def unpack_kernel(size, share, in_ref, inner_up_ref, outer_down_ref, inner_down_ref, outer_up_ref):
    spot = pl.program_id(1)
    got = in_ref[0, 0].astype(f32)
    hidden = size * share
    width = inner_down_ref.shape[2]
    start = pl.multiple_of(spot * share, 128)
    inner_up_ref[0, :, pl.ds(start, share)] = got[:, :share]
    inner_up_ref[0, :, pl.ds(pl.multiple_of(hidden + start, 128), share)] = got[:, share : 2 * share]
    outer_down_ref[0, :, pl.ds(start, share)] = got[:, 2 * share : 3 * share]
    inner_down = got[:, 3 * share : 3 * share + width]
    outer_up = got[:, 3 * share + width :]

    @pl.when(spot == 0)
    def _():
        inner_down_ref[0] = inner_down
        outer_up_ref[0] = outer_up

    @pl.when(spot > 0)
    def _():
        inner_down_ref[0] += inner_down
        outer_up_ref[0] += outer_up


def unpack_sums(sums, share, width):
    size, adapters, rank, columns = sums.shape
    hidden = size * share
    shapes = [2 * hidden, hidden, width, width]
    return pl.pallas_call(
        functools.partial(unpack_kernel, size, share),
        grid=(adapters, size),
        in_specs=[pl.BlockSpec((1, 1, rank, columns), lambda a, k: (k, a, 0, 0))],
        out_specs=[pl.BlockSpec((1, rank, n), lambda a, k: (a, 0, 0)) for n in shapes],
        out_shape=[jax.ShapeDtypeStruct((adapters, rank, n), f32) for n in shapes],
        compiler_params=pltpu.CompilerParams(vmem_limit_bytes=vmem_bytes),
        cost_estimate=pl.CostEstimate(
            flops=0, bytes_accessed=12 * adapters * rank * (3 * hidden + 2 * width), transcendentals=0
        ),
        name="unpack",
    )(sums)


def gather_adapters_kernel(adapters, ids_ref, in_ref, *out_refs):
    holders = in_ref.shape[1]
    start = 0
    for out_ref in out_refs:
        columns = out_ref.shape[2]
        parts = [in_ref[0, k, :, start : start + columns].astype(f32) for k in range(holders)]
        for a in range(adapters):
            total = None
            for k in range(holders):
                one = jnp.where(ids_ref[k] == a, parts[k], 0.0)
                total = one if total is None else total + one
            out_ref[a] = total
        start += columns


def gather_adapters(every, adapter_all, adapters, widths):
    size, holders, rank, columns = every.shape
    return pl.pallas_call(
        functools.partial(gather_adapters_kernel, adapters),
        grid_spec=pltpu.PrefetchScalarGridSpec(
            num_scalar_prefetch=1,
            grid=(size,),
            in_specs=[pl.BlockSpec((1, holders, rank, columns), lambda k, s: (k, 0, 0, 0))],
            out_specs=[
                pl.BlockSpec((adapters, rank, n // size), lambda k, s: (0, 0, k)) for n in widths
            ],
        ),
        out_shape=[jax.ShapeDtypeStruct((adapters, rank, n), f32) for n in widths],
        compiler_params=pltpu.CompilerParams(vmem_limit_bytes=vmem_bytes),
        name="gather_adapters",
    )(adapter_all, every)


def silu_parts(gate_part, up_part, hidden_grad):
    sigmoid = 1.0 / (1.0 + jnp.exp(-gate_part))
    active = gate_part * sigmoid
    activated = (active * up_part).astype(bf16)
    gate_grad = hidden_grad * up_part * sigmoid * (1.0 + gate_part * (1.0 - sigmoid))
    return activated, gate_grad.astype(bf16), (hidden_grad * active).astype(bf16)


def halves(value):
    high = value.astype(bf16)
    return high, (value - high.astype(f32)).astype(bf16)


def expert_kernel(size, share, spot_ref, x_ref, hidden_ref, mask_ref, up_ref, down_ref, *refs):
    w_refs = refs[:size]
    row_ref, active_ref, pre_ref, code_ref, back_ref = refs[size:]
    depth = w_refs[0].shape[0]
    width = size * depth
    columns = [pl.ds(pl.multiple_of((spot_ref[0] + k) % size * depth, 128), depth) for k in range(size)]
    code = nt(x_ref[...], down_ref[...]).astype(bf16) * mask_ref[...]
    code_ref[...] = code
    sums = None
    for start in range(0, share, 256):
        end = min(start + 256, share)

        def hidden(first, last):
            made = nn(code, up_ref[:, first:last])
            for k in range(size):
                made = made + nn(x_ref[:, columns[k]], w_refs[k][:, first:last])
            return made

        gate_part, up_part = hidden(start, end), hidden(share + start, share + end)
        hidden_grad = hidden_ref[:, start:end].astype(f32)
        activated, gate_grad, up_grad = silu_parts(gate_part, up_part, hidden_grad)
        active_ref[:, start:end] = activated
        pre_ref[:, start:end] = gate_grad
        pre_ref[:, share + start : share + end] = up_grad
        part = jnp.sum(activated.astype(f32) * hidden_grad, axis=1, keepdims=True)
        sums = part if sums is None else sums + part
    back = nt(pre_ref[...], up_ref[...]).astype(bf16) * mask_ref[...]
    back_ref[...] = back
    for k in range(size):
        base = (spot_ref[0] + k) % size * depth
        for start in range(0, depth, 256):
            end = min(start + 256, depth)
            here = pl.ds(pl.multiple_of(base + start, 128), end - start)
            made = nt(pre_ref[...], w_refs[k][start:end, :]) + nn(back, down_ref[:, here])
            row_ref[:, here] = made.astype(bf16)
    high, low = halves(sums)
    lane = lax.broadcasted_iota(jnp.int32, (sums.shape[0], 128), 1)
    packed = jnp.where(lane == 0, high.astype(f32), jnp.where(lane == 1, low.astype(f32), 0.0))
    row_ref[:, width:] = packed.astype(bf16)


def expert_block(got, hidden_grad, mask, inner_up, inner_down, inner_parts, spot):
    size = len(inner_parts)
    rows, width = got.shape
    share = hidden_grad.shape[1]
    codes = mask.shape[1]
    if share % 128 or width // size % 256:
        code = nt(got, inner_down).astype(bf16) * mask
        inner_full = in_order(inner_parts, spot)
        pre = nn(got, inner_full) + nn(code, inner_up)
        hidden_float = hidden_grad.astype(f32)
        activated, gate_grad, up_grad = silu_parts(pre[:, :share], pre[:, share:], hidden_float)
        pre_grad = jnp.concatenate([gate_grad, up_grad], axis=1)
        back = nt(pre_grad, inner_up).astype(bf16) * mask
        row_grad = (nt(pre_grad, inner_full) + nn(back, inner_down)).astype(bf16)
        sums = jnp.stack(halves(jnp.sum(activated.astype(f32) * hidden_float, axis=1)), axis=1)
        row_grad = jnp.concatenate([row_grad, jnp.pad(sums, ((0, 0), (0, 126)))], axis=1)
        return row_grad, activated, pre_grad, code, back
    block = rows // 2
    ahead = lambda n: pl.BlockSpec((block, n), lambda i, s: (i, 0))
    whole = lambda array: pl.BlockSpec(array.shape, lambda i, s: (0, 0), pipeline_mode=pl.Buffered(1))
    shapes = [width + 128, share, 2 * share, codes, codes]
    return pl.pallas_call(
        functools.partial(expert_kernel, size, share),
        grid_spec=pltpu.PrefetchScalarGridSpec(
            num_scalar_prefetch=1,
            grid=(2,),
            in_specs=[ahead(width), ahead(share), ahead(codes), whole(inner_up), whole(inner_down)]
            + [whole(part) for part in inner_parts],
            out_specs=[ahead(n) for n in shapes],
        ),
        out_shape=[jax.ShapeDtypeStruct((rows, n), bf16) for n in shapes],
        compiler_params=pltpu.CompilerParams(vmem_limit_bytes=vmem_bytes),
        cost_estimate=pl.CostEstimate(
            flops=8 * rows * width * share,
            bytes_accessed=4 * width * share + 10 * rows * width,
            transcendentals=rows * share,
        ),
        name="experts",
    )(spot.reshape(1).astype(jnp.int32), got, hidden_grad, mask, inner_up, inner_down, *inner_parts)


def picked(lookup, index):
    return lax.dynamic_index_in_dim(lookup, index, 0, keepdims=False)


def body(
    tokens,
    norm_gain,
    key_value_weight,
    router_weight,
    query_weight,
    output_weight,
    mlp_gain,
    mlp_router_weight,
    mlp_in_weight,
    mlp_out_weight,
    key_value_down,
    key_value_up,
    query_down,
    query_up,
    output_down,
    output_up,
    mlp_in_down,
    mlp_in_up,
    mlp_out_down,
    mlp_out_up,
    routes,
    mlp_routes,
    adapter_index,
    prefix_length,
    out_grad,
):
    seqs, rows, width = tokens.shape
    assert seqs == 1
    size, spot = lax.axis_size("seq"), lax.axis_index("seq")
    holders, holder = lax.axis_size("dp"), lax.axis_index("dp")
    experts = router_weight.shape[1]
    copies = holders // experts
    part = holder % copies
    capacity = 3 * rows // 8
    length = rows * size
    adapters, _, rank = key_value_down.shape
    codes = adapters * rank
    hidden = mlp_in_weight.shape[2] // 2
    share = hidden // size

    def flat_down(lookup):
        return lookup.transpose(0, 2, 1)

    adapter = adapter_index[0]
    adapter_all = exchange(jnp.broadcast_to(adapter_index[None], (holders, 128)))[:, 0]
    inputs = tokens[0].astype(f32)
    input_scale = norm_scale(inputs)
    normed = (inputs * input_scale * norm_gain).astype(bf16)

    gates, hits = gate_pair(nn(normed, router_weight), routes[0])
    place = slot_layout(routes[0], experts, capacity)
    place_any = either(place)
    query_rows = send_full(tn(place_any, normed).astype(bf16), experts, copies)
    query_full = lax.all_gather(query_weight[0], "seq", axis=0, tiled=True)
    block = key_value_weight.shape[1] // holders
    pair_piece = lax.dynamic_slice_in_dim(key_value_weight, holder * block, block, 1)
    packet = jnp.concatenate([normed, pair_piece.reshape(-1, width)], axis=0)
    packets = [packet] + [shifted(packet, d, size) for d in range(1, size)]
    normed_parts = [normed] + [p[:rows] for p in packets[1:]]
    pieces = [pair_piece] + [p[rows:].reshape(-1, block) for p in packets[1:]]
    place_mlp = slot_layout(mlp_routes[0], experts, capacity)
    grad_own = send_full(tn(either(place_mlp), out_grad[0]).astype(bf16), experts, copies)
    pair_own = in_order(pieces, spot)
    pair_own = after(pair_own, query_full, query_rows, grad_own, adapter_all)
    pair_weight = lax.all_gather(pair_own, "dp", axis=0, tiled=False)
    lanes = jnp.pad(mlp_routes[0].astype(bf16), ((0, 0), (0, 126)))
    packet = jnp.concatenate([out_grad[0], lanes], axis=1)
    packet_late = after(packet, query_full)
    early = [packet] + [shifted(packet_late, d, size) for d in range(1, size)]
    grad_parts = [out_grad[0]] + [p[:, :width] for p in early[1:]]
    routes_there = [p[:, width : width + 2].astype(jnp.int32) for p in early]
    outer_full = mlp_out_weight[0]

    pair_down, pair_up = picked(flat_down(key_value_down), adapter), picked(key_value_up, adapter)
    query_lower, query_upper = picked(flat_down(query_down), adapter), picked(query_up, adapter)
    output_lower, output_upper = picked(flat_down(output_down), adapter), picked(output_up, adapter)
    query_low = nt(normed, query_lower).astype(bf16)
    positions = spot * rows + jnp.arange(rows)
    key_pos = (spot * rows + jnp.arange(length)) % length
    cosine_all, sine_all = rope_full(length, spot * rows)
    cosine, sine = cosine_all[:rows], sine_all[:rows]
    allowed = (key_pos[None, :] <= positions[:, None]) | (key_pos[None, :] < prefix_length[0])
    bias = jnp.where(allowed, 0.0, masked_score).astype(f32)

    mask = (jnp.arange(codes)[None, None, :] // rank == adapter_all[:, None, None]).astype(bf16)
    mask = jnp.broadcast_to(mask, (holders, capacity, codes)).reshape(-1, codes)
    inner_down = flat_down(mlp_in_down).reshape(codes, width)
    outer_up = mlp_out_up.reshape(codes, width)
    inner_up = mlp_in_up.reshape(codes, 2, copies, size, share)
    inner_up = lax.dynamic_index_in_dim(inner_up, part, 2, keepdims=False)
    inner_up = lax.dynamic_index_in_dim(inner_up, spot, 2, keepdims=False).reshape(codes, 2 * share)
    outer_down = flat_down(mlp_out_down).reshape(codes, copies, size, share)
    outer_down = lax.dynamic_index_in_dim(outer_down, part, 1, keepdims=False)
    outer_down = lax.dynamic_index_in_dim(outer_down, spot, 1, keepdims=False)

    places = [place_mlp] + [slot_layout(r, experts, capacity) for r in routes_there[1:]]
    query_rows = after(query_rows, *normed_parts[1:])
    query_parts = nn(query_rows.reshape(-1, width), query_full).astype(bf16)
    query_home = home_join(query_parts.reshape(holders, capacity, -1), experts, copies)
    pairs, pair_low = project_pairs(
        normed_parts, pair_weight, pair_down, pair_up, cosine_all, sine_all
    )
    output_own = after(output_weight[0], pair_weight, query_home, *early[1:])
    output_full = lax.all_gather(output_own, "seq", axis=0, tiled=True)
    grad_rows = [grad_own.reshape(-1, width)]
    for d in range(1, size):
        sent = grad_parts[d] if d < 2 else after(grad_parts[d], pairs)
        sent = tn(either(places[d]), sent).astype(bf16)
        grad_rows.append(send_full(sent, experts, copies).reshape(-1, width))
    attended, output_slots, query_rot, totals = attend(
        query_home, place, query_low, query_upper, cosine, sine, pairs, bias
    )

    output_rows = send_cut(output_slots, experts, copies)
    inner_sent = [cut_share(mlp_in_weight[0], (spot - d) % size, size) for d in range(size)]
    output_rows = after(output_rows, *grad_rows[:3], *inner_sent)
    output_parts = nn(output_rows.reshape(holders * capacity, -1), output_full).astype(bf16)
    far = size // 2
    distances = [d for d in range(1, size) if d != far] + ([far] if size > 1 else [])
    inner_parts = list(inner_sent)
    for d in distances[:1]:
        inner_parts[d] = shifted(after(inner_sent[d], output_full), d, size)
    output_home = home_add(output_parts.reshape(holders, capacity, width), experts, copies)
    output_low = nt(attended, output_lower).astype(bf16)
    branch = nn(place, output_home) + nn(output_low, output_upper)
    branch = branch.reshape(2, rows, width)
    middle = inputs + gates[:, :1] * branch[0] + gates[:, 1:] * branch[1]
    middle_scale = norm_scale(middle)
    normed_mlp = (middle * middle_scale * mlp_gain).astype(bf16)
    mlp_gates, mlp_hits = gate_pair(nn(normed_mlp, mlp_router_weight), mlp_routes[0])

    lanes = jnp.pad(jnp.concatenate(halves(mlp_gates), axis=1), ((0, 0), (0, 124)))
    packet = jnp.concatenate([normed_mlp, lanes], axis=1)
    packet = after(packet, *(inner_parts[d] for d in distances[:1]))
    packet_all = lax.all_gather(packet, "seq", axis=0, tiled=True)
    before = packet_all
    for d in distances[1:]:
        before = inner_parts[d] = shifted(after(inner_sent[d], before), d, size)
    packets = [packet] + [
        lax.dynamic_slice_in_dim(packet_all, (spot + d) % size * rows, rows, 0)
        for d in range(1, size)
    ]
    gates_there = [
        (p[:, width : width + 2].astype(f32) + p[:, width + 2 : width + 4].astype(f32)).T.reshape(-1, 1)
        for p in packets
    ]
    combines = [either((places[d].astype(f32) * gates_there[d]).astype(bf16)) for d in range(size)]
    order = list(range(size))
    outer_codes = [nt(got, outer_up).astype(bf16) * mask for got in grad_rows]
    hidden_grads = [
        (nt(got, outer_full) + nn(code, outer_down)).astype(bf16)
        for got, code in zip(grad_rows, outer_codes)
    ]
    gate_slots = jnp.stack(
        [jnp.sum(places[d].astype(f32) * gates_there[d], axis=0) for d in range(size)]
    )
    gate_slots = gate_slots.reshape(size, experts, capacity).transpose(1, 0, 2)
    gate_slots = exchange(jnp.repeat(gate_slots, copies, axis=0))

    def send_rows(d, *earlier):
        sent = tn(either(places[d]), after(packets[d][:, :width], *earlier)).astype(bf16)
        return send_full(sent, experts, copies).reshape(-1, width)

    def work(d, got):
        return expert_block(got, hidden_grads[d], mask, inner_up, inner_down, inner_parts, spot)

    def rows_home(d, row_grad):
        home = home_add(row_grad.reshape(holders, capacity, -1), experts, copies)
        row_sum = nn(combines[d], home[:, :width])
        gate_sum = nn(places[d], home[:, width:])
        lanes = gate_sum[:rows] + jnp.roll(gate_sum[rows:], 2, axis=1)
        row_back = jnp.concatenate([row_sum, lanes], axis=1)
        return home, shifted(row_back.astype(bf16), -d % size, size) if d else row_back

    got_rows = [send_rows(0)]
    for d in order[1:]:
        earlier = [inner_parts[distances[min(d - 1, size - 2)]]]
        got_rows.append(send_rows(d, got_rows[-1], *earlier))
    kept = [work(0, after(got_rows[0], got_rows[-2]) if size > 1 else got_rows[0])]
    row_home, row_total = rows_home(0, kept[0][0])
    row_backs, row_homes = [row_total], [row_home]
    for d in order[1:]:
        kept.append(work(d, after(got_rows[d], kept[-1][0])))
        row_grad = kept[d][0]
        row_home, row_back = rows_home(d, row_grad)
        row_backs.append(row_back)
        row_homes.append(row_home)
        row_total = row_total + row_back.astype(f32)
    gate_sum = row_total[:, width : width + 4]
    row_total = row_total[:, :width]
    mlp_gate_grad = gate_sum.reshape(rows, 2, 2).sum(2)
    mlp_logit_grad = gate_back(mlp_gates, mlp_hits, mlp_gate_grad)

    outer_lows, sums = [], None
    for d in order:
        _, activated, pre_grad, code, back = kept[d]
        there = row_homes[min(d, size - 2)] if size > 1 else row_homes[0]
        activated, pre_grad = after(activated, there), after(pre_grad, there)
        outer_low = nt(activated, outer_down).astype(bf16) * mask
        outer_lows.append(outer_low)
        scale = gate_slots[:, d, :].reshape(-1, 1)

        def scaled(array):
            return (array.astype(f32) * scale).astype(bf16)

        new = (
            tn(scaled(code), pre_grad),
            tn(scaled(outer_codes[d]), activated),
            tn(scaled(back), got_rows[d]),
            tn(scaled(outer_low), grad_rows[d]),
        )
        sums = new if sums is None else tuple(a + b for a, b in zip(sums, new))


    inner_up_sum, outer_down_sum, inner_down_sum, outer_up_sum = sums

    def widened(array):
        if copies == 1:
            return array
        whole = jnp.zeros((codes, copies, array.shape[1]), f32)
        whole = lax.dynamic_update_index_in_dim(whole, array, part, 1)
        return whole.reshape(codes, -1)

    wide = [widened(inner_up_sum), widened(outer_down_sum), inner_down_sum, outer_up_sum]
    ends = [sum(a.shape[1] for a in wide[: k + 1]) for k in range(3)]
    mlp_own = after(jnp.concatenate(wide, axis=1).astype(bf16), row_home)
    mlp_sums = lax.psum_scatter(mlp_own, "dp", scatter_dimension=0, tiled=True)

    def down_back(d, before_matmul, before_sending):
        activated = after(kept[d][1], before_matmul)
        down = (nn(activated, outer_full) + nn(outer_lows[d], outer_up)).astype(bf16)
        down = after(down, before_sending).reshape(holders, capacity, width)
        home = home_add(down, experts, copies)
        made = nn(combines[d], home)
        return home, shifted(made.astype(bf16), -d % size, size).astype(f32) if d else made

    down_turns = order[1:] + [0]
    down_home, down_total = down_back(down_turns[0], row_homes[-2], row_home)

    normed_mlp_grad = row_total + nt(mlp_logit_grad.astype(bf16), mlp_router_weight)
    middle_grad = norm_back(middle, middle_scale, mlp_gain, normed_mlp_grad)
    middle_grad = middle_grad + out_grad[0].astype(f32)
    middle_low = middle_grad.astype(bf16)
    branch_sent = tn(place_any, after(middle_low, down_home)).astype(bf16)
    branch_rows = send_full(branch_sent, experts, copies)
    mlp_sums = lax.all_gather(after(mlp_sums, branch_rows), ("seq", "dp"), axis=0, tiled=True)
    head_parts = nt(branch_rows.reshape(-1, width), output_full).astype(bf16)
    head_home = home_join(head_parts.reshape(holders, capacity, -1), experts, copies)
    down_home, made = down_back(down_turns[1], head_parts, head_home)
    down_total = down_total + made
    head_home = after(head_home, mlp_own)
    gate_grad = jnp.sum(middle_grad[None] * branch, axis=2).T
    logit_grad = gate_back(gates, hits, gate_grad)
    gate_column = gates.T.reshape(-1, 1)
    output_low_grad = nt(middle_low, output_upper)
    output_low_back = output_low_grad.astype(bf16)
    output_low_scaled = (jnp.tile(output_low_grad, (2, 1)) * gate_column).astype(bf16)
    output_lower_grad = tn(output_low_scaled, attended)
    output_low_sum = (output_low.astype(f32) * gate_column).reshape(2, rows, rank).sum(0)
    output_upper_grad = tn(output_low_sum.astype(bf16), middle_low)

    def over_sequences(mine, widths):
        every = lax.all_gather(mine, ("seq", "dp"), axis=0, tiled=False)
        every = every.reshape(size, holders, rank, -1)
        return gather_adapters(every, adapter_all, adapters, widths)

    key_grad, value_grad, query_slots, query_sum = attend_back(
        query_rot,
        pairs,
        bias,
        totals,
        head_home,
        place,
        gate_column,
        output_low_back,
        output_lower,
        cosine,
        sine,
        cosine_all,
        sine_all,
    )
    query_back = send_cut(after(query_slots, down_home), experts, copies)
    input_parts = nt(query_back.reshape(holders * capacity, -1), query_full).astype(bf16)
    input_home = home_add(input_parts.reshape(holders, capacity, width), experts, copies)
    mlp_sums = after(mlp_sums, input_parts)
    if copies == 1 and share % 128 == 0:
        inner_up_grad, outer_down_grad, inner_down_grad, outer_up_grad = unpack_sums(
            mlp_sums.reshape(size, adapters, rank, -1), share, width
        )
    else:
        mlp_sums = mlp_sums.astype(f32).reshape(size, codes, -1)
        inner_up_grad, outer_down_grad, inner_down_grad, outer_up_grad = jnp.split(mlp_sums, ends, axis=2)
        inner_up_grad = inner_up_grad.reshape(size, codes, copies, 2, share).transpose(1, 3, 2, 0, 4)
        inner_up_grad = inner_up_grad.reshape(adapters, rank, -1)
        outer_down_grad = outer_down_grad.reshape(size, codes, copies, share).transpose(1, 2, 0, 3)
        outer_down_grad = outer_down_grad.reshape(adapters, rank, -1)
        inner_down_grad = jnp.sum(inner_down_grad, 0).reshape(adapters, rank, width)
        outer_up_grad = jnp.sum(outer_up_grad, 0).reshape(adapters, rank, width)
    half = key_grad.shape[1]
    pair_low_grad = nt(key_grad, pair_up[:, :half]) + nt(value_grad, pair_up[:, half:])
    pair_low_grad = pair_low_grad.astype(bf16)
    pair_upper_grad = jnp.concatenate([tn(pair_low, key_grad), tn(pair_low, value_grad)], axis=1)
    pair_lower_grad = sum(
        tn(pair_low_grad[d * rows : (d + 1) * rows], normed_parts[d]) for d in range(size)
    )
    query_low_grad = nt(query_sum, query_upper).astype(bf16)
    query_upper_grad = tn(query_low, query_sum)
    query_lower_grad = tn(query_low_grad, normed)
    sequence_grads = [
        pair_lower_grad,
        pair_upper_grad,
        query_lower_grad,
        query_upper_grad,
        output_lower_grad,
        output_upper_grad,
    ]
    joined = jnp.concatenate([a.reshape(rank, size, -1) for a in sequence_grads], axis=2)
    joined = joined.transpose(1, 0, 2)
    normed_grads = pair_back(key_grad, value_grad, pair_weight, pair_low_grad, pair_down)
    mine = picked(joined, spot)
    back_parts = []
    for d in range(1, size):
        theirs = picked(joined, (spot + d) % size).astype(bf16).reshape(-1, width)
        theirs = jnp.pad(theirs, ((0, -theirs.shape[0] % 16), (0, 0)))
        packet = jnp.concatenate([normed_grads[d * rows : (d + 1) * rows], theirs], axis=0)
        packet = after(shifted(packet, -d % size, size), inner_up_grad)
        back_parts.append(packet[:rows])
        adapter_rows = mine.size // width
        mine = mine + packet[rows : rows + adapter_rows].astype(f32).reshape(mine.shape)
    mine = after(mine.astype(bf16), mlp_sums)
    late = over_sequences(mine, [a.shape[1] for a in sequence_grads])
    normed_grad = normed_grads[:rows].astype(f32) + sum(back.astype(f32) for back in back_parts)
    normed_grad = normed_grad + nn(place_any, input_home) + nn(query_low_grad, query_lower)
    normed_grad = normed_grad + nt(logit_grad.astype(bf16), router_weight)
    input_grad = norm_back(inputs, input_scale, norm_gain, normed_grad) + middle_grad

    for d in down_turns[2:]:
        down_home, made = down_back(d, query_slots, input_home)
        down_total = down_total + made
    result = (middle + down_total).astype(bf16)

    return (
        result[None],
        input_grad[None],
        flat_down(late[0]),
        late[1],
        flat_down(late[2]),
        late[3],
        flat_down(late[4]),
        late[5],
        flat_down(inner_down_grad),
        inner_up_grad,
        flat_down(outer_down_grad),
        outer_up_grad,
    )


def solution(mesh):
    split = P("dp", "seq", None)
    placed = (
        (split, P(), P("seq", None), P(), split, split, P(), P(), split, split)
        + (P(),) * 10
        + (split, split, P("dp"), P("dp"), split)
    )
    return jax.shard_map(
        body,
        mesh=mesh,
        in_specs=placed,
        out_specs=(split, split) + (P(),) * 10,
        check_vma=False,
    )
```

```python
import functools
import math

import jax
import jax.numpy as jnp
import numpy as np
from jax import lax
from jax.experimental import pallas as pl
from jax.experimental.pallas import tpu as pltpu
from jax.sharding import PartitionSpec as P

KV_HEADS = 16
HD = 128

norm_eps = 1e-05
rope_base = 10000.0
masked_score = -1e30
vmem_bytes = 48 * 2**20

bf16 = jnp.bfloat16
f32 = jnp.float32


def product(left, right, left_dim, right_dim):
    return lax.dot_general(
        left, right, (((left_dim,), (right_dim,)), ((), ())), preferred_element_type=f32
    )


def nn(left, right):
    return product(left, right, 1, 0)


def nt(left, right):
    return product(left, right, 1, 1)


def tn(left, right):
    return product(left, right, 0, 0)


def pair_kernel(count, key_blocks, *refs):
    normed_refs = refs[:count]
    w_ref, down_ref, up_ref, cos_ref, sin_ref, out_ref, low_ref = refs[count:]
    rows = normed_refs[0].shape[0]
    step = pl.program_id(0)

    @pl.when(step == 0)
    def _():
        for k in range(count):
            low_ref[pl.ds(k * rows, rows), :] = nt(normed_refs[k][...], down_ref[...]).astype(bf16)

    for k in range(count):
        part = pl.ds(k * rows, rows)
        made = nn(normed_refs[k][...], w_ref[0]) + nn(low_ref[part, :], up_ref[...])

        @pl.when(step < key_blocks)
        def _():
            for start in range(0, made.shape[1], HD):
                head = made[:, start : start + HD]
                turned = head * cos_ref[part, :] + pltpu.roll(head, HD // 2, 1) * sin_ref[part, :]
                out_ref[part, start : start + HD] = turned.astype(bf16)

        @pl.when(step >= key_blocks)
        def _():
            out_ref[part, :] = made.astype(bf16)


def project_pairs(normed_parts, weight, down, upper, cosine, sine):
    count = len(normed_parts)
    rows, width = normed_parts[0].shape
    blocks, _, block = weight.shape
    columns = blocks * block
    whole = lambda array: pl.BlockSpec(array.shape, lambda i: (0, 0))
    return pl.pallas_call(
        functools.partial(pair_kernel, count, blocks // 2),
        grid=(blocks,),
        in_specs=[whole(n) for n in normed_parts]
        + [
            pl.BlockSpec((1, width, block), lambda i: (i, 0, 0)),
            whole(down),
            pl.BlockSpec((upper.shape[0], block), lambda i: (0, i)),
            whole(cosine),
            whole(sine),
        ],
        out_specs=[
            pl.BlockSpec((count * rows, block), lambda i: (0, i)),
            pl.BlockSpec((count * rows, down.shape[0]), lambda i: (0, 0)),
        ],
        out_shape=[
            jax.ShapeDtypeStruct((count * rows, columns), bf16),
            jax.ShapeDtypeStruct((count * rows, down.shape[0]), bf16),
        ],
        compiler_params=pltpu.CompilerParams(vmem_limit_bytes=vmem_bytes),
        cost_estimate=pl.CostEstimate(
            flops=2 * count * rows * width * columns,
            bytes_accessed=2 * width * columns,
            transcendentals=0,
        ),
        name="pairs",
    )(*normed_parts, weight, down, upper, cosine, sine)


def pair_back_kernel(key_blocks, key_ref, value_ref, w_ref, low_ref, down_ref, out_ref, sum_ref):
    step = pl.program_id(0)

    @pl.when(step == 0)
    def _():
        sum_ref[...] = nn(low_ref[...], down_ref[...])

    @pl.when(step < key_blocks)
    def _():
        sum_ref[...] += nt(key_ref[...], w_ref[0])

    @pl.when(step >= key_blocks)
    def _():
        sum_ref[...] += nt(value_ref[...], w_ref[0])

    @pl.when(step == pl.num_programs(0) - 1)
    def _():
        out_ref[...] = sum_ref[...].astype(bf16)


def pair_back(key_grad, value_grad, weight, low_grad, down):
    blocks, width, block = weight.shape
    rows = key_grad.shape[0]
    half = blocks // 2
    whole = lambda array: pl.BlockSpec(array.shape, lambda i: (0, 0))
    return pl.pallas_call(
        functools.partial(pair_back_kernel, half),
        grid=(blocks,),
        in_specs=[
            pl.BlockSpec((rows, block), lambda i: (0, jnp.minimum(i, half - 1))),
            pl.BlockSpec((rows, block), lambda i: (0, jnp.maximum(i - half, 0))),
            pl.BlockSpec((1, width, block), lambda i: (i, 0, 0)),
            whole(low_grad),
            whole(down),
        ],
        out_specs=pl.BlockSpec((rows, width), lambda i: (0, 0)),
        out_shape=jax.ShapeDtypeStruct((rows, width), bf16),
        scratch_shapes=[pltpu.VMEM((rows, width), f32)],
        compiler_params=pltpu.CompilerParams(vmem_limit_bytes=vmem_bytes),
        cost_estimate=pl.CostEstimate(
            flops=2 * rows * width * blocks * block,
            bytes_accessed=2 * width * blocks * block,
            transcendentals=0,
        ),
        name="pair_back",
    )(key_grad, value_grad, weight, low_grad, down)


def attend_kernel(
    scale,
    home_ref,
    place_ref,
    low_ref,
    up_ref,
    cos_ref,
    sin_ref,
    key_ref,
    value_ref,
    bias_ref,
    attended_ref,
    slots_ref,
    query_ref,
    total_ref,
):
    rows = cos_ref.shape[0]
    base = nn(place_ref[...], home_ref[...])
    extra = nn(low_ref[...], up_ref[...])
    keys, values = key_ref[...], value_ref[...]
    for route in range(2):
        part = pl.ds(route * rows, rows)
        query = base[route * rows : (route + 1) * rows] + extra
        query = query * cos_ref[...] + pltpu.roll(query, HD // 2, 1) * sin_ref[...]
        query = query.astype(bf16)
        query_ref[part, :] = query
        scores = nt(query, keys) * scale + bias_ref[...]
        highest = jnp.max(scores, axis=1, keepdims=True)
        weights = jnp.exp(scores - highest)
        total = jnp.sum(weights, axis=1, keepdims=True)
        attended = nn(weights.astype(bf16), values) / total
        attended_ref[part, :] = attended.astype(bf16)
        total_ref[0, part, :] = highest + jnp.log(total)
    slots_ref[...] = tn(place_ref[...], attended_ref[...]).astype(bf16)


def attend(home, place, low, upper, cosine, sine, pairs, bias):
    rows2, slots = place.shape
    rows, length = bias.shape
    heads = home.shape[1] // HD
    kv_heads = pairs.shape[1] // (2 * HD)
    whole = lambda array: pl.BlockSpec(array.shape, lambda h: (0, 0))
    return pl.pallas_call(
        functools.partial(attend_kernel, 1.0 / math.sqrt(HD)),
        grid=(heads,),
        in_specs=[
            pl.BlockSpec((slots, HD), lambda h: (0, h)),
            whole(place),
            whole(low),
            pl.BlockSpec((upper.shape[0], HD), lambda h: (0, h)),
            whole(cosine),
            whole(sine),
            pl.BlockSpec((length, HD), lambda h: (0, h)),
            pl.BlockSpec((length, HD), lambda h: (0, kv_heads + h)),
            whole(bias),
        ],
        out_specs=[
            pl.BlockSpec((rows2, HD), lambda h: (0, h)),
            pl.BlockSpec((slots, HD), lambda h: (0, h)),
            pl.BlockSpec((rows2, HD), lambda h: (0, h)),
            pl.BlockSpec((1, rows2, 1), lambda h: (h, 0, 0)),
        ],
        out_shape=[
            jax.ShapeDtypeStruct((rows2, heads * HD), bf16),
            jax.ShapeDtypeStruct((slots, heads * HD), bf16),
            jax.ShapeDtypeStruct((rows2, heads * HD), bf16),
            jax.ShapeDtypeStruct((heads, rows2, 1), f32),
        ],
        compiler_params=pltpu.CompilerParams(vmem_limit_bytes=vmem_bytes),
        cost_estimate=pl.CostEstimate(
            flops=4 * heads * rows2 * length * HD,
            bytes_accessed=4 * length * heads * HD,
            transcendentals=heads * rows2 * length,
        ),
        name="attend",
    )(home, place, low, upper, cosine, sine, pairs, pairs, bias)


def attend_back_kernel(
    scale,
    query_ref,
    key_ref,
    value_ref,
    bias_ref,
    total_ref,
    home_ref,
    place_ref,
    gate_ref,
    low_ref,
    down_ref,
    cos_ref,
    sin_ref,
    cos_all_ref,
    sin_all_ref,
    key_grad_ref,
    value_grad_ref,
    slots_ref,
    sum_ref,
    turned_ref,
):
    rows = cos_ref.shape[0]
    base = nn(place_ref[...], home_ref[...])
    extra = nn(low_ref[...], down_ref[...])
    keys, values = key_ref[...], value_ref[...]
    key_grad = value_grad = None
    for route in range(2):
        part = pl.ds(route * rows, rows)
        query = query_ref[part, :]
        grad = (base[route * rows : (route + 1) * rows] + extra) * gate_ref[part, :]
        grad = grad.astype(bf16)
        scores = nt(query, keys) * scale + bias_ref[...]
        weights = jnp.exp(scores - total_ref[0, part, :])
        weight_grad = nt(grad, values)
        mean_grad = jnp.sum(weights * weight_grad, axis=1, keepdims=True)
        score_grad = (weights * (weight_grad - mean_grad)).astype(bf16)
        query_grad = nn(score_grad, keys) * scale
        query_grad = query_grad * cos_ref[...] - pltpu.roll(query_grad, HD // 2, 1) * sin_ref[...]
        turned_ref[part, :] = query_grad.astype(bf16)
        key_part = tn(score_grad, query)
        value_part = tn(weights.astype(bf16), grad)
        key_grad = key_part if route == 0 else key_grad + key_part
        value_grad = value_part if route == 0 else value_grad + value_part
    key_grad = key_grad * scale
    key_grad = key_grad * cos_all_ref[...] - pltpu.roll(key_grad, HD // 2, 1) * sin_all_ref[...]
    key_grad_ref[...] = key_grad.astype(bf16)
    value_grad_ref[...] = value_grad.astype(bf16)
    slots_ref[...] = tn(place_ref[...], turned_ref[...]).astype(bf16)
    first = turned_ref[pl.ds(0, rows), :].astype(f32)
    sum_ref[...] = (first + turned_ref[pl.ds(rows, rows), :].astype(f32)).astype(bf16)


def attend_back(query, pairs, bias, totals, home, place, gates, low, down, cosine, sine, cosine_all, sine_all):
    rows2, slots = place.shape
    rows, length = bias.shape
    heads = home.shape[1] // HD
    kv_heads = pairs.shape[1] // (2 * HD)
    whole = lambda array: pl.BlockSpec(array.shape, lambda h: (0, 0))
    return pl.pallas_call(
        functools.partial(attend_back_kernel, 1.0 / math.sqrt(HD)),
        grid=(heads,),
        in_specs=[
            pl.BlockSpec((rows2, HD), lambda h: (0, h)),
            pl.BlockSpec((length, HD), lambda h: (0, h)),
            pl.BlockSpec((length, HD), lambda h: (0, kv_heads + h)),
            whole(bias),
            pl.BlockSpec((1, rows2, 1), lambda h: (h, 0, 0)),
            pl.BlockSpec((slots, HD), lambda h: (0, h)),
            whole(place),
            whole(gates),
            whole(low),
            pl.BlockSpec((down.shape[0], HD), lambda h: (0, h)),
            whole(cosine),
            whole(sine),
            whole(cosine_all),
            whole(sine_all),
        ],
        out_specs=[
            pl.BlockSpec((length, HD), lambda h: (0, h)),
            pl.BlockSpec((length, HD), lambda h: (0, h)),
            pl.BlockSpec((slots, HD), lambda h: (0, h)),
            pl.BlockSpec((rows, HD), lambda h: (0, h)),
        ],
        out_shape=[
            jax.ShapeDtypeStruct((length, heads * HD), bf16),
            jax.ShapeDtypeStruct((length, heads * HD), bf16),
            jax.ShapeDtypeStruct((slots, heads * HD), bf16),
            jax.ShapeDtypeStruct((rows, heads * HD), bf16),
        ],
        scratch_shapes=[pltpu.VMEM((rows2, HD), bf16)],
        compiler_params=pltpu.CompilerParams(vmem_limit_bytes=vmem_bytes),
        cost_estimate=pl.CostEstimate(
            flops=10 * heads * rows2 * length * HD,
            bytes_accessed=8 * length * heads * HD,
            transcendentals=heads * rows2 * length,
        ),
        name="attend_back",
    )(query, pairs, pairs, bias, totals, home, place, gates, low, down, cosine, sine, cosine_all, sine_all)


def exchange(buffer):
    return lax.all_to_all(buffer, "dp", split_axis=0, concat_axis=0, tiled=True)


def in_order(parts, spot):
    count = len(parts)
    twice = jnp.concatenate(parts + parts, axis=0)
    rows = parts[0].shape[0]
    return lax.dynamic_slice_in_dim(twice, (count - spot) % count * rows, count * rows, 0)


def shifted(array, shift, size):
    if shift == 0:
        return array
    return lax.ppermute(array, "seq", [(k, (k - shift) % size) for k in range(size)])


def send_full(slots, experts, copies):
    buffer = slots.reshape(experts, slots.shape[0] // experts, slots.shape[1])
    if copies > 1:
        buffer = jnp.repeat(buffer, copies, axis=0)
    return exchange(buffer)


def send_cut(slots, experts, copies):
    buffer = slots.reshape(experts, slots.shape[0] // experts, slots.shape[1])
    if copies > 1:
        _, rows, columns = buffer.shape
        buffer = buffer.reshape(experts, rows, copies, columns // copies).transpose(0, 2, 1, 3)
        buffer = buffer.reshape(experts * copies, rows, columns // copies)
    return exchange(buffer)


def home_join(parts, experts, copies):
    home = exchange(parts)
    _, rows, columns = home.shape
    if copies > 1:
        home = home.reshape(experts, copies, rows, columns).transpose(0, 2, 1, 3)
    return home.reshape(experts * rows, copies * columns)


def home_add(parts, experts, copies):
    home = exchange(parts)
    _, rows, columns = home.shape
    if copies > 1:
        home = home.reshape(experts, copies, rows, columns).astype(f32)
        home = jnp.sum(home, axis=1).astype(parts.dtype)
    return home.reshape(experts * rows, columns)


def slot_layout(route_ids, experts, capacity):
    flat = route_ids.T.reshape(-1)
    count = flat.shape[0]
    hits = flat[:, None] == jnp.arange(experts)[None, :]
    earlier = jnp.arange(count)[:, None] > jnp.arange(count)[None, :]
    before = nn(earlier.astype(bf16), hits.astype(bf16))
    rank = jnp.sum(jnp.where(hits, before, 0.0), axis=1).astype(jnp.int32)
    slot = flat * capacity + rank
    return (slot[:, None] == jnp.arange(experts * capacity)[None, :]).astype(bf16)


def either(place):
    rows = place.shape[0] // 2
    return place[:rows] + place[rows:]


def norm_back(values, scale, gain, grad):
    weighted = grad * gain
    mean = jnp.mean(weighted * values, axis=-1, keepdims=True)
    return weighted * scale - values * (scale * scale * scale * mean)


def norm_scale(values):
    return lax.rsqrt(jnp.mean(values * values, axis=-1, keepdims=True) + norm_eps)


def gate_pair(logits, route_ids):
    hits = (route_ids[:, :, None] == jnp.arange(logits.shape[1])).astype(f32)
    chosen = jnp.sum(hits * logits[:, None, :], axis=2)
    weights = jnp.exp(chosen - jnp.max(chosen, axis=1, keepdims=True))
    return weights / jnp.sum(weights, axis=1, keepdims=True), hits


def gate_back(gates, hits, grad):
    mean = jnp.sum(gates * grad, axis=1, keepdims=True)
    return jnp.sum((gates * (grad - mean))[:, :, None] * hits, axis=1)


def rope_full(length, start):
    half = HD // 2
    frequency = rope_base ** (-np.arange(half) / half)
    angles = np.arange(length)[:, None] * frequency[None, :]
    cosine, sine = np.cos(angles), np.sin(angles)
    tables = np.concatenate([cosine, cosine, -sine, sine], 1).astype(np.float32)
    tables = jnp.asarray(np.concatenate([tables, tables], 0))
    tables = lax.dynamic_slice_in_dim(tables, start, length, 0)
    return tables[:, :HD], tables[:, HD:]


def after(array, *earlier):
    return lax.optimization_barrier((array,) + earlier)[0]


def cut_kernel(target_ref, in_ref, out_ref):
    out_ref[...] = in_ref[...]


def cut_share(weight, target, size):
    rows, columns = weight.shape
    share = columns // 2 // size
    if share % 128:
        cut = weight.reshape(rows, 2, size, share)
        return lax.dynamic_index_in_dim(cut, target, 2, keepdims=False).reshape(rows, 2 * share)
    return pl.pallas_call(
        cut_kernel,
        grid_spec=pltpu.PrefetchScalarGridSpec(
            num_scalar_prefetch=1,
            grid=(2,),
            in_specs=[pl.BlockSpec((rows, share), lambda i, t: (0, i * size + t[0]))],
            out_specs=pl.BlockSpec((rows, share), lambda i, t: (0, i)),
        ),
        out_shape=jax.ShapeDtypeStruct((rows, 2 * share), bf16),
        compiler_params=pltpu.CompilerParams(vmem_limit_bytes=vmem_bytes),
        name="cut",
    )(target.reshape(1).astype(jnp.int32), weight)


def unpack_kernel(size, share, in_ref, inner_up_ref, outer_down_ref, inner_down_ref, outer_up_ref):
    spot = pl.program_id(1)
    got = in_ref[0, 0].astype(f32)
    hidden = size * share
    width = inner_down_ref.shape[2]
    start = pl.multiple_of(spot * share, 128)
    inner_up_ref[0, :, pl.ds(start, share)] = got[:, :share]
    inner_up_ref[0, :, pl.ds(pl.multiple_of(hidden + start, 128), share)] = got[:, share : 2 * share]
    outer_down_ref[0, :, pl.ds(start, share)] = got[:, 2 * share : 3 * share]
    inner_down = got[:, 3 * share : 3 * share + width]
    outer_up = got[:, 3 * share + width :]

    @pl.when(spot == 0)
    def _():
        inner_down_ref[0] = inner_down
        outer_up_ref[0] = outer_up

    @pl.when(spot > 0)
    def _():
        inner_down_ref[0] += inner_down
        outer_up_ref[0] += outer_up


def unpack_sums(sums, share, width):
    size, adapters, rank, columns = sums.shape
    hidden = size * share
    shapes = [2 * hidden, hidden, width, width]
    return pl.pallas_call(
        functools.partial(unpack_kernel, size, share),
        grid=(adapters, size),
        in_specs=[pl.BlockSpec((1, 1, rank, columns), lambda a, k: (k, a, 0, 0))],
        out_specs=[pl.BlockSpec((1, rank, n), lambda a, k: (a, 0, 0)) for n in shapes],
        out_shape=[jax.ShapeDtypeStruct((adapters, rank, n), f32) for n in shapes],
        compiler_params=pltpu.CompilerParams(vmem_limit_bytes=vmem_bytes),
        cost_estimate=pl.CostEstimate(
            flops=0, bytes_accessed=12 * adapters * rank * (3 * hidden + 2 * width), transcendentals=0
        ),
        name="unpack",
    )(sums)


def gather_adapters_kernel(adapters, ids_ref, in_ref, *out_refs):
    holders = in_ref.shape[1]
    start = 0
    for out_ref in out_refs:
        columns = out_ref.shape[2]
        parts = [in_ref[0, k, :, start : start + columns].astype(f32) for k in range(holders)]
        for a in range(adapters):
            total = None
            for k in range(holders):
                one = jnp.where(ids_ref[k] == a, parts[k], 0.0)
                total = one if total is None else total + one
            out_ref[a] = total
        start += columns


def gather_adapters(every, adapter_all, adapters, widths):
    size, holders, rank, columns = every.shape
    return pl.pallas_call(
        functools.partial(gather_adapters_kernel, adapters),
        grid_spec=pltpu.PrefetchScalarGridSpec(
            num_scalar_prefetch=1,
            grid=(size,),
            in_specs=[pl.BlockSpec((1, holders, rank, columns), lambda k, s: (k, 0, 0, 0))],
            out_specs=[
                pl.BlockSpec((adapters, rank, n // size), lambda k, s: (0, 0, k)) for n in widths
            ],
        ),
        out_shape=[jax.ShapeDtypeStruct((adapters, rank, n), f32) for n in widths],
        compiler_params=pltpu.CompilerParams(vmem_limit_bytes=vmem_bytes),
        name="gather_adapters",
    )(adapter_all, every)


def silu_parts(gate_part, up_part, hidden_grad):
    sigmoid = 1.0 / (1.0 + jnp.exp(-gate_part))
    active = gate_part * sigmoid
    activated = (active * up_part).astype(bf16)
    gate_grad = hidden_grad * up_part * sigmoid * (1.0 + gate_part * (1.0 - sigmoid))
    return activated, gate_grad.astype(bf16), (hidden_grad * active).astype(bf16)


def halves(value):
    high = value.astype(bf16)
    return high, (value - high.astype(f32)).astype(bf16)


def expert_kernel(size, share, spot_ref, x_ref, hidden_ref, mask_ref, up_ref, down_ref, *refs):
    w_refs = refs[:size]
    row_ref, active_ref, pre_ref, code_ref, back_ref = refs[size:]
    depth = w_refs[0].shape[0]
    width = size * depth
    columns = [pl.ds(pl.multiple_of((spot_ref[0] + k) % size * depth, 128), depth) for k in range(size)]
    code = nt(x_ref[...], down_ref[...]).astype(bf16) * mask_ref[...]
    code_ref[...] = code
    sums = None
    for start in range(0, share, 256):
        end = min(start + 256, share)

        def hidden(first, last):
            made = nn(code, up_ref[:, first:last])
            for k in range(size):
                made = made + nn(x_ref[:, columns[k]], w_refs[k][:, first:last])
            return made

        gate_part, up_part = hidden(start, end), hidden(share + start, share + end)
        hidden_grad = hidden_ref[:, start:end].astype(f32)
        activated, gate_grad, up_grad = silu_parts(gate_part, up_part, hidden_grad)
        active_ref[:, start:end] = activated
        pre_ref[:, start:end] = gate_grad
        pre_ref[:, share + start : share + end] = up_grad
        part = jnp.sum(activated.astype(f32) * hidden_grad, axis=1, keepdims=True)
        sums = part if sums is None else sums + part
    back = nt(pre_ref[...], up_ref[...]).astype(bf16) * mask_ref[...]
    back_ref[...] = back
    for k in range(size):
        base = (spot_ref[0] + k) % size * depth
        for start in range(0, depth, 256):
            end = min(start + 256, depth)
            here = pl.ds(pl.multiple_of(base + start, 128), end - start)
            made = nt(pre_ref[...], w_refs[k][start:end, :]) + nn(back, down_ref[:, here])
            row_ref[:, here] = made.astype(bf16)
    high, low = halves(sums)
    lane = lax.broadcasted_iota(jnp.int32, (sums.shape[0], 128), 1)
    packed = jnp.where(lane == 0, high.astype(f32), jnp.where(lane == 1, low.astype(f32), 0.0))
    row_ref[:, width:] = packed.astype(bf16)


def expert_block(got, hidden_grad, mask, inner_up, inner_down, inner_parts, spot):
    size = len(inner_parts)
    rows, width = got.shape
    share = hidden_grad.shape[1]
    codes = mask.shape[1]
    if share % 128 or width // size % 256:
        code = nt(got, inner_down).astype(bf16) * mask
        inner_full = in_order(inner_parts, spot)
        pre = nn(got, inner_full) + nn(code, inner_up)
        hidden_float = hidden_grad.astype(f32)
        activated, gate_grad, up_grad = silu_parts(pre[:, :share], pre[:, share:], hidden_float)
        pre_grad = jnp.concatenate([gate_grad, up_grad], axis=1)
        back = nt(pre_grad, inner_up).astype(bf16) * mask
        row_grad = (nt(pre_grad, inner_full) + nn(back, inner_down)).astype(bf16)
        sums = jnp.stack(halves(jnp.sum(activated.astype(f32) * hidden_float, axis=1)), axis=1)
        row_grad = jnp.concatenate([row_grad, jnp.pad(sums, ((0, 0), (0, 126)))], axis=1)
        return row_grad, activated, pre_grad, code, back
    block = rows // 2
    ahead = lambda n: pl.BlockSpec((block, n), lambda i, s: (i, 0))
    whole = lambda array: pl.BlockSpec(array.shape, lambda i, s: (0, 0), pipeline_mode=pl.Buffered(1))
    shapes = [width + 128, share, 2 * share, codes, codes]
    return pl.pallas_call(
        functools.partial(expert_kernel, size, share),
        grid_spec=pltpu.PrefetchScalarGridSpec(
            num_scalar_prefetch=1,
            grid=(2,),
            in_specs=[ahead(width), ahead(share), ahead(codes), whole(inner_up), whole(inner_down)]
            + [whole(part) for part in inner_parts],
            out_specs=[ahead(n) for n in shapes],
        ),
        out_shape=[jax.ShapeDtypeStruct((rows, n), bf16) for n in shapes],
        compiler_params=pltpu.CompilerParams(vmem_limit_bytes=vmem_bytes),
        cost_estimate=pl.CostEstimate(
            flops=8 * rows * width * share,
            bytes_accessed=4 * width * share + 10 * rows * width,
            transcendentals=rows * share,
        ),
        name="experts",
    )(spot.reshape(1).astype(jnp.int32), got, hidden_grad, mask, inner_up, inner_down, *inner_parts)


def picked(lookup, index):
    return lax.dynamic_index_in_dim(lookup, index, 0, keepdims=False)


def body(
    tokens,
    norm_gain,
    key_value_weight,
    router_weight,
    query_weight,
    output_weight,
    mlp_gain,
    mlp_router_weight,
    mlp_in_weight,
    mlp_out_weight,
    key_value_down,
    key_value_up,
    query_down,
    query_up,
    output_down,
    output_up,
    mlp_in_down,
    mlp_in_up,
    mlp_out_down,
    mlp_out_up,
    routes,
    mlp_routes,
    adapter_index,
    prefix_length,
    out_grad,
):
    seqs, rows, width = tokens.shape
    assert seqs == 1
    size, spot = lax.axis_size("seq"), lax.axis_index("seq")
    holders, holder = lax.axis_size("dp"), lax.axis_index("dp")
    experts = router_weight.shape[1]
    copies = holders // experts
    part = holder % copies
    capacity = 3 * rows // 8
    length = rows * size
    adapters, _, rank = key_value_down.shape
    codes = adapters * rank
    hidden = mlp_in_weight.shape[2] // 2
    share = hidden // size

    def flat_down(lookup):
        return lookup.transpose(0, 2, 1)

    adapter = adapter_index[0]
    adapter_all = exchange(jnp.broadcast_to(adapter_index[None], (holders, 128)))[:, 0]
    inputs = tokens[0].astype(f32)
    input_scale = norm_scale(inputs)
    normed = (inputs * input_scale * norm_gain).astype(bf16)

    gates, hits = gate_pair(nn(normed, router_weight), routes[0])
    place = slot_layout(routes[0], experts, capacity)
    place_any = either(place)
    query_rows = send_full(tn(place_any, normed).astype(bf16), experts, copies)
    query_full = lax.all_gather(query_weight[0], "seq", axis=0, tiled=True)
    block = key_value_weight.shape[1] // holders
    pair_piece = lax.dynamic_slice_in_dim(key_value_weight, holder * block, block, 1)
    packet = jnp.concatenate([normed, pair_piece.reshape(-1, width)], axis=0)
    packets = [packet] + [shifted(packet, d, size) for d in range(1, size)]
    normed_parts = [normed] + [p[:rows] for p in packets[1:]]
    pieces = [pair_piece] + [p[rows:].reshape(-1, block) for p in packets[1:]]
    place_mlp = slot_layout(mlp_routes[0], experts, capacity)
    grad_own = send_full(tn(either(place_mlp), out_grad[0]).astype(bf16), experts, copies)
    pair_own = in_order(pieces, spot)
    pair_own = after(pair_own, query_full, query_rows, grad_own, adapter_all)
    pair_weight = lax.all_gather(pair_own, "dp", axis=0, tiled=False)
    lanes = jnp.pad(mlp_routes[0].astype(bf16), ((0, 0), (0, 126)))
    packet = jnp.concatenate([out_grad[0], lanes], axis=1)
    packet_late = after(packet, query_full)
    early = [packet] + [shifted(packet_late, d, size) for d in range(1, size)]
    grad_parts = [out_grad[0]] + [p[:, :width] for p in early[1:]]
    routes_there = [p[:, width : width + 2].astype(jnp.int32) for p in early]
    outer_full = mlp_out_weight[0]

    pair_down, pair_up = picked(flat_down(key_value_down), adapter), picked(key_value_up, adapter)
    query_lower, query_upper = picked(flat_down(query_down), adapter), picked(query_up, adapter)
    output_lower, output_upper = picked(flat_down(output_down), adapter), picked(output_up, adapter)
    query_low = nt(normed, query_lower).astype(bf16)
    positions = spot * rows + jnp.arange(rows)
    key_pos = (spot * rows + jnp.arange(length)) % length
    cosine_all, sine_all = rope_full(length, spot * rows)
    cosine, sine = cosine_all[:rows], sine_all[:rows]
    allowed = (key_pos[None, :] <= positions[:, None]) | (key_pos[None, :] < prefix_length[0])
    bias = jnp.where(allowed, 0.0, masked_score).astype(f32)

    mask = (jnp.arange(codes)[None, None, :] // rank == adapter_all[:, None, None]).astype(bf16)
    mask = jnp.broadcast_to(mask, (holders, capacity, codes)).reshape(-1, codes)
    inner_down = flat_down(mlp_in_down).reshape(codes, width)
    outer_up = mlp_out_up.reshape(codes, width)
    inner_up = mlp_in_up.reshape(codes, 2, copies, size, share)
    inner_up = lax.dynamic_index_in_dim(inner_up, part, 2, keepdims=False)
    inner_up = lax.dynamic_index_in_dim(inner_up, spot, 2, keepdims=False).reshape(codes, 2 * share)
    outer_down = flat_down(mlp_out_down).reshape(codes, copies, size, share)
    outer_down = lax.dynamic_index_in_dim(outer_down, part, 1, keepdims=False)
    outer_down = lax.dynamic_index_in_dim(outer_down, spot, 1, keepdims=False)

    places = [place_mlp] + [slot_layout(r, experts, capacity) for r in routes_there[1:]]
    query_rows = after(query_rows, *normed_parts[1:])
    query_parts = nn(query_rows.reshape(-1, width), query_full).astype(bf16)
    query_home = home_join(query_parts.reshape(holders, capacity, -1), experts, copies)
    pairs, pair_low = project_pairs(
        normed_parts, pair_weight, pair_down, pair_up, cosine_all, sine_all
    )
    output_own = after(output_weight[0], pair_weight, query_home, *early[1:])
    output_full = lax.all_gather(output_own, "seq", axis=0, tiled=True)
    grad_rows = [grad_own.reshape(-1, width)]
    for d in range(1, size):
        sent = grad_parts[d] if d < 2 else after(grad_parts[d], pairs)
        sent = tn(either(places[d]), sent).astype(bf16)
        grad_rows.append(send_full(sent, experts, copies).reshape(-1, width))
    attended, output_slots, query_rot, totals = attend(
        query_home, place, query_low, query_upper, cosine, sine, pairs, bias
    )

    output_rows = send_cut(output_slots, experts, copies)
    inner_sent = [cut_share(mlp_in_weight[0], (spot - d) % size, size) for d in range(size)]
    output_rows = after(output_rows, *grad_rows[:3], *inner_sent)
    output_parts = nn(output_rows.reshape(holders * capacity, -1), output_full).astype(bf16)
    far = size // 2
    distances = [d for d in range(1, size) if d != far] + ([far] if size > 1 else [])
    inner_parts = list(inner_sent)
    for d in distances[:1]:
        inner_parts[d] = shifted(after(inner_sent[d], output_full), d, size)
    output_home = home_add(output_parts.reshape(holders, capacity, width), experts, copies)
    output_low = nt(attended, output_lower).astype(bf16)
    branch = nn(place, output_home) + nn(output_low, output_upper)
    branch = branch.reshape(2, rows, width)
    middle = inputs + gates[:, :1] * branch[0] + gates[:, 1:] * branch[1]
    middle_scale = norm_scale(middle)
    normed_mlp = (middle * middle_scale * mlp_gain).astype(bf16)
    mlp_gates, mlp_hits = gate_pair(nn(normed_mlp, mlp_router_weight), mlp_routes[0])

    lanes = jnp.pad(jnp.concatenate(halves(mlp_gates), axis=1), ((0, 0), (0, 124)))
    packet = jnp.concatenate([normed_mlp, lanes], axis=1)
    packet = after(packet, *(inner_parts[d] for d in distances[:1]))
    packet_all = lax.all_gather(packet, "seq", axis=0, tiled=True)
    before = packet_all
    for d in distances[1:]:
        before = inner_parts[d] = shifted(after(inner_sent[d], before), d, size)
    packets = [packet] + [
        lax.dynamic_slice_in_dim(packet_all, (spot + d) % size * rows, rows, 0)
        for d in range(1, size)
    ]
    gates_there = [
        (p[:, width : width + 2].astype(f32) + p[:, width + 2 : width + 4].astype(f32)).T.reshape(-1, 1)
        for p in packets
    ]
    combines = [either((places[d].astype(f32) * gates_there[d]).astype(bf16)) for d in range(size)]
    order = list(range(size))
    outer_codes = [nt(got, outer_up).astype(bf16) * mask for got in grad_rows]
    hidden_grads = [
        (nt(got, outer_full) + nn(code, outer_down)).astype(bf16)
        for got, code in zip(grad_rows, outer_codes)
    ]
    gate_slots = jnp.stack(
        [jnp.sum(places[d].astype(f32) * gates_there[d], axis=0) for d in range(size)]
    )
    gate_slots = gate_slots.reshape(size, experts, capacity).transpose(1, 0, 2)
    gate_slots = exchange(jnp.repeat(gate_slots, copies, axis=0))

    def send_rows(d, *earlier):
        sent = tn(either(places[d]), after(packets[d][:, :width], *earlier)).astype(bf16)
        return send_full(sent, experts, copies).reshape(-1, width)

    def work(d, got):
        return expert_block(got, hidden_grads[d], mask, inner_up, inner_down, inner_parts, spot)

    def rows_home(d, row_grad, *earlier):
        home = home_add(row_grad.reshape(holders, capacity, -1), experts, copies)
        home = after(home, *earlier)
        row_sum = nn(combines[d], home[:, :width])
        gate_sum = nn(places[d], home[:, width:])
        lanes = gate_sum[:rows] + jnp.roll(gate_sum[rows:], 2, axis=1)
        row_back = jnp.concatenate([row_sum, lanes], axis=1)
        return home, shifted(row_back.astype(bf16), -d % size, size) if d else row_back

    got_rows = [send_rows(0)]
    for d in order[1:]:
        earlier = [inner_parts[distances[min(d - 1, size - 2)]]]
        got_rows.append(send_rows(d, got_rows[-1], *earlier))
    turns = order[1:] + [0]
    kept, row_homes, row_backs, row_total = {}, [], [], None
    ready = got_rows[1:-1] + hidden_grads
    for d in turns:
        kept[d] = work(d, after(got_rows[d], *ready))
        ready = [kept[d][0]]
        row_home, row_back = rows_home(d, kept[d][0], *(row_backs if d == 0 else []))
        row_homes.append(row_home)
        row_backs.append(row_back)
        row_back = row_back.astype(f32)
        row_total = row_back if row_total is None else row_total + row_back
    gate_sum = row_total[:, width : width + 4]
    row_total = row_total[:, :width]
    mlp_gate_grad = gate_sum.reshape(rows, 2, 2).sum(2)
    mlp_logit_grad = gate_back(mlp_gates, mlp_hits, mlp_gate_grad)

    outer_lows, sums = [], None
    for d in order:
        _, activated, pre_grad, code, back = kept[d]
        there = row_homes[min(d, size - 2)] if size > 1 else row_homes[0]
        activated, pre_grad = after(activated, there), after(pre_grad, there)
        outer_low = nt(activated, outer_down).astype(bf16) * mask
        outer_lows.append(outer_low)
        scale = gate_slots[:, d, :].reshape(-1, 1)

        def scaled(array):
            return (array.astype(f32) * scale).astype(bf16)

        new = (
            tn(scaled(code), pre_grad),
            tn(scaled(outer_codes[d]), activated),
            tn(scaled(back), got_rows[d]),
            tn(scaled(outer_low), grad_rows[d]),
        )
        sums = new if sums is None else tuple(a + b for a, b in zip(sums, new))


    inner_up_sum, outer_down_sum, inner_down_sum, outer_up_sum = sums

    def widened(array):
        if copies == 1:
            return array
        whole = jnp.zeros((codes, copies, array.shape[1]), f32)
        whole = lax.dynamic_update_index_in_dim(whole, array, part, 1)
        return whole.reshape(codes, -1)

    wide = [widened(inner_up_sum), widened(outer_down_sum), inner_down_sum, outer_up_sum]
    ends = [sum(a.shape[1] for a in wide[: k + 1]) for k in range(3)]
    mlp_own = after(jnp.concatenate(wide, axis=1).astype(bf16), row_home)
    mlp_sums = lax.psum_scatter(mlp_own, "dp", scatter_dimension=0, tiled=True)

    def down_back(d, before_matmul, before_sending):
        activated = after(kept[d][1], before_matmul)
        down = (nn(activated, outer_full) + nn(outer_lows[d], outer_up)).astype(bf16)
        down = after(down, before_sending).reshape(holders, capacity, width)
        home = home_add(down, experts, copies)
        made = nn(combines[d], home)
        return home, shifted(made.astype(bf16), -d % size, size).astype(f32) if d else made

    down_turns = order[1:] + [0]
    down_home, down_total = down_back(down_turns[0], row_homes[-2], row_home)

    normed_mlp_grad = row_total + nt(mlp_logit_grad.astype(bf16), mlp_router_weight)
    middle_grad = norm_back(middle, middle_scale, mlp_gain, normed_mlp_grad)
    middle_grad = middle_grad + out_grad[0].astype(f32)
    middle_low = middle_grad.astype(bf16)
    branch_sent = tn(place_any, after(middle_low, down_home)).astype(bf16)
    branch_rows = send_full(branch_sent, experts, copies)
    mlp_sums = lax.all_gather(after(mlp_sums, branch_rows), ("seq", "dp"), axis=0, tiled=True)
    head_parts = nt(branch_rows.reshape(-1, width), output_full).astype(bf16)
    head_home = home_join(head_parts.reshape(holders, capacity, -1), experts, copies)
    down_home, made = down_back(down_turns[1], head_parts, head_home)
    down_total = down_total + made
    head_home = after(head_home, mlp_own)
    gate_grad = jnp.sum(middle_grad[None] * branch, axis=2).T
    logit_grad = gate_back(gates, hits, gate_grad)
    gate_column = gates.T.reshape(-1, 1)
    output_low_grad = nt(middle_low, output_upper)
    output_low_back = output_low_grad.astype(bf16)
    output_low_scaled = (jnp.tile(output_low_grad, (2, 1)) * gate_column).astype(bf16)
    output_lower_grad = tn(output_low_scaled, attended)
    output_low_sum = (output_low.astype(f32) * gate_column).reshape(2, rows, rank).sum(0)
    output_upper_grad = tn(output_low_sum.astype(bf16), middle_low)

    def over_sequences(mine, widths):
        every = lax.all_gather(mine, ("seq", "dp"), axis=0, tiled=False)
        every = every.reshape(size, holders, rank, -1)
        return gather_adapters(every, adapter_all, adapters, widths)

    key_grad, value_grad, query_slots, query_sum = attend_back(
        query_rot,
        pairs,
        bias,
        totals,
        head_home,
        place,
        gate_column,
        output_low_back,
        output_lower,
        cosine,
        sine,
        cosine_all,
        sine_all,
    )
    query_back = send_cut(after(query_slots, down_home), experts, copies)
    input_parts = nt(query_back.reshape(holders * capacity, -1), query_full).astype(bf16)
    input_home = home_add(input_parts.reshape(holders, capacity, width), experts, copies)
    mlp_sums = after(mlp_sums, input_parts)
    if copies == 1 and share % 128 == 0:
        inner_up_grad, outer_down_grad, inner_down_grad, outer_up_grad = unpack_sums(
            mlp_sums.reshape(size, adapters, rank, -1), share, width
        )
    else:
        mlp_sums = mlp_sums.astype(f32).reshape(size, codes, -1)
        inner_up_grad, outer_down_grad, inner_down_grad, outer_up_grad = jnp.split(mlp_sums, ends, axis=2)
        inner_up_grad = inner_up_grad.reshape(size, codes, copies, 2, share).transpose(1, 3, 2, 0, 4)
        inner_up_grad = inner_up_grad.reshape(adapters, rank, -1)
        outer_down_grad = outer_down_grad.reshape(size, codes, copies, share).transpose(1, 2, 0, 3)
        outer_down_grad = outer_down_grad.reshape(adapters, rank, -1)
        inner_down_grad = jnp.sum(inner_down_grad, 0).reshape(adapters, rank, width)
        outer_up_grad = jnp.sum(outer_up_grad, 0).reshape(adapters, rank, width)
    half = key_grad.shape[1]
    pair_low_grad = nt(key_grad, pair_up[:, :half]) + nt(value_grad, pair_up[:, half:])
    pair_low_grad = pair_low_grad.astype(bf16)
    pair_upper_grad = jnp.concatenate([tn(pair_low, key_grad), tn(pair_low, value_grad)], axis=1)
    pair_lower_grad = sum(
        tn(pair_low_grad[d * rows : (d + 1) * rows], normed_parts[d]) for d in range(size)
    )
    query_low_grad = nt(query_sum, query_upper).astype(bf16)
    query_upper_grad = tn(query_low, query_sum)
    query_lower_grad = tn(query_low_grad, normed)
    sequence_grads = [
        pair_lower_grad,
        pair_upper_grad,
        query_lower_grad,
        query_upper_grad,
        output_lower_grad,
        output_upper_grad,
    ]
    joined = jnp.concatenate([a.reshape(rank, size, -1) for a in sequence_grads], axis=2)
    joined = joined.transpose(1, 0, 2)
    normed_grads = pair_back(key_grad, value_grad, pair_weight, pair_low_grad, pair_down)
    mine = picked(joined, spot)
    back_parts = []
    for d in range(1, size):
        theirs = picked(joined, (spot + d) % size).astype(bf16).reshape(-1, width)
        theirs = jnp.pad(theirs, ((0, -theirs.shape[0] % 16), (0, 0)))
        packet = jnp.concatenate([normed_grads[d * rows : (d + 1) * rows], theirs], axis=0)
        packet = after(shifted(packet, -d % size, size), inner_up_grad)
        back_parts.append(packet[:rows])
        adapter_rows = mine.size // width
        mine = mine + packet[rows : rows + adapter_rows].astype(f32).reshape(mine.shape)
    mine = after(mine.astype(bf16), mlp_sums)
    late = over_sequences(mine, [a.shape[1] for a in sequence_grads])
    normed_grad = normed_grads[:rows].astype(f32) + sum(back.astype(f32) for back in back_parts)
    normed_grad = normed_grad + nn(place_any, input_home) + nn(query_low_grad, query_lower)
    normed_grad = normed_grad + nt(logit_grad.astype(bf16), router_weight)
    input_grad = norm_back(inputs, input_scale, norm_gain, normed_grad) + middle_grad

    for d in down_turns[2:]:
        down_home, made = down_back(d, query_slots, input_home)
        down_total = down_total + made
    result = (middle + down_total).astype(bf16)

    return (
        result[None],
        input_grad[None],
        flat_down(late[0]),
        late[1],
        flat_down(late[2]),
        late[3],
        flat_down(late[4]),
        late[5],
        flat_down(inner_down_grad),
        inner_up_grad,
        flat_down(outer_down_grad),
        outer_up_grad,
    )


def solution(mesh):
    split = P("dp", "seq", None)
    placed = (
        (split, P(), P("seq", None), P(), split, split, P(), P(), split, split)
        + (P(),) * 10
        + (split, split, P("dp"), P("dp"), split)
    )
    return jax.shard_map(
        body,
        mesh=mesh,
        in_specs=placed,
        out_specs=(split, split) + (P(),) * 10,
        check_vma=False,
    )
```

```python
import functools
import math

import jax
import jax.numpy as jnp
import numpy as np
from jax import lax
from jax.experimental import pallas as pl
from jax.experimental.pallas import tpu as pltpu
from jax.sharding import PartitionSpec as P

KV_HEADS = 16
HD = 128

norm_eps = 1e-05
rope_base = 10000.0
masked_score = -1e30
vmem_bytes = 48 * 2**20

bf16 = jnp.bfloat16
f32 = jnp.float32


def product(left, right, left_dim, right_dim):
    return lax.dot_general(
        left, right, (((left_dim,), (right_dim,)), ((), ())), preferred_element_type=f32
    )


def nn(left, right):
    return product(left, right, 1, 0)


def nt(left, right):
    return product(left, right, 1, 1)


def tn(left, right):
    return product(left, right, 0, 0)


def pair_kernel(count, key_blocks, *refs):
    normed_refs = refs[:count]
    w_ref, down_ref, up_ref, cos_ref, sin_ref, out_ref, low_ref = refs[count:]
    rows = normed_refs[0].shape[0]
    step = pl.program_id(0)

    @pl.when(step == 0)
    def _():
        for k in range(count):
            low_ref[pl.ds(k * rows, rows), :] = nt(normed_refs[k][...], down_ref[...]).astype(bf16)

    for k in range(count):
        part = pl.ds(k * rows, rows)
        made = nn(normed_refs[k][...], w_ref[0]) + nn(low_ref[part, :], up_ref[...])

        @pl.when(step < key_blocks)
        def _():
            for start in range(0, made.shape[1], HD):
                head = made[:, start : start + HD]
                turned = head * cos_ref[part, :] + pltpu.roll(head, HD // 2, 1) * sin_ref[part, :]
                out_ref[part, start : start + HD] = turned.astype(bf16)

        @pl.when(step >= key_blocks)
        def _():
            out_ref[part, :] = made.astype(bf16)


def project_pairs(normed_parts, weight, down, upper, cosine, sine):
    count = len(normed_parts)
    rows, width = normed_parts[0].shape
    blocks, _, block = weight.shape
    columns = blocks * block
    whole = lambda array: pl.BlockSpec(array.shape, lambda i: (0, 0))
    return pl.pallas_call(
        functools.partial(pair_kernel, count, blocks // 2),
        grid=(blocks,),
        in_specs=[whole(n) for n in normed_parts]
        + [
            pl.BlockSpec((1, width, block), lambda i: (i, 0, 0)),
            whole(down),
            pl.BlockSpec((upper.shape[0], block), lambda i: (0, i)),
            whole(cosine),
            whole(sine),
        ],
        out_specs=[
            pl.BlockSpec((count * rows, block), lambda i: (0, i)),
            pl.BlockSpec((count * rows, down.shape[0]), lambda i: (0, 0)),
        ],
        out_shape=[
            jax.ShapeDtypeStruct((count * rows, columns), bf16),
            jax.ShapeDtypeStruct((count * rows, down.shape[0]), bf16),
        ],
        compiler_params=pltpu.CompilerParams(vmem_limit_bytes=vmem_bytes),
        cost_estimate=pl.CostEstimate(
            flops=2 * count * rows * width * columns,
            bytes_accessed=2 * width * columns,
            transcendentals=0,
        ),
        name="pairs",
    )(*normed_parts, weight, down, upper, cosine, sine)


def pair_back_kernel(key_blocks, key_ref, value_ref, w_ref, low_ref, down_ref, out_ref, sum_ref):
    step = pl.program_id(0)

    @pl.when(step == 0)
    def _():
        sum_ref[...] = nn(low_ref[...], down_ref[...])

    @pl.when(step < key_blocks)
    def _():
        sum_ref[...] += nt(key_ref[...], w_ref[0])

    @pl.when(step >= key_blocks)
    def _():
        sum_ref[...] += nt(value_ref[...], w_ref[0])

    @pl.when(step == pl.num_programs(0) - 1)
    def _():
        out_ref[...] = sum_ref[...].astype(bf16)


def pair_back(key_grad, value_grad, weight, low_grad, down):
    blocks, width, block = weight.shape
    rows = key_grad.shape[0]
    half = blocks // 2
    whole = lambda array: pl.BlockSpec(array.shape, lambda i: (0, 0))
    return pl.pallas_call(
        functools.partial(pair_back_kernel, half),
        grid=(blocks,),
        in_specs=[
            pl.BlockSpec((rows, block), lambda i: (0, jnp.minimum(i, half - 1))),
            pl.BlockSpec((rows, block), lambda i: (0, jnp.maximum(i - half, 0))),
            pl.BlockSpec((1, width, block), lambda i: (i, 0, 0)),
            whole(low_grad),
            whole(down),
        ],
        out_specs=pl.BlockSpec((rows, width), lambda i: (0, 0)),
        out_shape=jax.ShapeDtypeStruct((rows, width), bf16),
        scratch_shapes=[pltpu.VMEM((rows, width), f32)],
        compiler_params=pltpu.CompilerParams(vmem_limit_bytes=vmem_bytes),
        cost_estimate=pl.CostEstimate(
            flops=2 * rows * width * blocks * block,
            bytes_accessed=2 * width * blocks * block,
            transcendentals=0,
        ),
        name="pair_back",
    )(key_grad, value_grad, weight, low_grad, down)


def attend_kernel(
    scale,
    home_ref,
    place_ref,
    low_ref,
    up_ref,
    cos_ref,
    sin_ref,
    key_ref,
    value_ref,
    bias_ref,
    attended_ref,
    slots_ref,
    query_ref,
    total_ref,
):
    rows = cos_ref.shape[0]
    base = nn(place_ref[...], home_ref[...])
    extra = nn(low_ref[...], up_ref[...])
    keys, values = key_ref[...], value_ref[...]
    for route in range(2):
        part = pl.ds(route * rows, rows)
        query = base[route * rows : (route + 1) * rows] + extra
        query = query * cos_ref[...] + pltpu.roll(query, HD // 2, 1) * sin_ref[...]
        query = query.astype(bf16)
        query_ref[part, :] = query
        scores = nt(query, keys) * scale + bias_ref[...]
        highest = jnp.max(scores, axis=1, keepdims=True)
        weights = jnp.exp(scores - highest)
        total = jnp.sum(weights, axis=1, keepdims=True)
        attended = nn(weights.astype(bf16), values) / total
        attended_ref[part, :] = attended.astype(bf16)
        total_ref[0, part, :] = highest + jnp.log(total)
    slots_ref[...] = tn(place_ref[...], attended_ref[...]).astype(bf16)


def attend(home, place, low, upper, cosine, sine, pairs, bias):
    rows2, slots = place.shape
    rows, length = bias.shape
    heads = home.shape[1] // HD
    kv_heads = pairs.shape[1] // (2 * HD)
    whole = lambda array: pl.BlockSpec(array.shape, lambda h: (0, 0))
    return pl.pallas_call(
        functools.partial(attend_kernel, 1.0 / math.sqrt(HD)),
        grid=(heads,),
        in_specs=[
            pl.BlockSpec((slots, HD), lambda h: (0, h)),
            whole(place),
            whole(low),
            pl.BlockSpec((upper.shape[0], HD), lambda h: (0, h)),
            whole(cosine),
            whole(sine),
            pl.BlockSpec((length, HD), lambda h: (0, h)),
            pl.BlockSpec((length, HD), lambda h: (0, kv_heads + h)),
            whole(bias),
        ],
        out_specs=[
            pl.BlockSpec((rows2, HD), lambda h: (0, h)),
            pl.BlockSpec((slots, HD), lambda h: (0, h)),
            pl.BlockSpec((rows2, HD), lambda h: (0, h)),
            pl.BlockSpec((1, rows2, 1), lambda h: (h, 0, 0)),
        ],
        out_shape=[
            jax.ShapeDtypeStruct((rows2, heads * HD), bf16),
            jax.ShapeDtypeStruct((slots, heads * HD), bf16),
            jax.ShapeDtypeStruct((rows2, heads * HD), bf16),
            jax.ShapeDtypeStruct((heads, rows2, 1), f32),
        ],
        compiler_params=pltpu.CompilerParams(vmem_limit_bytes=vmem_bytes),
        cost_estimate=pl.CostEstimate(
            flops=4 * heads * rows2 * length * HD,
            bytes_accessed=4 * length * heads * HD,
            transcendentals=heads * rows2 * length,
        ),
        name="attend",
    )(home, place, low, upper, cosine, sine, pairs, pairs, bias)


def attend_back_kernel(
    scale,
    query_ref,
    key_ref,
    value_ref,
    bias_ref,
    total_ref,
    home_ref,
    place_ref,
    gate_ref,
    low_ref,
    down_ref,
    cos_ref,
    sin_ref,
    cos_all_ref,
    sin_all_ref,
    key_grad_ref,
    value_grad_ref,
    slots_ref,
    sum_ref,
    turned_ref,
):
    rows = cos_ref.shape[0]
    base = nn(place_ref[...], home_ref[...])
    extra = nn(low_ref[...], down_ref[...])
    keys, values = key_ref[...], value_ref[...]
    key_grad = value_grad = None
    for route in range(2):
        part = pl.ds(route * rows, rows)
        query = query_ref[part, :]
        grad = (base[route * rows : (route + 1) * rows] + extra) * gate_ref[part, :]
        grad = grad.astype(bf16)
        scores = nt(query, keys) * scale + bias_ref[...]
        weights = jnp.exp(scores - total_ref[0, part, :])
        weight_grad = nt(grad, values)
        mean_grad = jnp.sum(weights * weight_grad, axis=1, keepdims=True)
        score_grad = (weights * (weight_grad - mean_grad)).astype(bf16)
        query_grad = nn(score_grad, keys) * scale
        query_grad = query_grad * cos_ref[...] - pltpu.roll(query_grad, HD // 2, 1) * sin_ref[...]
        turned_ref[part, :] = query_grad.astype(bf16)
        key_part = tn(score_grad, query)
        value_part = tn(weights.astype(bf16), grad)
        key_grad = key_part if route == 0 else key_grad + key_part
        value_grad = value_part if route == 0 else value_grad + value_part
    key_grad = key_grad * scale
    key_grad = key_grad * cos_all_ref[...] - pltpu.roll(key_grad, HD // 2, 1) * sin_all_ref[...]
    key_grad_ref[...] = key_grad.astype(bf16)
    value_grad_ref[...] = value_grad.astype(bf16)
    slots_ref[...] = tn(place_ref[...], turned_ref[...]).astype(bf16)
    first = turned_ref[pl.ds(0, rows), :].astype(f32)
    sum_ref[...] = (first + turned_ref[pl.ds(rows, rows), :].astype(f32)).astype(bf16)


def attend_back(query, pairs, bias, totals, home, place, gates, low, down, cosine, sine, cosine_all, sine_all):
    rows2, slots = place.shape
    rows, length = bias.shape
    heads = home.shape[1] // HD
    kv_heads = pairs.shape[1] // (2 * HD)
    whole = lambda array: pl.BlockSpec(array.shape, lambda h: (0, 0))
    return pl.pallas_call(
        functools.partial(attend_back_kernel, 1.0 / math.sqrt(HD)),
        grid=(heads,),
        in_specs=[
            pl.BlockSpec((rows2, HD), lambda h: (0, h)),
            pl.BlockSpec((length, HD), lambda h: (0, h)),
            pl.BlockSpec((length, HD), lambda h: (0, kv_heads + h)),
            whole(bias),
            pl.BlockSpec((1, rows2, 1), lambda h: (h, 0, 0)),
            pl.BlockSpec((slots, HD), lambda h: (0, h)),
            whole(place),
            whole(gates),
            whole(low),
            pl.BlockSpec((down.shape[0], HD), lambda h: (0, h)),
            whole(cosine),
            whole(sine),
            whole(cosine_all),
            whole(sine_all),
        ],
        out_specs=[
            pl.BlockSpec((length, HD), lambda h: (0, h)),
            pl.BlockSpec((length, HD), lambda h: (0, h)),
            pl.BlockSpec((slots, HD), lambda h: (0, h)),
            pl.BlockSpec((rows, HD), lambda h: (0, h)),
        ],
        out_shape=[
            jax.ShapeDtypeStruct((length, heads * HD), bf16),
            jax.ShapeDtypeStruct((length, heads * HD), bf16),
            jax.ShapeDtypeStruct((slots, heads * HD), bf16),
            jax.ShapeDtypeStruct((rows, heads * HD), bf16),
        ],
        scratch_shapes=[pltpu.VMEM((rows2, HD), bf16)],
        compiler_params=pltpu.CompilerParams(vmem_limit_bytes=vmem_bytes),
        cost_estimate=pl.CostEstimate(
            flops=10 * heads * rows2 * length * HD,
            bytes_accessed=8 * length * heads * HD,
            transcendentals=heads * rows2 * length,
        ),
        name="attend_back",
    )(query, pairs, pairs, bias, totals, home, place, gates, low, down, cosine, sine, cosine_all, sine_all)


def exchange(buffer):
    return lax.all_to_all(buffer, "dp", split_axis=0, concat_axis=0, tiled=True)


def in_order(parts, spot):
    count = len(parts)
    twice = jnp.concatenate(parts + parts, axis=0)
    rows = parts[0].shape[0]
    return lax.dynamic_slice_in_dim(twice, (count - spot) % count * rows, count * rows, 0)


def shifted(array, shift, size):
    if shift == 0:
        return array
    return lax.ppermute(array, "seq", [(k, (k - shift) % size) for k in range(size)])


def send_full(slots, experts, copies):
    buffer = slots.reshape(experts, slots.shape[0] // experts, slots.shape[1])
    if copies > 1:
        buffer = jnp.repeat(buffer, copies, axis=0)
    return exchange(buffer)


def send_cut(slots, experts, copies):
    buffer = slots.reshape(experts, slots.shape[0] // experts, slots.shape[1])
    if copies > 1:
        _, rows, columns = buffer.shape
        buffer = buffer.reshape(experts, rows, copies, columns // copies).transpose(0, 2, 1, 3)
        buffer = buffer.reshape(experts * copies, rows, columns // copies)
    return exchange(buffer)


def home_join(parts, experts, copies):
    home = exchange(parts)
    _, rows, columns = home.shape
    if copies > 1:
        home = home.reshape(experts, copies, rows, columns).transpose(0, 2, 1, 3)
    return home.reshape(experts * rows, copies * columns)


def home_add(parts, experts, copies):
    home = exchange(parts)
    _, rows, columns = home.shape
    if copies > 1:
        home = home.reshape(experts, copies, rows, columns).astype(f32)
        home = jnp.sum(home, axis=1).astype(parts.dtype)
    return home.reshape(experts * rows, columns)


def slot_layout(route_ids, experts, capacity):
    flat = route_ids.T.reshape(-1)
    count = flat.shape[0]
    hits = flat[:, None] == jnp.arange(experts)[None, :]
    earlier = jnp.arange(count)[:, None] > jnp.arange(count)[None, :]
    before = nn(earlier.astype(bf16), hits.astype(bf16))
    rank = jnp.sum(jnp.where(hits, before, 0.0), axis=1).astype(jnp.int32)
    slot = flat * capacity + rank
    return (slot[:, None] == jnp.arange(experts * capacity)[None, :]).astype(bf16)


def either(place):
    rows = place.shape[0] // 2
    return place[:rows] + place[rows:]


def norm_back(values, scale, gain, grad):
    weighted = grad * gain
    mean = jnp.mean(weighted * values, axis=-1, keepdims=True)
    return weighted * scale - values * (scale * scale * scale * mean)


def norm_scale(values):
    return lax.rsqrt(jnp.mean(values * values, axis=-1, keepdims=True) + norm_eps)


def gate_pair(logits, route_ids):
    hits = (route_ids[:, :, None] == jnp.arange(logits.shape[1])).astype(f32)
    chosen = jnp.sum(hits * logits[:, None, :], axis=2)
    weights = jnp.exp(chosen - jnp.max(chosen, axis=1, keepdims=True))
    return weights / jnp.sum(weights, axis=1, keepdims=True), hits


def gate_back(gates, hits, grad):
    mean = jnp.sum(gates * grad, axis=1, keepdims=True)
    return jnp.sum((gates * (grad - mean))[:, :, None] * hits, axis=1)


def rope_full(length, start):
    half = HD // 2
    frequency = rope_base ** (-np.arange(half) / half)
    angles = np.arange(length)[:, None] * frequency[None, :]
    cosine, sine = np.cos(angles), np.sin(angles)
    tables = np.concatenate([cosine, cosine, -sine, sine], 1).astype(np.float32)
    tables = jnp.asarray(np.concatenate([tables, tables], 0))
    tables = lax.dynamic_slice_in_dim(tables, start, length, 0)
    return tables[:, :HD], tables[:, HD:]


def after(array, *earlier):
    return lax.optimization_barrier((array,) + earlier)[0]


def cut_kernel(target_ref, in_ref, out_ref):
    out_ref[...] = in_ref[...]


def cut_share(weight, target, size):
    rows, columns = weight.shape
    share = columns // 2 // size
    if share % 128:
        cut = weight.reshape(rows, 2, size, share)
        return lax.dynamic_index_in_dim(cut, target, 2, keepdims=False).reshape(rows, 2 * share)
    return pl.pallas_call(
        cut_kernel,
        grid_spec=pltpu.PrefetchScalarGridSpec(
            num_scalar_prefetch=1,
            grid=(2,),
            in_specs=[pl.BlockSpec((rows, share), lambda i, t: (0, i * size + t[0]))],
            out_specs=pl.BlockSpec((rows, share), lambda i, t: (0, i)),
        ),
        out_shape=jax.ShapeDtypeStruct((rows, 2 * share), bf16),
        compiler_params=pltpu.CompilerParams(vmem_limit_bytes=vmem_bytes),
        name="cut",
    )(target.reshape(1).astype(jnp.int32), weight)


def unpack_kernel(size, share, in_ref, inner_up_ref, outer_down_ref, inner_down_ref, outer_up_ref):
    spot = pl.program_id(1)
    got = in_ref[0, 0].astype(f32)
    hidden = size * share
    width = inner_down_ref.shape[2]
    start = pl.multiple_of(spot * share, 128)
    inner_up_ref[0, :, pl.ds(start, share)] = got[:, :share]
    inner_up_ref[0, :, pl.ds(pl.multiple_of(hidden + start, 128), share)] = got[:, share : 2 * share]
    outer_down_ref[0, :, pl.ds(start, share)] = got[:, 2 * share : 3 * share]
    inner_down = got[:, 3 * share : 3 * share + width]
    outer_up = got[:, 3 * share + width :]

    @pl.when(spot == 0)
    def _():
        inner_down_ref[0] = inner_down
        outer_up_ref[0] = outer_up

    @pl.when(spot > 0)
    def _():
        inner_down_ref[0] += inner_down
        outer_up_ref[0] += outer_up


def unpack_sums(sums, share, width):
    size, adapters, rank, columns = sums.shape
    hidden = size * share
    shapes = [2 * hidden, hidden, width, width]
    return pl.pallas_call(
        functools.partial(unpack_kernel, size, share),
        grid=(adapters, size),
        in_specs=[pl.BlockSpec((1, 1, rank, columns), lambda a, k: (k, a, 0, 0))],
        out_specs=[pl.BlockSpec((1, rank, n), lambda a, k: (a, 0, 0)) for n in shapes],
        out_shape=[jax.ShapeDtypeStruct((adapters, rank, n), f32) for n in shapes],
        compiler_params=pltpu.CompilerParams(vmem_limit_bytes=vmem_bytes),
        cost_estimate=pl.CostEstimate(
            flops=0, bytes_accessed=12 * adapters * rank * (3 * hidden + 2 * width), transcendentals=0
        ),
        name="unpack",
    )(sums)


def gather_adapters_kernel(adapters, ids_ref, in_ref, *out_refs):
    holders = in_ref.shape[1]
    start = 0
    for out_ref in out_refs:
        columns = out_ref.shape[2]
        parts = [in_ref[0, k, :, start : start + columns].astype(f32) for k in range(holders)]
        for a in range(adapters):
            total = None
            for k in range(holders):
                one = jnp.where(ids_ref[k] == a, parts[k], 0.0)
                total = one if total is None else total + one
            out_ref[a] = total
        start += columns


def gather_adapters(every, adapter_all, adapters, widths):
    size, holders, rank, columns = every.shape
    return pl.pallas_call(
        functools.partial(gather_adapters_kernel, adapters),
        grid_spec=pltpu.PrefetchScalarGridSpec(
            num_scalar_prefetch=1,
            grid=(size,),
            in_specs=[pl.BlockSpec((1, holders, rank, columns), lambda k, s: (k, 0, 0, 0))],
            out_specs=[
                pl.BlockSpec((adapters, rank, n // size), lambda k, s: (0, 0, k)) for n in widths
            ],
        ),
        out_shape=[jax.ShapeDtypeStruct((adapters, rank, n), f32) for n in widths],
        compiler_params=pltpu.CompilerParams(vmem_limit_bytes=vmem_bytes),
        name="gather_adapters",
    )(adapter_all, every)


def silu_parts(gate_part, up_part, hidden_grad):
    sigmoid = 1.0 / (1.0 + jnp.exp(-gate_part))
    active = gate_part * sigmoid
    activated = (active * up_part).astype(bf16)
    gate_grad = hidden_grad * up_part * sigmoid * (1.0 + gate_part * (1.0 - sigmoid))
    return activated, gate_grad.astype(bf16), (hidden_grad * active).astype(bf16)


def halves(value):
    high = value.astype(bf16)
    return high, (value - high.astype(f32)).astype(bf16)


def expert_kernel(size, share, spot_ref, x_ref, hidden_ref, mask_ref, up_ref, down_ref, *refs):
    w_refs = refs[:size]
    row_ref, active_ref, pre_ref, code_ref, back_ref = refs[size:]
    depth = w_refs[0].shape[0]
    width = size * depth
    columns = [pl.ds(pl.multiple_of((spot_ref[0] + k) % size * depth, 128), depth) for k in range(size)]
    code = nt(x_ref[...], down_ref[...]).astype(bf16) * mask_ref[...]
    code_ref[...] = code
    sums = None
    for start in range(0, share, 256):
        end = min(start + 256, share)

        def hidden(first, last):
            made = nn(code, up_ref[:, first:last])
            for k in range(size):
                made = made + nn(x_ref[:, columns[k]], w_refs[k][:, first:last])
            return made

        gate_part, up_part = hidden(start, end), hidden(share + start, share + end)
        hidden_grad = hidden_ref[:, start:end].astype(f32)
        activated, gate_grad, up_grad = silu_parts(gate_part, up_part, hidden_grad)
        active_ref[:, start:end] = activated
        pre_ref[:, start:end] = gate_grad
        pre_ref[:, share + start : share + end] = up_grad
        part = jnp.sum(activated.astype(f32) * hidden_grad, axis=1, keepdims=True)
        sums = part if sums is None else sums + part
    back = nt(pre_ref[...], up_ref[...]).astype(bf16) * mask_ref[...]
    back_ref[...] = back
    for k in range(size):
        base = (spot_ref[0] + k) % size * depth
        for start in range(0, depth, 256):
            end = min(start + 256, depth)
            here = pl.ds(pl.multiple_of(base + start, 128), end - start)
            made = nt(pre_ref[...], w_refs[k][start:end, :]) + nn(back, down_ref[:, here])
            row_ref[:, here] = made.astype(bf16)
    high, low = halves(sums)
    lane = lax.broadcasted_iota(jnp.int32, (sums.shape[0], 128), 1)
    packed = jnp.where(lane == 0, high.astype(f32), jnp.where(lane == 1, low.astype(f32), 0.0))
    row_ref[:, width:] = packed.astype(bf16)


def expert_block(got, hidden_grad, mask, inner_up, inner_down, inner_parts, spot):
    size = len(inner_parts)
    rows, width = got.shape
    share = hidden_grad.shape[1]
    codes = mask.shape[1]
    if share % 128 or width // size % 256:
        code = nt(got, inner_down).astype(bf16) * mask
        inner_full = in_order(inner_parts, spot)
        pre = nn(got, inner_full) + nn(code, inner_up)
        hidden_float = hidden_grad.astype(f32)
        activated, gate_grad, up_grad = silu_parts(pre[:, :share], pre[:, share:], hidden_float)
        pre_grad = jnp.concatenate([gate_grad, up_grad], axis=1)
        back = nt(pre_grad, inner_up).astype(bf16) * mask
        row_grad = (nt(pre_grad, inner_full) + nn(back, inner_down)).astype(bf16)
        sums = jnp.stack(halves(jnp.sum(activated.astype(f32) * hidden_float, axis=1)), axis=1)
        row_grad = jnp.concatenate([row_grad, jnp.pad(sums, ((0, 0), (0, 126)))], axis=1)
        return row_grad, activated, pre_grad, code, back
    block = rows // 2
    ahead = lambda n: pl.BlockSpec((block, n), lambda i, s: (i, 0))
    whole = lambda array: pl.BlockSpec(array.shape, lambda i, s: (0, 0), pipeline_mode=pl.Buffered(1))
    shapes = [width + 128, share, 2 * share, codes, codes]
    return pl.pallas_call(
        functools.partial(expert_kernel, size, share),
        grid_spec=pltpu.PrefetchScalarGridSpec(
            num_scalar_prefetch=1,
            grid=(2,),
            in_specs=[ahead(width), ahead(share), ahead(codes), whole(inner_up), whole(inner_down)]
            + [whole(part) for part in inner_parts],
            out_specs=[ahead(n) for n in shapes],
        ),
        out_shape=[jax.ShapeDtypeStruct((rows, n), bf16) for n in shapes],
        compiler_params=pltpu.CompilerParams(vmem_limit_bytes=vmem_bytes),
        cost_estimate=pl.CostEstimate(
            flops=8 * rows * width * share,
            bytes_accessed=4 * width * share + 10 * rows * width,
            transcendentals=rows * share,
        ),
        name="experts",
    )(spot.reshape(1).astype(jnp.int32), got, hidden_grad, mask, inner_up, inner_down, *inner_parts)


def picked(lookup, index):
    return lax.dynamic_index_in_dim(lookup, index, 0, keepdims=False)


def body(
    tokens,
    norm_gain,
    key_value_weight,
    router_weight,
    query_weight,
    output_weight,
    mlp_gain,
    mlp_router_weight,
    mlp_in_weight,
    mlp_out_weight,
    key_value_down,
    key_value_up,
    query_down,
    query_up,
    output_down,
    output_up,
    mlp_in_down,
    mlp_in_up,
    mlp_out_down,
    mlp_out_up,
    routes,
    mlp_routes,
    adapter_index,
    prefix_length,
    out_grad,
):
    seqs, rows, width = tokens.shape
    assert seqs == 1
    size, spot = lax.axis_size("seq"), lax.axis_index("seq")
    holders, holder = lax.axis_size("dp"), lax.axis_index("dp")
    experts = router_weight.shape[1]
    copies = holders // experts
    part = holder % copies
    capacity = 3 * rows // 8
    length = rows * size
    adapters, _, rank = key_value_down.shape
    codes = adapters * rank
    hidden = mlp_in_weight.shape[2] // 2
    share = hidden // size

    def flat_down(lookup):
        return lookup.transpose(0, 2, 1)

    adapter = adapter_index[0]
    adapter_all = exchange(jnp.broadcast_to(adapter_index[None], (holders, 128)))[:, 0]
    inputs = tokens[0].astype(f32)
    input_scale = norm_scale(inputs)
    normed = (inputs * input_scale * norm_gain).astype(bf16)

    gates, hits = gate_pair(nn(normed, router_weight), routes[0])
    place = slot_layout(routes[0], experts, capacity)
    place_any = either(place)
    query_rows = send_full(tn(place_any, normed).astype(bf16), experts, copies)
    query_full = lax.all_gather(query_weight[0], "seq", axis=0, tiled=True)
    block = key_value_weight.shape[1] // holders
    pair_piece = lax.dynamic_slice_in_dim(key_value_weight, holder * block, block, 1)
    packet = jnp.concatenate([normed, pair_piece.reshape(-1, width)], axis=0)
    packets = [packet] + [shifted(packet, d, size) for d in range(1, size)]
    normed_parts = [normed] + [p[:rows] for p in packets[1:]]
    pieces = [pair_piece] + [p[rows:].reshape(-1, block) for p in packets[1:]]
    place_mlp = slot_layout(mlp_routes[0], experts, capacity)
    grad_own = send_full(tn(either(place_mlp), out_grad[0]).astype(bf16), experts, copies)
    pair_own = in_order(pieces, spot)
    pair_own = after(pair_own, query_full, query_rows, grad_own, adapter_all)
    pair_weight = lax.all_gather(pair_own, "dp", axis=0, tiled=False)
    lanes = jnp.pad(mlp_routes[0].astype(bf16), ((0, 0), (0, 126)))
    packet = jnp.concatenate([out_grad[0], lanes], axis=1)
    packet_late = after(packet, query_full)
    early = [packet] + [shifted(packet_late, d, size) for d in range(1, size)]
    grad_parts = [out_grad[0]] + [p[:, :width] for p in early[1:]]
    routes_there = [p[:, width : width + 2].astype(jnp.int32) for p in early]
    outer_full = mlp_out_weight[0]

    pair_down, pair_up = picked(flat_down(key_value_down), adapter), picked(key_value_up, adapter)
    query_lower, query_upper = picked(flat_down(query_down), adapter), picked(query_up, adapter)
    output_lower, output_upper = picked(flat_down(output_down), adapter), picked(output_up, adapter)
    query_low = nt(normed, query_lower).astype(bf16)
    positions = spot * rows + jnp.arange(rows)
    key_pos = (spot * rows + jnp.arange(length)) % length
    cosine_all, sine_all = rope_full(length, spot * rows)
    cosine, sine = cosine_all[:rows], sine_all[:rows]
    allowed = (key_pos[None, :] <= positions[:, None]) | (key_pos[None, :] < prefix_length[0])
    bias = jnp.where(allowed, 0.0, masked_score).astype(f32)

    mask = (jnp.arange(codes)[None, None, :] // rank == adapter_all[:, None, None]).astype(bf16)
    mask = jnp.broadcast_to(mask, (holders, capacity, codes)).reshape(-1, codes)
    inner_down = flat_down(mlp_in_down).reshape(codes, width)
    outer_up = mlp_out_up.reshape(codes, width)
    inner_up = mlp_in_up.reshape(codes, 2, copies, size, share)
    inner_up = lax.dynamic_index_in_dim(inner_up, part, 2, keepdims=False)
    inner_up = lax.dynamic_index_in_dim(inner_up, spot, 2, keepdims=False).reshape(codes, 2 * share)
    outer_down = flat_down(mlp_out_down).reshape(codes, copies, size, share)
    outer_down = lax.dynamic_index_in_dim(outer_down, part, 1, keepdims=False)
    outer_down = lax.dynamic_index_in_dim(outer_down, spot, 1, keepdims=False)

    places = [place_mlp] + [slot_layout(r, experts, capacity) for r in routes_there[1:]]
    query_rows = after(query_rows, *normed_parts[1:])
    query_parts = nn(query_rows.reshape(-1, width), query_full).astype(bf16)
    query_home = home_join(query_parts.reshape(holders, capacity, -1), experts, copies)
    pairs, pair_low = project_pairs(
        normed_parts, pair_weight, pair_down, pair_up, cosine_all, sine_all
    )
    output_own = after(output_weight[0], pair_weight, query_home, *early[1:])
    output_full = lax.all_gather(output_own, "seq", axis=0, tiled=True)
    grad_rows = [grad_own.reshape(-1, width)]
    for d in range(1, size):
        sent = grad_parts[d] if d < 2 else after(grad_parts[d], pairs)
        sent = tn(either(places[d]), sent).astype(bf16)
        grad_rows.append(send_full(sent, experts, copies).reshape(-1, width))
    attended, output_slots, query_rot, totals = attend(
        query_home, place, query_low, query_upper, cosine, sine, pairs, bias
    )

    output_rows = send_cut(output_slots, experts, copies)
    inner_sent = [cut_share(mlp_in_weight[0], (spot - d) % size, size) for d in range(size)]
    output_rows = after(output_rows, *grad_rows[:3], *inner_sent)
    output_parts = nn(output_rows.reshape(holders * capacity, -1), output_full).astype(bf16)
    far = size // 2
    distances = [d for d in range(1, size) if d != far] + ([far] if size > 1 else [])
    inner_parts = list(inner_sent)
    for d in distances[:1]:
        inner_parts[d] = shifted(after(inner_sent[d], output_full), d, size)
    output_home = home_add(output_parts.reshape(holders, capacity, width), experts, copies)
    output_low = nt(attended, output_lower).astype(bf16)
    branch = nn(place, output_home) + nn(output_low, output_upper)
    branch = branch.reshape(2, rows, width)
    middle = inputs + gates[:, :1] * branch[0] + gates[:, 1:] * branch[1]
    middle_scale = norm_scale(middle)
    normed_mlp = (middle * middle_scale * mlp_gain).astype(bf16)
    mlp_gates, mlp_hits = gate_pair(nn(normed_mlp, mlp_router_weight), mlp_routes[0])

    lanes = jnp.pad(jnp.concatenate(halves(mlp_gates), axis=1), ((0, 0), (0, 124)))
    packet = jnp.concatenate([normed_mlp, lanes], axis=1)
    packet = after(packet, *(inner_parts[d] for d in distances[:1]))
    packet_all = lax.all_gather(packet, "seq", axis=0, tiled=True)
    before = packet_all
    for d in distances[1:]:
        before = inner_parts[d] = shifted(after(inner_sent[d], before), d, size)
    packets = [packet] + [
        lax.dynamic_slice_in_dim(packet_all, (spot + d) % size * rows, rows, 0)
        for d in range(1, size)
    ]
    gates_there = [
        (p[:, width : width + 2].astype(f32) + p[:, width + 2 : width + 4].astype(f32)).T.reshape(-1, 1)
        for p in packets
    ]
    combines = [either((places[d].astype(f32) * gates_there[d]).astype(bf16)) for d in range(size)]
    order = list(range(size))
    outer_codes = [nt(got, outer_up).astype(bf16) * mask for got in grad_rows]
    hidden_grads = [
        (nt(got, outer_full) + nn(code, outer_down)).astype(bf16)
        for got, code in zip(grad_rows, outer_codes)
    ]
    gate_slots = jnp.stack(
        [jnp.sum(places[d].astype(f32) * gates_there[d], axis=0) for d in range(size)]
    )
    gate_slots = gate_slots.reshape(size, experts, capacity).transpose(1, 0, 2)
    gate_slots = exchange(jnp.repeat(gate_slots, copies, axis=0))

    def send_rows(d, *earlier):
        sent = tn(either(places[d]), after(packets[d][:, :width], *earlier)).astype(bf16)
        return send_full(sent, experts, copies).reshape(-1, width)

    def work(d, got):
        return expert_block(got, hidden_grads[d], mask, inner_up, inner_down, inner_parts, spot)

    def rows_home(d, row_grad):
        home = home_add(row_grad.reshape(holders, capacity, -1), experts, copies)
        row_sum = nn(combines[d], home[:, :width])
        gate_sum = nn(places[d], home[:, width:])
        lanes = gate_sum[:rows] + jnp.roll(gate_sum[rows:], 2, axis=1)
        row_back = jnp.concatenate([row_sum, lanes], axis=1)
        return home, shifted(row_back.astype(bf16), -d % size, size) if d else row_back

    got_rows = [send_rows(0)]
    for d in order[1:]:
        earlier = [inner_parts[distances[min(d - 1, size - 2)]]]
        got_rows.append(send_rows(d, got_rows[-1], *earlier))
    kept = [work(0, after(got_rows[0], *got_rows[1:-1], *hidden_grads))]
    row_home, row_total = rows_home(0, kept[0][0])
    row_backs, row_homes = [row_total], [row_home]
    for d in order[1:]:
        kept.append(work(d, after(got_rows[d], kept[-1][0])))
        row_grad = kept[d][0]
        row_home, row_back = rows_home(d, row_grad)
        row_backs.append(row_back)
        row_homes.append(row_home)
        row_total = row_total + row_back.astype(f32)
    gate_sum = row_total[:, width : width + 4]
    row_total = row_total[:, :width]
    mlp_gate_grad = gate_sum.reshape(rows, 2, 2).sum(2)
    mlp_logit_grad = gate_back(mlp_gates, mlp_hits, mlp_gate_grad)

    outer_lows, sums = [], None
    for d in order:
        _, activated, pre_grad, code, back = kept[d]
        there = row_homes[min(d, size - 2)] if size > 1 else row_homes[0]
        activated, pre_grad = after(activated, there), after(pre_grad, there)
        outer_low = nt(activated, outer_down).astype(bf16) * mask
        outer_lows.append(outer_low)
        scale = gate_slots[:, d, :].reshape(-1, 1)

        def scaled(array):
            return (array.astype(f32) * scale).astype(bf16)

        new = (
            tn(scaled(code), pre_grad),
            tn(scaled(outer_codes[d]), activated),
            tn(scaled(back), got_rows[d]),
            tn(scaled(outer_low), grad_rows[d]),
        )
        sums = new if sums is None else tuple(a + b for a, b in zip(sums, new))


    inner_up_sum, outer_down_sum, inner_down_sum, outer_up_sum = sums

    def widened(array):
        if copies == 1:
            return array
        whole = jnp.zeros((codes, copies, array.shape[1]), f32)
        whole = lax.dynamic_update_index_in_dim(whole, array, part, 1)
        return whole.reshape(codes, -1)

    wide = [widened(inner_up_sum), widened(outer_down_sum), inner_down_sum, outer_up_sum]
    ends = [sum(a.shape[1] for a in wide[: k + 1]) for k in range(3)]
    mlp_own = after(jnp.concatenate(wide, axis=1).astype(bf16), row_home)
    mlp_sums = lax.psum_scatter(mlp_own, "dp", scatter_dimension=0, tiled=True)

    def down_back(d, before_matmul, before_sending):
        activated = after(kept[d][1], before_matmul)
        down = (nn(activated, outer_full) + nn(outer_lows[d], outer_up)).astype(bf16)
        down = after(down, before_sending).reshape(holders, capacity, width)
        home = home_add(down, experts, copies)
        made = nn(combines[d], home)
        return home, shifted(made.astype(bf16), -d % size, size).astype(f32) if d else made

    down_turns = order[1:] + [0]
    down_home, down_total = down_back(down_turns[0], row_homes[-2], row_home)

    normed_mlp_grad = row_total + nt(mlp_logit_grad.astype(bf16), mlp_router_weight)
    middle_grad = norm_back(middle, middle_scale, mlp_gain, normed_mlp_grad)
    middle_grad = middle_grad + out_grad[0].astype(f32)
    middle_low = middle_grad.astype(bf16)
    branch_sent = tn(place_any, after(middle_low, down_home)).astype(bf16)
    branch_rows = send_full(branch_sent, experts, copies)
    mlp_sums = lax.all_gather(after(mlp_sums, branch_rows), ("seq", "dp"), axis=0, tiled=True)
    head_parts = nt(branch_rows.reshape(-1, width), output_full).astype(bf16)
    head_home = home_join(head_parts.reshape(holders, capacity, -1), experts, copies)
    down_home, made = down_back(down_turns[1], head_parts, head_home)
    down_total = down_total + made
    head_home = after(head_home, mlp_own)
    gate_grad = jnp.sum(middle_grad[None] * branch, axis=2).T
    logit_grad = gate_back(gates, hits, gate_grad)
    gate_column = gates.T.reshape(-1, 1)
    output_low_grad = nt(middle_low, output_upper)
    output_low_back = output_low_grad.astype(bf16)
    output_low_scaled = (jnp.tile(output_low_grad, (2, 1)) * gate_column).astype(bf16)
    output_lower_grad = tn(output_low_scaled, attended)
    output_low_sum = (output_low.astype(f32) * gate_column).reshape(2, rows, rank).sum(0)
    output_upper_grad = tn(output_low_sum.astype(bf16), middle_low)

    def over_sequences(mine, widths):
        every = lax.all_gather(mine, ("seq", "dp"), axis=0, tiled=False)
        every = every.reshape(size, holders, rank, -1)
        return gather_adapters(every, adapter_all, adapters, widths)

    key_grad, value_grad, query_slots, query_sum = attend_back(
        query_rot,
        pairs,
        bias,
        totals,
        head_home,
        place,
        gate_column,
        output_low_back,
        output_lower,
        cosine,
        sine,
        cosine_all,
        sine_all,
    )
    query_back = send_cut(after(query_slots, down_home), experts, copies)
    input_parts = nt(query_back.reshape(holders * capacity, -1), query_full).astype(bf16)
    input_home = home_add(input_parts.reshape(holders, capacity, width), experts, copies)
    mlp_sums = after(mlp_sums, input_parts)
    if copies == 1 and share % 128 == 0:
        inner_up_grad, outer_down_grad, inner_down_grad, outer_up_grad = unpack_sums(
            mlp_sums.reshape(size, adapters, rank, -1), share, width
        )
    else:
        mlp_sums = mlp_sums.astype(f32).reshape(size, codes, -1)
        inner_up_grad, outer_down_grad, inner_down_grad, outer_up_grad = jnp.split(mlp_sums, ends, axis=2)
        inner_up_grad = inner_up_grad.reshape(size, codes, copies, 2, share).transpose(1, 3, 2, 0, 4)
        inner_up_grad = inner_up_grad.reshape(adapters, rank, -1)
        outer_down_grad = outer_down_grad.reshape(size, codes, copies, share).transpose(1, 2, 0, 3)
        outer_down_grad = outer_down_grad.reshape(adapters, rank, -1)
        inner_down_grad = jnp.sum(inner_down_grad, 0).reshape(adapters, rank, width)
        outer_up_grad = jnp.sum(outer_up_grad, 0).reshape(adapters, rank, width)
    half = key_grad.shape[1]
    pair_low_grad = nt(key_grad, pair_up[:, :half]) + nt(value_grad, pair_up[:, half:])
    pair_low_grad = pair_low_grad.astype(bf16)
    pair_upper_grad = jnp.concatenate([tn(pair_low, key_grad), tn(pair_low, value_grad)], axis=1)
    pair_lower_grad = sum(
        tn(pair_low_grad[d * rows : (d + 1) * rows], normed_parts[d]) for d in range(size)
    )
    query_low_grad = nt(query_sum, query_upper).astype(bf16)
    query_upper_grad = tn(query_low, query_sum)
    query_lower_grad = tn(query_low_grad, normed)
    sequence_grads = [
        pair_lower_grad,
        pair_upper_grad,
        query_lower_grad,
        query_upper_grad,
        output_lower_grad,
        output_upper_grad,
    ]
    joined = jnp.concatenate([a.reshape(rank, size, -1) for a in sequence_grads], axis=2)
    joined = joined.transpose(1, 0, 2)
    normed_grads = pair_back(key_grad, value_grad, pair_weight, pair_low_grad, pair_down)
    mine = picked(joined, spot)
    back_parts = []
    for d in range(1, size):
        theirs = picked(joined, (spot + d) % size).astype(bf16).reshape(-1, width)
        theirs = jnp.pad(theirs, ((0, -theirs.shape[0] % 16), (0, 0)))
        packet = jnp.concatenate([normed_grads[d * rows : (d + 1) * rows], theirs], axis=0)
        packet = after(shifted(packet, -d % size, size), inner_up_grad)
        back_parts.append(packet[:rows])
        adapter_rows = mine.size // width
        mine = mine + packet[rows : rows + adapter_rows].astype(f32).reshape(mine.shape)
    mine = after(mine.astype(bf16), mlp_sums)
    late = over_sequences(mine, [a.shape[1] for a in sequence_grads])
    normed_grad = normed_grads[:rows].astype(f32) + sum(back.astype(f32) for back in back_parts)
    normed_grad = normed_grad + nn(place_any, input_home) + nn(query_low_grad, query_lower)
    normed_grad = normed_grad + nt(logit_grad.astype(bf16), router_weight)
    input_grad = norm_back(inputs, input_scale, norm_gain, normed_grad) + middle_grad

    for d in down_turns[2:]:
        down_home, made = down_back(d, query_slots, input_home)
        down_total = down_total + made
    result = (middle + down_total).astype(bf16)

    return (
        result[None],
        input_grad[None],
        flat_down(late[0]),
        late[1],
        flat_down(late[2]),
        late[3],
        flat_down(late[4]),
        late[5],
        flat_down(inner_down_grad),
        inner_up_grad,
        flat_down(outer_down_grad),
        outer_up_grad,
    )


def solution(mesh):
    split = P("dp", "seq", None)
    placed = (
        (split, P(), P("seq", None), P(), split, split, P(), P(), split, split)
        + (P(),) * 10
        + (split, split, P("dp"), P("dp"), split)
    )
    return jax.shard_map(
        body,
        mesh=mesh,
        in_specs=placed,
        out_specs=(split, split) + (P(),) * 10,
        check_vma=False,
    )
```
